32 devices in a mesh: ctx: 8 (over z, core), fsdp: 4 (over y, x).
Axes of the slice: x: 2, y: 2, z: 4, core: 2. Of those that a mesh axis runs over, the one named last changes fastest.
Arguments:
- tokens: bfloat16 [4, 2048, 2048], P('fsdp', 'ctx'), may hold values from -6 to 6
- block_place: int32 [128], replicated, may hold values from 0 to 127, as said below
- seq_lengths: int32 [4, 4], P('fsdp'), may hold values from 1 to 1024, 2048 in all within a row
- norm_gain: bfloat16 [2048], P('fsdp'), may hold values from 0.5 to 1.5
- norm_bias: bfloat16 [2048], P('fsdp'), may hold values from -3 to 3
- qkv_weight: bfloat16 [2048, 6144], P('fsdp'), may hold values from -0.125 to 0.125
- qkv_bias: bfloat16 [6144], P('fsdp'), may hold values from -3 to 3
- out_weight: bfloat16 [2048, 2048], P('fsdp'), may hold values from -0.5 to 0.5
- out_bias: bfloat16 [2048], P('fsdp'), may hold values from -3 to 3
- up_weight: bfloat16 [2048, 8192], P('fsdp'), may hold values from -0.125 to 0.125
- up_bias: bfloat16 [8192], P('fsdp'), may hold values from -3 to 3
- down_weight: bfloat16 [8192, 2048], P('fsdp'), may hold values from -0.0625 to 0.0625
- down_bias: bfloat16 [2048], P('fsdp'), may hold values from -3 to 3
- out_grad: bfloat16 [4, 2048, 2048], P('fsdp', 'ctx'), may hold values from -6 to 6
Outputs:
- layer_output: bfloat16 [4, 2048, 2048], P('fsdp', 'ctx')
- input_grad: bfloat16 [4, 2048, 2048], P('fsdp', 'ctx')
- norm_gain_grad: float32 [2048], P('fsdp')
- norm_bias_grad: float32 [2048], P('fsdp')
- qkv_weight_grad: float32 [2048, 6144], P('fsdp')
- qkv_bias_grad: float32 [6144], P('fsdp')
- out_weight_grad: float32 [2048, 2048], P('fsdp')
- out_bias_grad: float32 [2048], P('fsdp')
- up_weight_grad: float32 [2048, 8192], P('fsdp')
- up_bias_grad: float32 [8192], P('fsdp')
- down_weight_grad: float32 [8192, 2048], P('fsdp')
- down_bias_grad: float32 [2048], P('fsdp')
The draws below stay inside these ranges and needn't reach their ends.
Inputs may be any that keep to these rules, and one draw needn't show every extreme that they name: `block_place`: A permutation of the group's blocks. For each device d of ctx, its entries d * 16 to (d + 1) * 16 - 1 hold exactly 2 places of each remainder modulo 8. `seq_lengths`: each row sums to 2048.
All inputs are finite; a program needn't handle non-finite values.
Results may differ from the reference program's by a relative error of at most 0.017.
Values may be sent and summed in bfloat16 or wider, within the bound.
No kernel may reach another device: no remote copies, remote signals or barrier semaphores. Data moves between devices by JAX's collectives and lax.ppermute only.
A program may use at most 704 MiB of HBM per device.

```python
import math
import jax
import jax.numpy as jnp
import numpy as np
from jax import lax

D = 2048
HEADS = 32
HEAD_DIM = 64
ROT = 32
FF = 8192
BLK = 16
NSEQ = 4
BPD = 16
GROUP_TOK = 2048
BLOCKS = 128
MAXLEN = 1024
N_FSDP = 4


def draw_block_place(key, part):
    key = jax.random.fold_in(key, 11)
    cycle_count = BLOCKS // BPD
    repeat = BPD // cycle_count
    class_keys = jax.random.split(jax.random.fold_in(key, 1), cycle_count)

    def shuffle(sub_key):
        return jax.random.permutation(sub_key, BPD)
    band_ids = jax.vmap(shuffle)(class_keys).astype(jnp.int32)
    places = band_ids * cycle_count + jnp.arange(cycle_count, dtype=jnp.int32)[:, None]
    grouped = jnp.transpose(places.reshape(cycle_count, cycle_count, repeat), (1, 0, 2)).reshape(cycle_count, BPD)
    device_keys = jax.random.split(jax.random.fold_in(key, 2), cycle_count)
    shuffles = jax.vmap(shuffle)(device_keys).astype(jnp.int32)
    mixed_rows = jnp.take_along_axis(grouped, shuffles, axis=1)
    return mixed_rows.reshape(-1).astype(jnp.int32)


def steps_of(key, shape, shards, low, largest):
    level, own = 1.0, jax.random.fold_in(key, 6)
    for dim, shards_of in shards:
        steps = jnp.exp(jax.random.uniform(jax.random.fold_in(own, dim), (shards_of,), jnp.float32, low / len(shards), largest / len(shards)))
        level = level * jnp.repeat(steps, shape[dim] // shards_of).reshape([-1 if axis == dim else 1 for axis in range(len(shape))])
    return level


def split_up(amount, total, limit, slope):
    weights = [(1 << 20) // math.isqrt(standing ** slope) + 1 for standing in range(2, amount + 1)]
    rest, given = total - limit - (amount - 1), [1] * (amount - 1)
    while rest > 0:
        free = [i for i in range(amount - 1) if given[i] < limit]
        mass, budget = sum([weights[i] for i in free]), rest
        for i in free:
            extra = min(limit - given[i], max(1, budget * weights[i] // mass), rest)
            given[i] = given[i] + extra
            rest = rest - extra
    return np.array([limit] + given)


def uneven_parts(stream_key, amount, total, most, lean):
    if amount == 2:
        one = jax.random.randint(stream_key, (), max(1, total - most), min(most, total - 1) + 1)
        return jnp.stack([one, total - one])
    sizes = jnp.asarray(split_up(amount, total, most, lean), jnp.int32)
    pairs = (amount - 1) // 2
    source_of, taker = sizes[1:1 + 2 * pairs:2], sizes[2:2 + 2 * pairs:2]
    margin = jnp.minimum(source_of - 1, most - taker)
    shifted = jax.random.randint(jax.random.fold_in(stream_key, 1), (pairs,), 0, 1 << 20) % (margin + 1)
    sizes = sizes.at[1:1 + 2 * pairs:2].set(source_of - shifted).at[2:2 + 2 * pairs:2].set(taker + shifted)
    return sizes[jax.random.permutation(jax.random.fold_in(stream_key, 2), amount)]


def normal_values(stream_key, dims, scale, limit, cuts=(), kind=jnp.bfloat16):
    result = scale * jax.random.normal(stream_key, dims, jnp.float32)
    if cuts:
        result = result * steps_of(stream_key, dims, cuts, -0.22, 0.18)
    return jnp.clip(result, -limit, limit).astype(kind)


def setup_inputs(seed: int = 0) -> dict:
    key_list = jax.random.split(jax.random.key(seed), 15)
    return {
        "tokens": normal_values(key_list[0], (N_FSDP, GROUP_TOK, D), 1.0, 6.0, ((0, 4), (1, 8))),
        "block_place": draw_block_place(jax.random.fold_in(key_list[14], 71), 0),
        "seq_lengths": jax.vmap(lambda own: uneven_parts(own, NSEQ, GROUP_TOK, MAXLEN, 2))(jax.random.split(key_list[2], N_FSDP)).reshape((N_FSDP, NSEQ)).astype(jnp.int32),
        "norm_gain": jnp.clip(1.0 + 0.1 * jax.random.normal(key_list[3], (D,), jnp.float32), 0.5, 1.5).astype(jnp.bfloat16),
        "norm_bias": normal_values(key_list[4], (D,), 0.3, 3.0, ((0, 4),)),
        "qkv_weight": normal_values(key_list[5], (D, 3 * D), D ** -0.5, 0.125, ((0, 4),)),
        "qkv_bias": normal_values(key_list[6], (3 * D,), 0.3, 3.0, ((0, 4),)),
        "out_weight": normal_values(key_list[7], (D, D), (D // 16) ** -0.5, 0.5, ((0, 4),)),
        "out_bias": normal_values(key_list[8], (D,), 0.3, 3.0, ((0, 4),)),
        "up_weight": normal_values(key_list[9], (D, FF), D ** -0.5, 0.125, ((0, 4),)),
        "up_bias": normal_values(key_list[10], (FF,), 0.5, 3.0, ((0, 4),)),
        "down_weight": normal_values(key_list[11], (FF, D), FF ** -0.5, 0.0625, ((0, 4),)),
        "down_bias": normal_values(key_list[12], (D,), 0.3, 3.0, ((0, 4),)),
        "out_grad": normal_values(key_list[13], (N_FSDP, GROUP_TOK, D), 1.0, 6.0, ((0, 4), (1, 8))),
    }


@jax.custom_vjp
def low(v):
    return lax.optimization_barrier(v.astype(jnp.bfloat16)).astype(jnp.float32)

@jax.custom_vjp
def low_back(v):
    return v

def low_keep(v):
    return (low(v), None)

def low_pass(kept, grad):
    return (grad,)

def back_keep(v):
    return (v, None)

def back_low(kept, grad):
    return (low(grad),)
low.defvjp(low_keep, low_pass)
low_back.defvjp(back_keep, back_low)

def matmul(left, right):
    return jnp.dot(left, right, precision=lax.Precision.HIGHEST)

def token_layout(block_place, lengths):
    row_index = jnp.arange(GROUP_TOK, dtype=jnp.int32)
    places = block_place[row_index // BLK].astype(jnp.int32)
    position = places * BLK + row_index % BLK
    seq_ends = jnp.cumsum(lengths).astype(jnp.int32)
    seq_starts = seq_ends - lengths.astype(jnp.int32)
    segment = lax.optimization_barrier(jnp.sum((position[:, None] >= seq_ends[None, :]).astype(jnp.int32), axis=1)).astype(jnp.int32)
    which = segment[:, None] == jnp.arange(NSEQ, dtype=jnp.int32)[None, :]
    seq_begin = lax.optimization_barrier(jnp.sum(jnp.where(which, seq_starts[None, :], 0), axis=1)).astype(jnp.int32)
    return (position, segment, position - seq_begin)

def rotate(values, within, direction):
    half_rot = ROT // 2
    frequency = 10000.0 ** (-jnp.arange(half_rot, dtype=jnp.float32) * 2.0 / ROT)
    angles = within.astype(jnp.float32)[:, None] * frequency[None, :]
    cosine = jnp.cos(angles)[:, None, :]
    sine_part = direction * jnp.sin(angles)[:, None, :]
    first_half = values[..., :half_rot]
    second_half = values[..., half_rot:ROT]
    return jnp.concatenate([first_half * cosine - second_half * sine_part, second_half * cosine + first_half * sine_part, values[..., ROT:]], axis=-1)

def group_forward(params, inputs, block_place, lengths):
    norm_scale, norm_shift, qkv_mat, qkv_vec, out_mat, out_vec, up_mat, up_vec, down_mat, down_vec = params
    position, segment, within = token_layout(block_place, lengths)
    row_mean = lax.optimization_barrier(jnp.mean(inputs, axis=1, keepdims=True))
    centred = inputs - row_mean
    scaled = centred * lax.rsqrt(lax.optimization_barrier(jnp.mean(centred * centred, axis=1, keepdims=True)) + 1e-05)
    normed = low(scaled * norm_scale + norm_shift)
    projected = matmul(normed, qkv_mat) + qkv_vec
    query_lin = low_back(projected[:, :D])
    key_lin = low_back(projected[:, D:2 * D])
    value_rows = low(low_back(projected[:, 2 * D:]))
    head_shape = (GROUP_TOK, HEADS, HEAD_DIM)
    queries = low(rotate(query_lin.reshape(head_shape), within, 1.0))
    key_rows = low(rotate(key_lin.reshape(head_shape), within, 1.0))
    value_rows = value_rows.reshape(head_shape)
    block_rows = min(512, GROUP_TOK)

    def attend(query_block):
        query_part, query_pos, query_seg = query_block
        scores = jnp.einsum('qhd,khd->hqk', query_part, key_rows, precision=lax.Precision.HIGHEST) * HEAD_DIM ** (-0.5)
        scores = low_back(scores)
        visible = (query_seg[:, None] == segment[None, :]) & (position[None, :] <= query_pos[:, None])
        scores = jnp.where(visible[None], scores, -1e+30)
        row_top = lax.optimization_barrier(jnp.max(scores, axis=2, keepdims=True))
        weights = jnp.exp(scores - row_top)
        weights = low(weights / lax.optimization_barrier(jnp.sum(weights, axis=2, keepdims=True)))
        return jnp.einsum('hqk,khd->qhd', weights, value_rows, precision=lax.Precision.HIGHEST)
    blocks_in = (queries.reshape(GROUP_TOK // block_rows, block_rows, HEADS, HEAD_DIM), position.reshape(-1, block_rows), segment.reshape(-1, block_rows))
    attended = lax.map(jax.checkpoint(attend), blocks_in)
    attended = low(low_back(attended.reshape(GROUP_TOK, D)))
    branch = matmul(attended, out_mat) + out_vec
    hidden = low_back(matmul(normed, up_mat) + up_vec)
    active = low(jax.nn.gelu(hidden, approximate=True))
    feed_out = matmul(active, down_mat) + down_vec
    return inputs + branch + feed_out

def reference(tokens, block_place, seq_lengths, norm_gain, norm_bias, qkv_weight, qkv_bias, out_weight, out_bias, up_weight, up_bias, down_weight, down_bias, out_grad):
    params = tuple((item.astype(jnp.float32) for item in (norm_gain, norm_bias, qkv_weight, qkv_bias, out_weight, out_bias, up_weight, up_bias, down_weight, down_bias)))
    inputs = tokens.astype(jnp.float32)

    def forward(params, inputs):

        def per_group(group_data):
            values, lengths = group_data
            return group_forward(params, values, block_place, lengths)
        return lax.map(jax.checkpoint(per_group), (inputs, seq_lengths))
    outputs, pullback = jax.vjp(forward, params, inputs)
    weight_grads, input_grad = pullback(out_grad.astype(jnp.float32))
    return (outputs.astype(jnp.bfloat16), input_grad.astype(jnp.bfloat16), weight_grads[0], weight_grads[1], weight_grads[2], weight_grads[3], weight_grads[4], weight_grads[5], weight_grads[6], weight_grads[7], weight_grads[8], weight_grads[9])
```

```python
import functools

import jax
import jax.numpy as jnp
from jax import lax
from jax.experimental import pallas as pl
from jax.experimental.pallas import tpu as pltpu
from jax.sharding import PartitionSpec as P

HEAD_DIM = 64
ROT = 32
BLK = 16
TILE = 256
LANES = 128
F32 = jnp.float32
BF16 = jnp.bfloat16


def dot_nn(left, right):
    return lax.dot_general(left, right, (((1,), (0,)), ((), ())), preferred_element_type=F32)


def dot_nt(left, right):
    return lax.dot_general(left, right, (((1,), (1,)), ((), ())), preferred_element_type=F32)


def dot_tn(left, right):
    return lax.dot_general(left, right, (((0,), (0,)), ((), ())), preferred_element_type=F32)


def swap(value, axis, mask):
    devices = lax.axis_size(axis)
    return lax.ppermute(value, axis, [(i, i ^ mask) for i in range(devices)])


def bits_of(axis):
    return range(lax.axis_size(axis).bit_length() - 1)


def gather_rows(own, order):
    index = lax.axis_index("fsdp")
    count = lax.axis_size("fsdp")
    rows = own.shape[0]
    whole = lax.dynamic_update_slice_in_dim(
        jnp.zeros((count * rows, own.shape[1]), own.dtype), own, index * rows, 0
    )
    held = [(index, own)]
    for bit in order:
        arrived = [(where ^ (1 << bit), swap(piece, "fsdp", 1 << bit)) for where, piece in held]
        for where, piece in arrived:
            whole = lax.dynamic_update_slice_in_dim(whole, piece, where * rows, 0)
        held = held + arrived
    return whole


def scatter_sum(parts, order):
    index = lax.axis_index("fsdp")
    bits = len(order)
    left = list(range(bits))[::-1]
    held = parts.reshape((2,) * bits + parts.shape[1:])
    for bit in order:
        axis = left.index(bit)
        mine = (index >> bit) & 1
        send = lax.dynamic_index_in_dim(held, 1 - mine, axis, keepdims=False)
        keep = lax.dynamic_index_in_dim(held, mine, axis, keepdims=False)
        got = swap(send, "fsdp", 1 << bit)
        held = (keep.astype(F32) + got.astype(F32)).astype(BF16)
        left.pop(axis)
    return held


def line_sum(parts):
    index = lax.axis_index("ctx")
    count = lax.axis_size("ctx")
    line = count // 2
    core, place = index % 2, index // 2
    pairs = parts.reshape((line, 2, parts.shape[0] // count) + parts.shape[1:])
    other = lax.dynamic_index_in_dim(pairs, 1 - core, 1, keepdims=False)
    mine = lax.dynamic_index_in_dim(pairs, core, 1, keepdims=False)
    held = (mine.astype(F32) + swap(other, "ctx", 1).astype(F32)).astype(BF16)

    def block(target):
        return lax.dynamic_index_in_dim(
            held, jnp.clip(target, 0, line - 1), 0, keepdims=False
        ).astype(F32)

    ups = downs = None
    for step in range(line - 1):
        far = line - 1 - step
        up = block(place + far)
        down = block(place - far)
        if step:
            up, down = up + ups, down + downs
        ups = lax.ppermute(
            up.astype(BF16), "ctx", [(i, i + 2) for i in range(count - 2) if i // 2 + far < line]
        ).astype(F32)
        downs = lax.ppermute(
            down.astype(BF16), "ctx", [(i, i - 2) for i in range(2, count) if i // 2 - far >= 0]
        ).astype(F32)
    total = block(place)
    return total + ups + downs if line > 1 else total


def sum_everywhere(vector):
    for axis in ("ctx", "fsdp"):
        for bit in bits_of(axis):
            vector = vector + swap(vector, axis, 1 << bit)
    return vector


def turn(values, cosine, sine):
    lane = lax.broadcasted_iota(jnp.int32, values.shape, 1) % HEAD_DIM
    half = ROT // 2
    partner = jnp.where(
        lane < half, pltpu.roll(values, LANES - half, 1), pltpu.roll(values, half, 1)
    )
    return values * cosine + partner * sine


def attention_kernel(
    place_ref, ends_ref, cos_ref, sin_ref, lin_hbm, grad_hbm, att_hbm, mixed_hbm,
    lin, grad, rows, keys_t, values_t, grad_t, grad_k, grad_v, weights, grad_w, att, mixed, sems,
):
    tokens, width = grad.shape
    tile = TILE
    tiles = tokens // tile
    blocks = tokens // BLK
    sequences = ends_ref.shape[0]
    pairs = width // LANES

    @pl.loop(0, blocks)
    def _(block):
        source = pl.ds(pl.multiple_of(block * BLK, BLK), BLK)
        target = pl.ds(pl.multiple_of(place_ref[block] * BLK, BLK), BLK)
        pltpu.make_async_copy(lin_hbm.at[source], lin.at[target], sems.at[0]).start()
        pltpu.make_async_copy(grad_hbm.at[source], grad.at[target], sems.at[1]).start()

    grad_k[...] = jnp.zeros_like(grad_k)
    grad_v[...] = jnp.zeros_like(grad_v)
    pltpu.make_async_copy(lin_hbm, lin, sems.at[0]).wait()
    pltpu.make_async_copy(grad_hbm, grad, sems.at[1]).wait()

    @pl.loop(0, tiles)
    def _(step):
        part = pl.ds(pl.multiple_of(step * tile, tile), tile)
        cosine, sine = cos_ref[part, :], sin_ref[part, :]
        for pair in range(pairs):
            lanes = slice(pair * LANES, (pair + 1) * LANES)
            key_lanes = slice(width + pair * LANES, width + (pair + 1) * LANES)
            value_lanes = slice(2 * width + pair * LANES, 2 * width + (pair + 1) * LANES)
            query = turn(lin[part, lanes], cosine, sine) * HEAD_DIM ** (-0.5)
            rows[part, lanes] = query.astype(BF16)
            key = turn(lin[part, key_lanes], cosine, sine).astype(BF16)
            rows[part, key_lanes] = key
            keys_t[lanes, part] = key.T
            value = lin[part, value_lanes].astype(BF16)
            rows[part, value_lanes] = value
            values_t[lanes, part] = value.T
            grad_t[lanes, part] = grad[part, lanes].T

    def first_half(values):
        lane = lax.broadcasted_iota(jnp.int32, values.shape, 1)
        return lane < HEAD_DIM

    for pair in range(pairs):
        lanes = slice(pair * LANES, (pair + 1) * LANES)
        key_lanes = slice(width + pair * LANES, width + (pair + 1) * LANES)
        value_lanes = slice(2 * width + pair * LANES, 2 * width + (pair + 1) * LANES)
        head_rows = [
            slice(pair * LANES + head * HEAD_DIM, pair * LANES + (head + 1) * HEAD_DIM)
            for head in range(2)
        ]

        @pl.loop(0, tiles)
        def _(step):
            top = step * tile
            part = pl.ds(pl.multiple_of(top, tile), tile)
            column = top + lax.broadcasted_iota(jnp.int32, (1, tile), 1)
            begin = jnp.zeros((1, tile), jnp.int32)
            first = jnp.int32(0)
            for sequence in range(sequences):
                end = ends_ref[sequence]
                begin = jnp.where(column >= end, jnp.maximum(begin, end), begin)
                first = jnp.where(top >= end, jnp.maximum(first, end), first)
            low = first // tile
            query = rows[part, lanes]
            back = grad[part, lanes]
            half = first_half(query)
            zero = jnp.zeros_like(query)
            queries = [jnp.where(half, query, zero), jnp.where(half, zero, query)]
            backs = [jnp.where(half, back, zero), jnp.where(half, zero, back)]

            def score(index, tops):
                there = pl.ds(pl.multiple_of(index * tile, tile), tile)
                row = index * tile + lax.broadcasted_iota(jnp.int32, (tile, tile), 0)
                visible = (row <= column) & (row >= begin)
                key = rows[there, key_lanes]
                result = []
                for head in range(2):
                    scores = jnp.where(visible, dot_nt(key, queries[head]), -1e30)
                    weights[head, there, :] = scores
                    result.append(
                        jnp.maximum(tops[head], jnp.max(scores, axis=0, keepdims=True))
                    )
                return tuple(result)

            tops = lax.fori_loop(
                low, step + 1, score, (jnp.full((1, tile), -1e30, F32),) * 2
            )

            def combine(index, state):
                there = pl.ds(pl.multiple_of(index * tile, tile), tile)
                value = rows[there, value_lanes]
                result = []
                for head in range(2):
                    total, summed = state[head]
                    weight = jnp.exp(weights[head, there, :] - tops[head])
                    weights[head, there, :] = weight
                    grad_w[head, there, :] = dot_nt(value, backs[head])
                    total = total + jnp.sum(weight, axis=0, keepdims=True)
                    summed = summed + dot_nn(
                        values_t[head_rows[head], there], weight.astype(BF16)
                    )
                    result.append((total, summed))
                return tuple(result)

            state = lax.fori_loop(
                low,
                step + 1,
                combine,
                ((jnp.zeros((1, tile), F32), jnp.zeros((HEAD_DIM, tile), F32)),) * 2,
            )
            inverse = [1.0 / total for total, summed in state]
            attended = [state[head][1] * inverse[head] for head in range(2)]
            delta = [
                jnp.sum(
                    attended[head] * grad_t[head_rows[head], part].astype(F32),
                    axis=0,
                    keepdims=True,
                )
                for head in range(2)
            ]
            att[part, lanes] = jnp.concatenate(attended, axis=0).T.astype(BF16)

            def back_step(index, sums):
                there = pl.ds(pl.multiple_of(index * tile, tile), tile)
                result = []
                add_k = add_v = None
                for head in range(2):
                    weight = weights[head, there, :] * inverse[head]
                    grad_s = (weight * (grad_w[head, there, :] - delta[head])).astype(BF16)
                    part_k = dot_nn(grad_s, queries[head])
                    part_v = dot_nn(weight.astype(BF16), backs[head])
                    add_k = part_k if head == 0 else add_k + part_k
                    add_v = part_v if head == 0 else add_v + part_v
                    result.append(sums[head] + dot_nn(keys_t[head_rows[head], there], grad_s))
                grad_k[there, lanes] += add_k
                grad_v[there, lanes] += add_v
                return tuple(result)

            sums = lax.fori_loop(
                low, step + 1, back_step, (jnp.zeros((HEAD_DIM, tile), F32),) * 2
            )
            grad_q = jnp.concatenate(sums, axis=0).T * HEAD_DIM ** (-0.5)
            mixed[part, lanes] = turn(grad_q, cos_ref[part, :], -sin_ref[part, :]).astype(BF16)

    @pl.loop(0, tiles)
    def _(step):
        part = pl.ds(pl.multiple_of(step * tile, tile), tile)
        cosine, sine = cos_ref[part, :], sin_ref[part, :]
        for pair in range(pairs):
            lanes = slice(pair * LANES, (pair + 1) * LANES)
            key_lanes = slice(width + pair * LANES, width + (pair + 1) * LANES)
            value_lanes = slice(2 * width + pair * LANES, 2 * width + (pair + 1) * LANES)
            mixed[part, key_lanes] = turn(grad_k[part, lanes], cosine, -sine).astype(BF16)
            mixed[part, value_lanes] = grad_v[part, lanes].astype(BF16)

    @pl.loop(0, blocks)
    def _(block):
        target = pl.ds(pl.multiple_of(block * BLK, BLK), BLK)
        source = pl.ds(pl.multiple_of(place_ref[block] * BLK, BLK), BLK)
        pltpu.make_async_copy(att.at[source], att_hbm.at[target], sems.at[0]).start()
        pltpu.make_async_copy(mixed.at[source], mixed_hbm.at[target], sems.at[1]).start()

    pltpu.make_async_copy(att, att_hbm, sems.at[0]).wait()
    pltpu.make_async_copy(mixed, mixed_hbm, sems.at[1]).wait()


def attention(block_place, lengths, linear, grad_att):
    tokens, width = grad_att.shape
    ends = jnp.cumsum(lengths).astype(jnp.int32)
    position = jnp.arange(tokens, dtype=jnp.int32)
    begin = jnp.max(jnp.where(position[:, None] >= ends[None, :], ends[None, :], 0), axis=1)
    within = (position - begin).astype(F32)
    half = ROT // 2
    frequency = 10000.0 ** (-jnp.arange(half, dtype=F32) * 2.0 / ROT)
    angles = within[:, None] * frequency[None, :]
    cosine, sine = jnp.cos(angles), jnp.sin(angles)
    ones = jnp.ones((tokens, HEAD_DIM - ROT), F32)
    cos_table = jnp.concatenate([cosine, cosine, ones] * 2, axis=1)
    sin_table = jnp.concatenate([-sine, sine, 0.0 * ones] * 2, axis=1)
    smem = pl.BlockSpec(memory_space=pltpu.SMEM)
    vmem = pl.BlockSpec(memory_space=pltpu.VMEM)
    anywhere = pl.BlockSpec(memory_space=pl.ANY)
    return pl.pallas_call(
        attention_kernel,
        out_shape=(
            jax.ShapeDtypeStruct((tokens, width), BF16),
            jax.ShapeDtypeStruct((tokens, 3 * width), BF16),
        ),
        in_specs=[smem, smem, vmem, vmem, anywhere, anywhere],
        out_specs=(anywhere, anywhere),
        scratch_shapes=[
            pltpu.VMEM((tokens, 3 * width), F32),
            pltpu.VMEM((tokens, width), BF16),
            pltpu.VMEM((tokens, 3 * width), BF16),
            pltpu.VMEM((width, tokens), BF16),
            pltpu.VMEM((width, tokens), BF16),
            pltpu.VMEM((width, tokens), BF16),
            pltpu.VMEM((tokens, width), F32),
            pltpu.VMEM((tokens, width), F32),
            pltpu.VMEM((2, tokens, TILE), F32),
            pltpu.VMEM((2, tokens, TILE), F32),
            pltpu.VMEM((tokens, width), BF16),
            pltpu.VMEM((tokens, 3 * width), BF16),
            pltpu.SemaphoreType.DMA((2,)),
        ],
        compiler_params=pltpu.CompilerParams(vmem_limit_bytes=56 << 20),
        cost_estimate=pl.CostEstimate(
            flops=30 * 10**9, bytes_accessed=15 * 10**6, transcendentals=0
        ),
    )(block_place, ends, cos_table, sin_table, linear, grad_att)


def shards(
    tokens,
    block_place,
    seq_lengths,
    norm_gain,
    norm_bias,
    qkv_weight,
    qkv_bias,
    out_weight,
    out_bias,
    up_weight,
    up_bias,
    down_weight,
    down_bias,
    out_grad,
):
    ctx_count, ctx_index = lax.axis_size("ctx"), lax.axis_index("ctx")
    shard_count, shard_index = lax.axis_size("fsdp"), lax.axis_index("fsdp")
    own_tokens, own_grad = tokens[0], out_grad[0]
    own_rows, model_width = own_tokens.shape
    hidden_width = up_weight.shape[1]
    heads = model_width // HEAD_DIM
    own_heads = heads // ctx_count
    shard_heads = heads // shard_count
    unit = hidden_width // shard_count // ctx_count
    own_width = own_heads * HEAD_DIM
    head_turns = ctx_count // shard_heads
    low_first = list(bits_of("fsdp"))
    high_first = low_first[::-1]

    def pick(value, axis):
        return lax.dynamic_index_in_dim(value, ctx_index, axis, keepdims=False)

    half_width = model_width // 2
    grad_rows = [
        lax.all_gather(piece, "ctx", axis=0, tiled=True)
        for piece in (own_grad[:, :half_width], own_grad[:, half_width:])
    ]

    vectors = (norm_gain, norm_bias, qkv_bias, out_bias, up_bias, down_bias)
    packed = lax.all_gather(jnp.concatenate(vectors), "fsdp", axis=0, tiled=False)
    cuts = [0]
    for vector in vectors:
        cuts.append(cuts[-1] + vector.shape[0])
    gain_all, shift_all, qkv_bias_all, out_bias_all, up_bias_all, down_bias_all = [
        packed[:, start:stop].reshape(-1).astype(F32) for start, stop in zip(cuts, cuts[1:])
    ]
    own_qkv_bias = pick(qkv_bias_all.reshape(3 * own_heads, ctx_count, HEAD_DIM), 1).reshape(-1)
    own_up_bias = pick(up_bias_all.reshape(shard_count, ctx_count, unit), 1).reshape(-1)

    inputs = own_tokens.astype(F32)
    row_mean = jnp.mean(inputs, axis=1, keepdims=True)
    centred = inputs - row_mean
    inv_std = lax.rsqrt(jnp.mean(centred * centred, axis=1, keepdims=True) + 1e-05)
    scaled = centred * inv_std
    own_normed = (scaled * gain_all + shift_all).astype(BF16)
    normed = lax.all_gather(own_normed, "ctx", axis=0, tiled=True)

    own_up = pick(up_weight.reshape(-1, shard_count, ctx_count, unit), 2)
    up_all = gather_rows(own_up.reshape(-1, shard_count * unit), low_first)
    own_down = pick(down_weight.reshape(ctx_count, unit, model_width), 0)
    down_all = gather_rows(own_down, high_first)
    own_qkv = pick(qkv_weight.reshape(-1, 3 * own_heads, ctx_count, HEAD_DIM), 2)
    qkv_all = gather_rows(own_qkv.reshape(-1, 3 * own_width), high_first)
    turn_index, head_slot = ctx_index // shard_heads, ctx_index % shard_heads
    own_out = lax.dynamic_index_in_dim(
        out_weight.reshape(shard_heads, HEAD_DIM, model_width), head_slot, 0, keepdims=False
    )
    out_all = gather_rows(own_out, low_first).reshape(
        own_heads, head_turns, HEAD_DIM, model_width
    )
    out_all = lax.dynamic_index_in_dim(out_all, turn_index, 1, keepdims=False).reshape(
        own_width, model_width
    )

    hidden = dot_nn(normed, up_all) + own_up_bias
    active = jax.nn.gelu(hidden, approximate=True).astype(BF16)
    linear = dot_nn(normed, qkv_all) + own_qkv_bias

    down_parts = [
        scatter_sum(
            dot_tn(active, piece).astype(BF16).reshape(shard_count, unit, half_width),
            order,
        )
        for piece, order in zip(grad_rows, (low_first, high_first))
    ]
    grad_active = dot_nt(grad_rows[0], down_all[:, :half_width]) + dot_nt(
        grad_rows[1], down_all[:, half_width:]
    )
    unused_out, gelu_back = jax.vjp(lambda inner: jax.nn.gelu(inner, approximate=True), hidden)
    grad_hidden = gelu_back(grad_active)[0].astype(BF16)
    up_part = scatter_sum(
        dot_tn(normed, grad_hidden).astype(BF16).reshape(shard_count, -1, shard_count * unit),
        low_first,
    )
    grad_att = (
        dot_nt(grad_rows[0], out_all[:, :half_width])
        + dot_nt(grad_rows[1], out_all[:, half_width:])
    ).astype(BF16)
    attended, grad_mixed = attention(block_place, seq_lengths[0], linear, grad_att)
    qkv_part = scatter_sum(
        dot_tn(normed, grad_mixed).astype(BF16).reshape(shard_count, -1, 3 * own_width),
        high_first,
    )
    out_terms = jnp.concatenate([dot_tn(attended, piece) for piece in grad_rows], axis=1)
    out_terms = out_terms.astype(BF16).reshape(own_heads, 1, HEAD_DIM, model_width)
    if head_turns > 1:
        out_terms = lax.dynamic_update_slice_in_dim(
            jnp.zeros((own_heads, head_turns, HEAD_DIM, model_width), BF16),
            out_terms,
            turn_index,
            1,
        )
    out_part = scatter_sum(out_terms.reshape(shard_count, HEAD_DIM, model_width), low_first)

    out_partial = (dot_nn(attended, out_all) + dot_nn(active, down_all)).astype(BF16)
    output = (inputs + line_sum(out_partial) + (out_bias_all + down_bias_all)).astype(BF16)
    norm_partial = (dot_nt(grad_mixed, qkv_all) + dot_nt(grad_hidden, up_all)).astype(BF16)
    grad_normed = line_sum(norm_partial)

    grad_float = own_grad.astype(F32)
    grad_scaled = grad_normed * gain_all
    grad_input = inv_std * (
        grad_scaled
        - jnp.mean(grad_scaled, axis=1, keepdims=True)
        - scaled * jnp.mean(grad_scaled * scaled, axis=1, keepdims=True)
    )
    input_grad = (grad_float + grad_input).astype(BF16)

    def spread(value, count):
        value = value.reshape(-1, 1, value.shape[0] // count)
        whole = jnp.zeros((count, ctx_count, value.shape[2]), F32)
        return lax.dynamic_update_slice_in_dim(whole, value, ctx_index, 1).reshape(-1)

    sums = (
        jnp.sum(grad_normed * scaled, axis=0),
        jnp.sum(grad_normed, axis=0),
        spread(jnp.sum(grad_mixed.astype(F32), axis=0), 3 * own_heads),
        jnp.sum(grad_float, axis=0),
        spread(jnp.sum(grad_hidden.astype(F32), axis=0), shard_count),
    )
    total = sum_everywhere(jnp.concatenate(sums))
    own_sums, start = [], 0
    for item in sums:
        size = item.shape[0] // shard_count
        own_sums.append(lax.dynamic_slice_in_dim(total, start + shard_index * size, size))
        start += item.shape[0]
    gain_total, shift_total, qkv_bias_total, bias_total, up_bias_total = own_sums

    down_total = [
        lax.all_gather(piece, "ctx", axis=0, tiled=True).astype(F32) for piece in down_parts
    ]
    up_total = lax.all_gather(up_part, "ctx", axis=0, tiled=False)
    qkv_total = lax.all_gather(qkv_part, "ctx", axis=0, tiled=False)
    out_total = lax.all_gather(out_part, "ctx", axis=0, tiled=False)

    def deal(value, size):
        rows = value.shape[1]
        value = value.reshape(ctx_count, rows, -1, size)
        return jnp.transpose(value, (1, 2, 0, 3)).reshape(rows, -1).astype(F32)

    out_total = lax.dynamic_index_in_dim(
        out_total.reshape(head_turns, shard_heads * HEAD_DIM, model_width),
        shard_index % head_turns,
        0,
        keepdims=False,
    )
    return (
        output[None],
        input_grad[None],
        gain_total,
        shift_total,
        deal(qkv_total, HEAD_DIM),
        qkv_bias_total,
        out_total.astype(F32),
        bias_total,
        deal(up_total, unit),
        up_bias_total,
        jnp.concatenate(down_total, axis=1),
        bias_total,
    )


def solution(mesh):
    in_specs = (
        P("fsdp", "ctx", None),
        P(),
        P("fsdp", None),
        P("fsdp"),
        P("fsdp"),
        P("fsdp", None),
        P("fsdp"),
        P("fsdp", None),
        P("fsdp"),
        P("fsdp", None),
        P("fsdp"),
        P("fsdp", None),
        P("fsdp"),
        P("fsdp", "ctx", None),
    )
    out_specs = (
        P("fsdp", "ctx", None),
        P("fsdp", "ctx", None),
        P("fsdp"),
        P("fsdp"),
        P("fsdp", None),
        P("fsdp"),
        P("fsdp", None),
        P("fsdp"),
        P("fsdp", None),
        P("fsdp"),
        P("fsdp", None),
        P("fsdp"),
    )
    return jax.shard_map(shards, mesh=mesh, in_specs=in_specs, out_specs=out_specs, check_vma=False)
```

```python
import functools

import jax
import jax.numpy as jnp
from jax import lax
from jax.experimental import pallas as pl
from jax.experimental.pallas import tpu as pltpu
from jax.sharding import PartitionSpec as P

HEAD_DIM = 64
ROT = 32
BLK = 16
TILE = 256
LANES = 128
F32 = jnp.float32
BF16 = jnp.bfloat16


def dot_nn(left, right):
    return lax.dot_general(left, right, (((1,), (0,)), ((), ())), preferred_element_type=F32)


def dot_nt(left, right):
    return lax.dot_general(left, right, (((1,), (1,)), ((), ())), preferred_element_type=F32)


def dot_tn(left, right):
    return lax.dot_general(left, right, (((0,), (0,)), ((), ())), preferred_element_type=F32)


def bits_of(axis):
    return range(lax.axis_size(axis).bit_length() - 1)


def swaps(axis, mask):
    return axis, [(i, i ^ mask) for i in range(lax.axis_size(axis))]


class Flow:
    def __init__(self, steps):
        self.steps = steps
        self.result = None
        self.moves = next(steps)

    def arrive(self, values):
        try:
            self.moves = self.steps.send(values)
        except StopIteration as stop:
            self.moves, self.result = [], stop.value


def beside(work, inputs, flows, late=(), early=()):
    starting = [*flows, *late]
    sends = [[value for value, _, _ in flow.moves] for flow in starting]
    inputs, sends = lax.optimization_barrier((inputs, sends))
    for flow, values in zip(starting, sends):
        flow.moving = [
            lax.ppermute(value, axis, pairs) for value, (_, axis, pairs) in zip(values, flow.moves)
        ]
    outputs = work(*inputs)
    ending = [*flows, *early]
    outputs, arrived = lax.optimization_barrier((outputs, [flow.moving for flow in ending]))
    for flow, values in zip(ending, arrived):
        flow.arrive(values)
    return outputs


def gather_steps(own, *orders):
    share = own.shape[0] // len(orders)
    held = [[(0, own[i * share : (i + 1) * share])] for i in range(len(orders))]
    for step in range(len(orders[0])):
        moves = [
            (piece, *swaps("fsdp", 1 << order[step]))
            for pieces, order in zip(held, orders)
            for _, piece in pieces
        ]
        arrived = iter((yield moves))
        for i, order in enumerate(orders):
            held[i] = held[i] + [(mask ^ (1 << order[step]), next(arrived)) for mask, _ in held[i]]
    return [
        (mask, i * share, piece) for i, pieces in enumerate(held) for mask, piece in pieces
    ]


def direct_steps(own):
    masks = range(1, lax.axis_size("fsdp"))
    arrived = yield [(own, *swaps("fsdp", mask)) for mask in masks]
    return [(0, 0, own)] + [(mask, 0, piece) for mask, piece in zip(masks, arrived)]


def scatter_steps(parts, *orders):
    index = lax.axis_index("fsdp")
    bits = len(orders[0])
    share = parts.shape[1] // len(orders)
    held = [
        parts[:, i * share : (i + 1) * share].reshape((2,) * bits + (share, parts.shape[2]))
        for i in range(len(orders))
    ]
    left = [list(range(bits))[::-1] for _ in orders]
    for step in range(bits):
        moves, keeps = [], []
        for i, order in enumerate(orders):
            axis = left[i].index(order[step])
            left[i].pop(axis)
            mine = (index >> order[step]) & 1
            send = lax.dynamic_index_in_dim(held[i], 1 - mine, axis, keepdims=False)
            keeps.append(lax.dynamic_index_in_dim(held[i], mine, axis, keepdims=False))
            moves.append((send, *swaps("fsdp", 1 << order[step])))
        arrived = yield moves
        held = [
            (keep.astype(F32) + got.astype(F32)).astype(BF16) for keep, got in zip(keeps, arrived)
        ]
    return jnp.concatenate(held, axis=0)


def line_steps(mine, other):
    count = lax.axis_size("ctx")
    line = count // 2
    place = lax.axis_index("ctx") // 2
    (got,) = yield [(other, *swaps("ctx", 1))]

    def block(target):
        target = jnp.clip(target, 0, line - 1)
        return sum(
            lax.dynamic_index_in_dim(half, target, 0, keepdims=False).astype(F32)
            for half in (mine, got)
        )

    for step in range(line - 1):
        far = line - 1 - step
        up = block(place + far)
        down = block(place - far)
        if step:
            up, down = up + ups.astype(F32), down + downs.astype(F32)
        ups, downs = yield [
            (up.astype(BF16), "ctx", [(i, i + 2) for i in range(count - 2) if i // 2 + far < line]),
            (down.astype(BF16), "ctx", [(i, i - 2) for i in range(2, count) if i // 2 - far >= 0]),
        ]
    return block(place) + ups.astype(F32) + downs.astype(F32)


def total_steps(vector):
    for axis in ("ctx", "fsdp"):
        for bit in bits_of(axis):
            (got,) = yield [(vector, *swaps(axis, 1 << bit))]
            vector = vector + got
    return vector


def turn(values, cosine, sine):
    lane = lax.broadcasted_iota(jnp.int32, values.shape, 1) % HEAD_DIM
    half = ROT // 2
    partner = jnp.where(
        lane < half, pltpu.roll(values, LANES - half, 1), pltpu.roll(values, half, 1)
    )
    return values * cosine + partner * sine


def first_half(shape):
    return lax.broadcasted_iota(jnp.int32, shape, 1) < HEAD_DIM


def visible_range(ends_ref, step, tile):
    top = step * tile
    column = top + lax.broadcasted_iota(jnp.int32, (1, tile), 1)
    begin = jnp.zeros((1, tile), jnp.int32)
    first = jnp.int32(0)
    for sequence in range(ends_ref.shape[0]):
        end = ends_ref[sequence]
        begin = jnp.where(column >= end, jnp.maximum(begin, end), begin)
        first = jnp.where(top >= end, jnp.maximum(first, end), first)
    return column, begin, first // tile


def each_head(values, axis=1):
    half = lax.broadcasted_iota(jnp.int32, values.shape, axis) < HEAD_DIM
    zero = jnp.zeros_like(values)
    return [jnp.where(half, values, zero), jnp.where(half, zero, values)]


def part_lanes(pair, which):
    start = (3 * pair + which) * LANES
    return slice(start, start + LANES)


def forward_kernel(
    place_ref, ends_ref, cos_ref, sin_ref, lin_hbm,
    att_hbm, rows, summed_ref, lse_ref, lin, values_t, att, sems,
):
    tokens = lin.shape[0]
    tile = TILE
    tiles = tokens // tile
    blocks = tokens // BLK
    pairs = lin.shape[1] // LANES // 3
    heads = 2 * pairs

    @pl.loop(0, blocks)
    def _(block):
        source = pl.ds(pl.multiple_of(block * BLK, BLK), BLK)
        target = pl.ds(pl.multiple_of(place_ref[block] * BLK, BLK), BLK)
        pltpu.make_async_copy(lin_hbm.at[source], lin.at[target], sems.at[0]).start()

    pltpu.make_async_copy(lin_hbm, lin, sems.at[0]).wait()

    @pl.loop(0, tiles)
    def _(step):
        part = pl.ds(pl.multiple_of(step * tile, tile), tile)
        cosine, sine = cos_ref[part, :], sin_ref[part, :]
        for pair in range(pairs):
            q, k, v = (part_lanes(pair, i) for i in range(3))
            query = turn(lin[part, q], cosine, sine) * HEAD_DIM ** (-0.5)
            rows[part, q] = query.astype(BF16)
            rows[part, k] = turn(lin[part, k], cosine, sine).astype(BF16)
            value = lin[part, v].astype(BF16)
            rows[part, v] = value
            values_t[pair * LANES : (pair + 1) * LANES, part] = value.T

    @pl.loop(0, tiles)
    def _(step):
        part = pl.ds(pl.multiple_of(step * tile, tile), tile)
        column, begin, low = visible_range(ends_ref, step, tile)
        queries = [item for pair in range(pairs) for item in each_head(rows[part, part_lanes(pair, 0)].T, 0)]
        summed_ref[:, part] = jnp.zeros((heads * HEAD_DIM, tile), F32)

        def combine(index, state):
            there = pl.ds(pl.multiple_of(index * tile, tile), tile)
            row = index * tile + lax.broadcasted_iota(jnp.int32, (tile, tile), 0)
            visible = (row <= column) & (row >= begin)
            result = []
            for head in range(heads):
                top, total = state[head]
                here = slice(head * HEAD_DIM, (head + 1) * HEAD_DIM)
                key = rows[there, part_lanes(head // 2, 1)]
                scores = jnp.where(visible, dot_nn(key, queries[head]), -1e30)
                new_top = jnp.maximum(top, jnp.max(scores, axis=0, keepdims=True))
                weight = jnp.exp(scores - new_top)
                factor = jnp.exp(top - new_top)
                total = total * factor + jnp.sum(weight, axis=0, keepdims=True)
                summed_ref[here, part] = summed_ref[here, part] * factor + dot_nn(
                    values_t[here, there], weight.astype(BF16)
                )
                result.append((new_top, total))
            return tuple(result)

        empty = (jnp.full((1, tile), -1e30, F32), jnp.zeros((1, tile), F32))
        state = lax.fori_loop(low, step + 1, combine, (empty,) * heads)
        for head in range(heads):
            top, total = state[head]
            here = slice(head * HEAD_DIM, (head + 1) * HEAD_DIM)
            summed_ref[here, part] = summed_ref[here, part] * (1.0 / total)
            lse_ref[head : head + 1, part] = top + jnp.log(total)
        for pair in range(pairs):
            lanes = slice(pair * LANES, (pair + 1) * LANES)
            att[part, lanes] = summed_ref[lanes, part].T.astype(BF16)

    @pl.loop(0, blocks)
    def _(block):
        target = pl.ds(pl.multiple_of(block * BLK, BLK), BLK)
        source = pl.ds(pl.multiple_of(place_ref[block] * BLK, BLK), BLK)
        pltpu.make_async_copy(att.at[source], att_hbm.at[target], sems.at[0]).start()

    pltpu.make_async_copy(att, att_hbm, sems.at[0]).wait()


def backward_kernel(
    place_ref, ends_ref, cos_ref, sin_ref, rows, summed_ref, lse_ref, grad_hbm,
    mixed_hbm, grad, grad_t, keys_t, grad_q, grad_k, grad_v, mixed, sems,
):
    tokens = grad.shape[0]
    tile = TILE
    tiles = tokens // tile
    blocks = tokens // BLK
    pairs = grad.shape[1] // LANES
    heads = 2 * pairs

    @pl.loop(0, blocks)
    def _(block):
        source = pl.ds(pl.multiple_of(block * BLK, BLK), BLK)
        target = pl.ds(pl.multiple_of(place_ref[block] * BLK, BLK), BLK)
        pltpu.make_async_copy(grad_hbm.at[source], grad.at[target], sems.at[0]).start()

    grad_k[...] = jnp.zeros_like(grad_k)
    grad_v[...] = jnp.zeros_like(grad_v)

    @pl.loop(0, tiles)
    def _(step):
        part = pl.ds(pl.multiple_of(step * tile, tile), tile)
        for pair in range(pairs):
            keys_t[pair * LANES : (pair + 1) * LANES, part] = rows[part, part_lanes(pair, 1)].T

    pltpu.make_async_copy(grad_hbm, grad, sems.at[0]).wait()

    @pl.loop(0, tiles)
    def _(step):
        part = pl.ds(pl.multiple_of(step * tile, tile), tile)
        column, begin, low = visible_range(ends_ref, step, tile)
        queries, backs, delta, lse, queries_t, backs_t = [], [], [], [], [], []
        for pair in range(pairs):
            lanes = slice(pair * LANES, (pair + 1) * LANES)
            queries += each_head(rows[part, part_lanes(pair, 0)])
            backs += each_head(grad[part, lanes])
            queries_t += each_head(rows[part, part_lanes(pair, 0)].T, 0)
            backs_t += each_head(grad[part, lanes].T, 0)
            grad_t[lanes, :] = grad[part, lanes].T.astype(F32)
        for head in range(heads):
            here = slice(head * HEAD_DIM, (head + 1) * HEAD_DIM)
            delta.append(jnp.sum(summed_ref[here, part] * grad_t[here, :], axis=0, keepdims=True))
            lse.append(lse_ref[head : head + 1, part])
        grad_q[...] = jnp.zeros_like(grad_q)

        def back_step(index, _):
            there = pl.ds(pl.multiple_of(index * tile, tile), tile)
            row = index * tile + lax.broadcasted_iota(jnp.int32, (tile, tile), 0)
            visible = (row <= column) & (row >= begin)
            for head in range(heads):
                pair = head // 2
                lanes = slice(pair * LANES, (pair + 1) * LANES)
                here = slice(head * HEAD_DIM, (head + 1) * HEAD_DIM)
                key, value = rows[there, part_lanes(pair, 1)], rows[there, part_lanes(pair, 2)]
                scores = jnp.where(visible, dot_nn(key, queries_t[head]), -1e30)
                weight = jnp.exp(scores - lse[head])
                grad_w = dot_nn(value, backs_t[head])
                grad_s = (weight * (grad_w - delta[head])).astype(BF16)
                part_k = dot_nn(grad_s, queries[head])
                part_v = dot_nn(weight.astype(BF16), backs[head])
                add_k = part_k if head % 2 == 0 else add_k + part_k
                add_v = part_v if head % 2 == 0 else add_v + part_v
                grad_q[here, :] += dot_nn(keys_t[here, there], grad_s)
                if head % 2:
                    grad_k[there, lanes] += add_k
                    grad_v[there, lanes] += add_v
            return 0

        lax.fori_loop(low, step + 1, back_step, 0)
        for pair in range(pairs):
            lanes = slice(pair * LANES, (pair + 1) * LANES)
            turned = turn(grad_q[lanes, :].T * HEAD_DIM ** (-0.5), cos_ref[part, :], -sin_ref[part, :])
            mixed[part, part_lanes(pair, 0)] = turned.astype(BF16)

    @pl.loop(0, tiles)
    def _(step):
        part = pl.ds(pl.multiple_of(step * tile, tile), tile)
        cosine, sine = cos_ref[part, :], sin_ref[part, :]
        for pair in range(pairs):
            lanes = slice(pair * LANES, (pair + 1) * LANES)
            mixed[part, part_lanes(pair, 1)] = turn(grad_k[part, lanes], cosine, -sine).astype(BF16)
            mixed[part, part_lanes(pair, 2)] = grad_v[part, lanes].astype(BF16)

    @pl.loop(0, blocks)
    def _(block):
        target = pl.ds(pl.multiple_of(block * BLK, BLK), BLK)
        source = pl.ds(pl.multiple_of(place_ref[block] * BLK, BLK), BLK)
        pltpu.make_async_copy(mixed.at[source], mixed_hbm.at[target], sems.at[0]).start()

    pltpu.make_async_copy(mixed, mixed_hbm, sems.at[0]).wait()


def turn_tables(ends, tokens):
    position = jnp.arange(tokens, dtype=jnp.int32)
    begin = jnp.max(jnp.where(position[:, None] >= ends[None, :], ends[None, :], 0), axis=1)
    within = (position - begin).astype(F32)
    half = ROT // 2
    frequency = 10000.0 ** (-jnp.arange(half, dtype=F32) * 2.0 / ROT)
    angles = within[:, None] * frequency[None, :]
    cosine, sine = jnp.cos(angles), jnp.sin(angles)
    ones = jnp.ones((tokens, HEAD_DIM - ROT), F32)
    cos_table = jnp.concatenate([cosine, cosine, ones] * 2, axis=1)
    sin_table = jnp.concatenate([-sine, sine, 0.0 * ones] * 2, axis=1)
    return cos_table, sin_table


SMEM = pl.BlockSpec(memory_space=pltpu.SMEM)
VMEM = pl.BlockSpec(memory_space=pltpu.VMEM)
ANYWHERE = pl.BlockSpec(memory_space=pl.ANY)


def attention_forward(block_place, ends, tables, linear):
    tokens, width3 = linear.shape
    width = width3 // 3
    return pl.pallas_call(
        forward_kernel,
        out_shape=(
            jax.ShapeDtypeStruct((tokens, width), BF16),
            jax.ShapeDtypeStruct((tokens, width3), BF16),
            jax.ShapeDtypeStruct((width, tokens), F32),
            jax.ShapeDtypeStruct((width // HEAD_DIM, tokens), F32),
        ),
        in_specs=[SMEM, SMEM, VMEM, VMEM, ANYWHERE],
        out_specs=(ANYWHERE, VMEM, VMEM, VMEM),
        scratch_shapes=[
            pltpu.VMEM((tokens, width3), F32),
            pltpu.VMEM((width, tokens), BF16),
            pltpu.VMEM((tokens, width), BF16),
            pltpu.SemaphoreType.DMA((1,)),
        ],
        compiler_params=pltpu.CompilerParams(vmem_limit_bytes=48 << 20),
        cost_estimate=pl.CostEstimate(
            flops=40 * 10**9, bytes_accessed=16 * 10**6, transcendentals=0
        ),
    )(block_place, ends, *tables, linear)


def attention_backward(block_place, ends, tables, kept, grad_att):
    tokens, width = grad_att.shape
    return pl.pallas_call(
        backward_kernel,
        out_shape=jax.ShapeDtypeStruct((tokens, 3 * width), BF16),
        in_specs=[SMEM, SMEM] + [VMEM] * 5 + [ANYWHERE],
        out_specs=ANYWHERE,
        scratch_shapes=[
            pltpu.VMEM((tokens, width), BF16),
            pltpu.VMEM((width, TILE), F32),
            pltpu.VMEM((width, tokens), BF16),
            pltpu.VMEM((width, TILE), F32),
            pltpu.VMEM((tokens, width), F32),
            pltpu.VMEM((tokens, width), F32),
            pltpu.VMEM((tokens, 3 * width), BF16),
            pltpu.SemaphoreType.DMA((1,)),
        ],
        compiler_params=pltpu.CompilerParams(vmem_limit_bytes=48 << 20),
        cost_estimate=pl.CostEstimate(
            flops=40 * 10**9, bytes_accessed=16 * 10**6, transcendentals=0
        ),
    )(block_place, ends, *tables, *kept, grad_att)

def row_call(kernel, where, rows, whole, assembled, outs, sums, flops, split=False):
    count = rows[0].shape[0]
    tiles = count // TILE
    shards = lax.axis_size("fsdp")
    pieces = [piece for _, group in assembled for _, _, piece in group]
    scratch = [
        pltpu.VMEM(
            (height * (shards if group[0][0] is not None else 1), group[0][2].shape[1]), BF16
        )
        for height, group in assembled
    ]

    def tile_of(step, at):
        return step % (tiles // 2) * 2 + (at[1] ^ (step // (tiles // 2))) if split else step

    def body(at, *refs):
        inputs = refs[: len(rows) + len(whole)]
        sources = refs[len(inputs) : len(inputs) + len(pieces)]
        targets = refs[len(inputs) + len(pieces) : -len(scratch) - 1]
        buffers, sems = refs[-len(scratch) - 1 : -1], refs[-1]

        @pl.when(pl.program_id(0) == 0)
        def _():
            copies = []
            for buffer, (height, group) in zip(buffers, assembled):
                for mask, start, piece in group:
                    first = start if mask is None else (at[0] ^ mask) * height + start
                    size = piece.shape[0]
                    target = buffer.at[pl.ds(pl.multiple_of(first, size), size)]
                    slot = len(copies)
                    copies.append(pltpu.make_async_copy(sources[slot], target, sems.at[slot]))
            for copy in copies:
                copy.start()
            for copy in copies:
                copy.wait()

        if not split:
            kernel(*inputs, *buffers, *targets)
            return
        mine, other, *rest = targets

        @pl.when(pl.program_id(0) < tiles // 2)
        def _():
            kernel(*inputs, *buffers, mine.at[0], *rest)

        @pl.when(pl.program_id(0) >= tiles // 2)
        def _():
            kernel(*inputs, *buffers, other.at[0], *rest)

    by_tile = lambda columns: pl.BlockSpec((TILE, columns), lambda i, at: (tile_of(i, at), 0))
    stay = lambda shape: pl.BlockSpec(shape, lambda i, at: (0, 0))
    moved = sum(item.size * item.dtype.itemsize for item in (*rows, *whole, *pieces))
    moved += sum(count * columns * jnp.dtype(kind).itemsize for columns, kind in outs)
    if split:
        ((columns, kind),) = outs
        half = tiles // 2
        out_shape = [jax.ShapeDtypeStruct((half, TILE, columns), kind)] * 2
        out_specs = [
            pl.BlockSpec((1, TILE, columns), lambda i, at: (jnp.minimum(i, half - 1), 0, 0)),
            pl.BlockSpec((1, TILE, columns), lambda i, at: (jnp.maximum(i - half, 0), 0, 0)),
        ]
    else:
        out_shape = [jax.ShapeDtypeStruct((count, columns), kind) for columns, kind in outs]
        out_specs = [by_tile(columns) for columns, _ in outs]
    return pl.pallas_call(
        body,
        out_shape=out_shape + [jax.ShapeDtypeStruct(shape, F32) for shape in sums],
        grid_spec=pltpu.PrefetchScalarGridSpec(
            num_scalar_prefetch=1,
            grid=(tiles,),
            in_specs=[by_tile(item.shape[1]) for item in rows]
            + [stay(item.shape) for item in whole]
            + [ANYWHERE] * len(pieces),
            out_specs=out_specs + [stay(shape) for shape in sums],
            scratch_shapes=[*scratch, pltpu.SemaphoreType.DMA((len(pieces),))],
        ),
        compiler_params=pltpu.CompilerParams(vmem_limit_bytes=56 << 20),
        cost_estimate=pl.CostEstimate(flops=flops, bytes_accessed=moved, transcendentals=0),
    )(where, *rows, *whole, *pieces)


def chunks_of(columns, size=256):
    return [slice(start, min(start + size, columns)) for start in range(0, columns, size)]


def standard(rows):
    values = rows.astype(F32)
    centred = values - jnp.mean(values, axis=1, keepdims=True)
    inv_std = lax.rsqrt(jnp.mean(centred * centred, axis=1, keepdims=True) + 1e-05)
    return centred * inv_std, inv_std


def enter_kernel(
    tokens, gain, shift, bias, inner, normed_out, slope_out, active_out, linear_out
):
    scaled, _ = standard(tokens[...])
    normed = (scaled * gain[...] + shift[...]).astype(BF16)
    normed_out[...] = normed
    units = active_out.shape[1]
    for part in chunks_of(units):
        hidden = dot_nn(normed, inner[:, part]) + bias[:, part]
        square = hidden * hidden
        bent = jnp.tanh(0.7978845608028654 * hidden * (1.0 + 0.044715 * square))
        active_out[:, part] = (0.5 * hidden * (1.0 + bent)).astype(BF16)
        slope = (1.0 - bent * bent) * (0.7978845608028654 * (1.0 + 0.134145 * square))
        slope_out[:, part] = 0.5 * (1.0 + bent + hidden * slope)
    for part in chunks_of(linear_out.shape[1]):
        there = slice(units + part.start, units + part.stop)
        linear_out[:, part] = dot_nn(normed, inner[:, there]) + bias[:, there]


def back_kernel(first, second, slope, down, out, hidden_out, att_out, hidden_sum):
    @pl.when(pl.program_id(0) == 0)
    def _():
        hidden_sum[...] = jnp.zeros_like(hidden_sum)

    left, right = first[...], second[...]
    middle = left.shape[1]

    def back(weights, part):
        return dot_nt(left, weights[part, :middle]) + dot_nt(right, weights[part, middle:])

    for part in chunks_of(down.shape[0]):
        grad = (back(down, part) * slope[:, part]).astype(BF16)
        hidden_out[:, part] = grad
        hidden_sum[:, part] += jnp.sum(grad.astype(F32), axis=0, keepdims=True)
    for part in chunks_of(out.shape[0]):
        att_out[:, part] = back(out, part).astype(BF16)


def leave_kernel(attended, active, out, down, result):
    left, right = attended[...], active[...]
    for part in chunks_of(out.shape[1], 512):
        result[:, part] = (dot_nn(left, out[:, part]) + dot_nn(right, down[:, part])).astype(BF16)


def norm_back_kernel(tokens, mixed, hidden, inner, result, gain_sum, shift_sum, mixed_sum):
    @pl.when(pl.program_id(0) == 0)
    def _():
        for total in (gain_sum, shift_sum, mixed_sum):
            total[...] = jnp.zeros_like(total)

    scaled, _ = standard(tokens[...])
    left, right = mixed[...], hidden[...]
    mixed_sum[...] += jnp.sum(left.astype(F32), axis=0, keepdims=True)
    units = right.shape[1]
    for part in chunks_of(inner.shape[0], 512):
        grad = dot_nt(left, inner[part, units:]) + dot_nt(right, inner[part, :units])
        result[:, part] = grad.astype(BF16)
        shift_sum[:, part] += jnp.sum(grad, axis=0, keepdims=True)
        gain_sum[:, part] += jnp.sum(grad * scaled[:, part], axis=0, keepdims=True)


def pick_kernel(plans, index_ref, *refs):
    *weights, target, tiles, sems = refs
    at = index_ref[0]
    count = plans[0][2]
    copies, late, slot, column = [], [], 0, 0
    for weight, (unit, order, _) in zip(weights, plans):
        if unit % LANES == 0:
            for place in order:
                first = pl.multiple_of((place * count + at) * unit, unit)
                copies.append(
                    (weight.at[:, pl.ds(first, unit)], target.at[:, column : column + unit])
                )
                column += unit
            continue
        for one, two in zip(order[::2], order[1::2]):
            for which, place in enumerate((one, two)):
                first = pl.multiple_of((place * count + at) // 2 * LANES, LANES)
                copies.append((weight.at[:, pl.ds(first, LANES)], tiles.at[slot, which]))
            late.append((slot, column))
            slot, column = slot + 1, column + LANES
    copies = [
        pltpu.make_async_copy(source, there, sems.at[i])
        for i, (source, there) in enumerate(copies)
    ]
    for copy in copies:
        copy.start()
    for copy in copies:
        copy.wait()
    for slot, column in late:
        first, second = tiles[slot, 0].astype(F32), tiles[slot, 1].astype(F32)
        odd = at % 2 == 1
        first = jnp.where(odd, pltpu.roll(first, HEAD_DIM, 1), first)
        second = jnp.where(odd, second, pltpu.roll(second, HEAD_DIM, 1))
        target[:, column : column + LANES] = jnp.where(
            first_half(first.shape), first, second
        ).astype(target.dtype)


def pick_columns(weights, units, orders, index, count):
    rows = weights[0].shape[0]
    width = sum(unit * len(order) for unit, order in zip(units, orders))
    narrow = [len(order) // 2 for unit, order in zip(units, orders) if unit % LANES]
    copies = sum(len(order) for order in orders)
    return pl.pallas_call(
        functools.partial(pick_kernel, [(unit, order, count) for unit, order in zip(units, orders)]),
        out_shape=jax.ShapeDtypeStruct((rows, width), weights[0].dtype),
        in_specs=[SMEM] + [ANYWHERE] * len(weights),
        out_specs=VMEM,
        scratch_shapes=[
            pltpu.VMEM((sum(narrow), 2, rows, LANES), weights[0].dtype),
            pltpu.SemaphoreType.DMA((copies,)),
        ],
        compiler_params=pltpu.CompilerParams(vmem_limit_bytes=32 << 20),
        cost_estimate=pl.CostEstimate(
            flops=0, bytes_accessed=4 * rows * width, transcendentals=0
        ),
    )(index.reshape(1), *weights)


def deal_kernel(unit, order, turn_ref, parts, target, *rest):
    count = parts.shape[0]
    for group, place in enumerate(order):
        if unit % LANES == 0:
            for owner in range(count):
                start = (place * count + owner) * unit
                target[:, start : start + unit] = parts[
                    owner, :, group * unit : (group + 1) * unit
                ].astype(F32)
            continue
        tile = slice(group // 2 * LANES, (group // 2 + 1) * LANES)
        for owner in range(0, count, 2):
            first = parts[owner, :, tile].astype(F32)
            second = parts[owner + 1, :, tile].astype(F32)
            if group % 2:
                first = pltpu.roll(first, HEAD_DIM, 1)
            else:
                second = pltpu.roll(second, HEAD_DIM, 1)
            start = (place * count + owner) * unit
            target[:, start : start + LANES] = jnp.where(
                first_half(first.shape), first, second
            )
    for out in rest:
        slots = out.shape[0] // HEAD_DIM
        for slot in range(slots):
            owner = slot if slots == count else turn_ref[0] * slots + slot
            out[slot * HEAD_DIM : (slot + 1) * HEAD_DIM, :] = parts[
                owner, :, len(order) * unit :
            ].astype(F32)


def deal_columns(parts, unit, order, turn_index, with_out=False):
    count, rows, columns = parts.shape
    width = len(order) * unit
    step = HEAD_DIM
    out_shape = [jax.ShapeDtypeStruct((rows, count * width), F32)]
    out_specs = [pl.BlockSpec((step, count * width), lambda i, at: (i, 0))]
    if with_out:
        out_shape.append(jax.ShapeDtypeStruct((rows, (columns - width) * (rows // step)), F32))
        out_specs.append(pl.BlockSpec((rows, columns - width), lambda i, at: (0, i)))
    return pl.pallas_call(
        functools.partial(deal_kernel, unit, order),
        out_shape=out_shape,
        grid_spec=pltpu.PrefetchScalarGridSpec(
            num_scalar_prefetch=1,
            grid=(rows // step,),
            in_specs=[pl.BlockSpec((count, step, columns), lambda i, at: (0, i, 0))],
            out_specs=out_specs,
        ),
        compiler_params=pltpu.CompilerParams(vmem_limit_bytes=32 << 20),
        cost_estimate=pl.CostEstimate(
            flops=0, bytes_accessed=6 * rows * count * columns, transcendentals=0
        ),
    )(turn_index.reshape(1), parts)


def join_kernel(turns, turn_ref, left, *refs):
    *pieces, target = refs
    width = left.shape[1]
    size = target.shape[1] - width
    target[:, :width] = left[...]
    keep = pl.program_id(0) % turns == turn_ref[0]
    for piece_index, piece in enumerate(pieces):
        for chunk in range(piece.shape[1] // size):
            value = piece[:, chunk * size : (chunk + 1) * size]
            if turns > 1:
                value = jnp.where(keep, value, jnp.zeros_like(value))
            row = (piece_index * (piece.shape[1] // size) + chunk) * HEAD_DIM
            target[row : row + HEAD_DIM, width:] = value


def join_terms(left, pieces, shards, turns, turn_index):
    rows = left.shape[0] // shards
    extra = sum(piece.shape[1] for piece in pieces) * HEAD_DIM // rows
    width = left.shape[1]
    return pl.pallas_call(
        functools.partial(join_kernel, turns),
        out_shape=jax.ShapeDtypeStruct((left.shape[0], width + extra), left.dtype),
        grid_spec=pltpu.PrefetchScalarGridSpec(
            num_scalar_prefetch=1,
            grid=(shards,),
            in_specs=[pl.BlockSpec((rows, width), lambda i, at: (i, 0))]
            + [
                pl.BlockSpec((HEAD_DIM, piece.shape[1]), lambda i, at: (i // turns, 0))
                for piece in pieces
            ],
            out_specs=pl.BlockSpec((rows, width + extra), lambda i, at: (i, 0)),
        ),
        cost_estimate=pl.CostEstimate(
            flops=0, bytes_accessed=4 * left.shape[0] * (width + extra), transcendentals=0
        ),
    )(turn_index.reshape(1), left, *pieces)


def side_kernel(*refs):
    *pieces, target = refs
    start = 0
    for piece in pieces:
        target[:, start : start + piece.shape[1]] = piece[...].astype(F32)
        start += piece.shape[1]


def side_by_side(*pieces):
    rows = pieces[0].shape[0]
    width = sum(piece.shape[1] for piece in pieces)
    return pl.pallas_call(
        side_kernel,
        out_shape=jax.ShapeDtypeStruct((rows, width), F32),
        grid=(rows // TILE,),
        in_specs=[pl.BlockSpec((TILE, piece.shape[1]), lambda i: (i, 0)) for piece in pieces],
        out_specs=pl.BlockSpec((TILE, width), lambda i: (i, 0)),
        cost_estimate=pl.CostEstimate(flops=0, bytes_accessed=6 * rows * width, transcendentals=0),
    )(*pieces)


def after(value, *others):
    return lax.optimization_barrier((value,) + others)[0]


def shards(
    tokens,
    block_place,
    seq_lengths,
    norm_gain,
    norm_bias,
    qkv_weight,
    qkv_bias,
    out_weight,
    out_bias,
    up_weight,
    up_bias,
    down_weight,
    down_bias,
    out_grad,
):
    ctx_count, ctx_index = lax.axis_size("ctx"), lax.axis_index("ctx")
    shard_count, shard_index = lax.axis_size("fsdp"), lax.axis_index("fsdp")
    own_tokens, own_grad = tokens[0], out_grad[0]
    own_rows, model_width = own_tokens.shape
    hidden_width = up_weight.shape[1]
    heads = model_width // HEAD_DIM
    own_heads = heads // ctx_count
    shard_heads = heads // shard_count
    unit = hidden_width // shard_count // ctx_count
    own_width = own_heads * HEAD_DIM
    head_turns = ctx_count // shard_heads
    low_first = list(bits_of("fsdp"))
    high_first = low_first[::-1]

    def pick(value, axis):
        return lax.dynamic_index_in_dim(value, ctx_index, axis, keepdims=False)

    half_width = model_width // 2
    pairs = own_heads // 2

    def section_order(slot):
        pair, rest = slot // 6, slot % 6
        return rest // 2 * own_heads + pair * 2 + rest % 2

    def by_ctx(value):
        return lax.all_gather(value, "ctx", axis=0, tiled=True)

    def as_row(value):
        return value.reshape(1, -1)

    token_count = ctx_count * own_rows
    units = shard_count * unit
    flops = 2 * token_count * model_width
    shard_rows = model_width // shard_count
    both = (low_first, high_first)
    qkv_order = [section_order(slot) for slot in range(3 * own_heads)]
    turn_index, head_slot = ctx_index // shard_heads, ctx_index % shard_heads
    where = jnp.stack([shard_index, ctx_index % 2]).astype(jnp.int32)

    all_tokens = by_ctx(own_tokens)
    own_inner = pick_columns(
        [up_weight, qkv_weight],
        [unit, HEAD_DIM],
        [list(range(shard_count)), qkv_order],
        ctx_index,
        ctx_count,
    )
    vectors = (norm_gain, norm_bias, qkv_bias, out_bias, up_bias, down_bias)
    inner_flow = Flow(gather_steps(own_inner, *both))
    vector_flow = Flow(direct_steps(jnp.concatenate(vectors).reshape(8, -1)))
    grad_first = by_ctx(after(own_grad[:, :half_width], own_inner))

    def prepare(ends, down_weight, out_weight):
        own_down = pick(down_weight.reshape(ctx_count, unit, model_width), 0)
        own_out = lax.dynamic_index_in_dim(
            out_weight.reshape(shard_heads, HEAD_DIM, model_width), head_slot, 0, keepdims=False
        )
        return own_down, own_out, turn_tables(ends, token_count)

    ends = jnp.cumsum(seq_lengths[0]).astype(jnp.int32)
    own_down, own_out, tables = beside(
        prepare, (ends, down_weight, out_weight), [inner_flow, vector_flow]
    )
    grad_second = by_ctx(after(own_grad[:, half_width:], own_down))
    packed = jnp.stack([piece.reshape(-1) for _, _, piece in vector_flow.result])
    packed = jnp.concatenate(
        [lax.dynamic_index_in_dim(packed, shard_index ^ i, 0) for i in range(shard_count)]
    )
    cuts = [0]
    for vector in vectors:
        cuts.append(cuts[-1] + vector.shape[0])
    gain_all, shift_all, qkv_bias_all, out_bias_all, up_bias_all, down_bias_all = [
        packed[:, start:stop].reshape(-1).astype(F32) for start, stop in zip(cuts, cuts[1:])
    ]
    own_qkv_bias = pick(qkv_bias_all.reshape(3, pairs, 2, ctx_count, HEAD_DIM), 3)
    own_qkv_bias = jnp.transpose(own_qkv_bias, (1, 0, 2, 3)).reshape(-1)
    own_up_bias = pick(up_bias_all.reshape(shard_count, ctx_count, unit), 1).reshape(-1)
    inner_bias = jnp.concatenate([own_up_bias, own_qkv_bias])
    while inner_flow.moves:
        own_down, own_out, inner_bias = beside(
            lambda *same: same, (own_down, own_out, inner_bias), [inner_flow]
        )
    inner = (shard_rows, inner_flow.result)
    down_flow = Flow(gather_steps(own_down, *both))
    out_flow = Flow(direct_steps(own_out))

    def enter(rows):
        return row_call(
            enter_kernel,
            where,
            [rows],
            [as_row(gain_all), as_row(shift_all), as_row(inner_bias)],
            [inner],
            [(model_width, BF16), (units, F32), (units, BF16), (3 * own_width, F32)],
            [],
            flops * (units + 3 * own_width),
        )

    normed, slope, active, linear = beside(enter, (all_tokens,), [down_flow, out_flow])
    attended, *kept = beside(
        lambda rows: attention_forward(block_place, ends, tables, rows), (linear,), [down_flow]
    )
    while down_flow.moves:
        attended = beside(lambda same: same, (attended,), [down_flow])
    down = (unit, down_flow.result)
    out = (HEAD_DIM, out_flow.result)
    if head_turns > 1:
        out_all = jnp.stack([piece for _, _, piece in out_flow.result])
        out_all = jnp.concatenate(
            [
                lax.dynamic_index_in_dim(
                    out_all, shard_index ^ (i * head_turns + turn_index), 0, keepdims=False
                )
                for i in range(own_heads)
            ]
        )
        out = (own_width, [(None, 0, out_all)])

    def down_terms(rows):
        return dot_tn(active, rows).astype(BF16).reshape(shard_count, unit, half_width)

    first_terms = down_terms(after(grad_first, attended))
    first_flow = Flow(scatter_steps(first_terms, *both))

    def leave(rows):
        return row_call(
            leave_kernel,
            where,
            [rows, active],
            [],
            [out, down],
            [(model_width, BF16)],
            [],
            flops * (units + own_width),
            split=True,
        )

    line_flow = Flow(line_steps(*beside(leave, (attended,), [first_flow])))
    grad_second = beside(lambda same: same, (grad_second,), [first_flow, line_flow])
    while first_flow.moves:
        grad_second = beside(lambda same: same, (grad_second,), [first_flow])
    second_terms = beside(down_terms, (grad_second,), [], late=[line_flow])
    second_flow = Flow(scatter_steps(second_terms, *both))

    def back(rows):
        return row_call(
            back_kernel,
            where,
            [grad_first, rows, slope],
            [],
            [down, out],
            [(units, BF16), (own_width, BF16)],
            [(1, units)],
            flops * (units + own_width),
        )

    grad_hidden, grad_att, hidden_sum = beside(
        back, (grad_second,), [second_flow], early=[line_flow]
    )
    up_terms = beside(
        lambda rows: dot_tn(normed, rows).astype(BF16),
        (grad_hidden,),
        [second_flow],
        late=[line_flow],
    )
    up_flow = Flow(scatter_steps(up_terms.reshape(shard_count, shard_rows, units), *both))
    grad_mixed = beside(
        lambda rows: attention_backward(block_place, ends, tables, kept, rows),
        (grad_att,),
        [up_flow],
        early=[line_flow],
    )

    def joint(rows):
        out_terms = [dot_tn(attended, piece).astype(BF16) for piece in (grad_first, grad_second)]
        return join_terms(
            dot_tn(normed, rows).astype(BF16), out_terms, shard_count, head_turns, turn_index
        )

    joint_terms = beside(joint, (grad_mixed,), [up_flow, line_flow])
    joint_flow = Flow(
        scatter_steps(joint_terms.reshape(shard_count, shard_rows, -1), *both)
    )

    def norm_back(rows):
        return row_call(
            norm_back_kernel,
            where,
            [all_tokens, rows, grad_hidden],
            [],
            [inner],
            [(model_width, BF16)],
            [(1, model_width), (1, model_width), (1, 3 * own_width)],
            flops * (units + 3 * own_width),
            split=True,
        )

    mine, other, gain_sum, shift_sum, mixed_sum = beside(norm_back, (grad_mixed,), [joint_flow])
    for flow in (second_flow, up_flow, line_flow):
        while flow.moves:
            mine = beside(lambda same: same, (mine,), [flow])

    def spread(value, count):
        value = value.reshape(count, 1, -1)
        whole = jnp.zeros((count, ctx_count, value.shape[2]), F32)
        return lax.dynamic_update_slice_in_dim(whole, value, ctx_index, 1).reshape(-1)

    grad_float = own_grad.astype(F32)
    mixed_sum = jnp.transpose(mixed_sum.reshape(pairs, 3, 2 * HEAD_DIM), (1, 0, 2))
    sums = (
        gain_sum.reshape(-1),
        shift_sum.reshape(-1),
        spread(mixed_sum, 3 * own_heads),
        jnp.sum(grad_float, axis=0),
        spread(hidden_sum, shard_count),
    )
    total_flow = Flow(total_steps(jnp.concatenate(sums)))
    norm_flow = Flow(line_steps(mine, other))
    beside(lambda: (), (), [norm_flow, total_flow, joint_flow])
    while joint_flow.moves:
        beside(lambda: (), (), [joint_flow])
    down_total = [by_ctx(flow.result) for flow in (first_flow, second_flow)]
    up_total = by_ctx(up_flow.result).reshape(ctx_count, shard_rows, -1)
    joint_total = by_ctx(joint_flow.result).reshape(ctx_count, shard_rows, -1)
    down_total = beside(side_by_side, tuple(down_total), [norm_flow, total_flow])
    while norm_flow.moves or total_flow.moves:
        beside(lambda: (), (), [flow for flow in (norm_flow, total_flow) if flow.moves])
    grad_normed = norm_flow.result

    inputs = own_tokens.astype(F32)
    output = (inputs + line_flow.result + (out_bias_all + down_bias_all)).astype(BF16)

    scaled, inv_std = standard(own_tokens)
    grad_scaled = grad_normed * gain_all
    grad_input = inv_std * (
        grad_scaled
        - jnp.mean(grad_scaled, axis=1, keepdims=True)
        - scaled * jnp.mean(grad_scaled * scaled, axis=1, keepdims=True)
    )
    input_grad = (grad_float + grad_input).astype(BF16)

    total = total_flow.result
    own_sums, start = [], 0
    for item in sums:
        size = item.shape[0] // shard_count
        own_sums.append(lax.dynamic_slice_in_dim(total, start + shard_index * size, size))
        start += item.shape[0]
    gain_total, shift_total, qkv_bias_total, bias_total, up_bias_total = own_sums

    out_turn = shard_index % head_turns
    up_dealt = deal_columns(up_total, unit, list(range(shard_count)), out_turn)[0]
    joint_total = after(joint_total, up_dealt)
    qkv_dealt, out_dealt = deal_columns(joint_total, HEAD_DIM, qkv_order, out_turn, with_out=True)
    return (
        output[None],
        input_grad[None],
        gain_total,
        shift_total,
        qkv_dealt,
        qkv_bias_total,
        out_dealt,
        bias_total,
        up_dealt,
        up_bias_total,
        down_total,
        bias_total,
    )


def solution(mesh):
    in_specs = (
        P("fsdp", "ctx", None),
        P(),
        P("fsdp", None),
        P("fsdp"),
        P("fsdp"),
        P("fsdp", None),
        P("fsdp"),
        P("fsdp", None),
        P("fsdp"),
        P("fsdp", None),
        P("fsdp"),
        P("fsdp", None),
        P("fsdp"),
        P("fsdp", "ctx", None),
    )
    out_specs = (
        P("fsdp", "ctx", None),
        P("fsdp", "ctx", None),
        P("fsdp"),
        P("fsdp"),
        P("fsdp", None),
        P("fsdp"),
        P("fsdp", None),
        P("fsdp"),
        P("fsdp", None),
        P("fsdp"),
        P("fsdp", None),
        P("fsdp"),
    )
    return jax.shard_map(shards, mesh=mesh, in_specs=in_specs, out_specs=out_specs, check_vma=False)
```

```python
import functools

import jax
import jax.numpy as jnp
from jax import lax
from jax.experimental import pallas as pl
from jax.experimental.pallas import tpu as pltpu
from jax.sharding import PartitionSpec as P

HEAD_DIM = 64
ROT = 32
BLK = 16
TILE = 256
ROWS = 512
LANES = 128
F32 = jnp.float32
BF16 = jnp.bfloat16


def dot_nn(left, right):
    return lax.dot_general(left, right, (((1,), (0,)), ((), ())), preferred_element_type=F32)


def dot_nt(left, right):
    return lax.dot_general(left, right, (((1,), (1,)), ((), ())), preferred_element_type=F32)


def dot_tn(left, right):
    return lax.dot_general(left, right, (((0,), (0,)), ((), ())), preferred_element_type=F32)


def bits_of(axis):
    return range(lax.axis_size(axis).bit_length() - 1)


def swaps(axis, mask):
    return axis, [(i, i ^ mask) for i in range(lax.axis_size(axis))]


class Flow:
    def __init__(self, steps):
        self.steps = steps
        self.result = None
        self.moves = next(steps)

    def arrive(self, values):
        try:
            self.moves = self.steps.send(values)
        except StopIteration as stop:
            self.moves, self.result = [], stop.value


def beside(work, inputs, flows, late=(), early=()):
    starting = [*flows, *late]
    sends = [[value for value, _, _ in flow.moves] for flow in starting]
    inputs, sends = lax.optimization_barrier((inputs, sends))
    for flow, values in zip(starting, sends):
        flow.moving = [
            lax.ppermute(value, axis, pairs) for value, (_, axis, pairs) in zip(values, flow.moves)
        ]
    outputs = work(*inputs)
    ending = [*flows, *early]
    outputs, arrived = lax.optimization_barrier((outputs, [flow.moving for flow in ending]))
    for flow, values in zip(ending, arrived):
        flow.arrive(values)
    return outputs


def gather_steps(own, *orders):
    share = own.shape[0] // len(orders)
    held = [[(0, own[i * share : (i + 1) * share])] for i in range(len(orders))]
    for step in range(len(orders[0])):
        moves = [
            (piece, *swaps("fsdp", 1 << order[step]))
            for pieces, order in zip(held, orders)
            for _, piece in pieces
        ]
        arrived = iter((yield moves))
        for i, order in enumerate(orders):
            held[i] = held[i] + [(mask ^ (1 << order[step]), next(arrived)) for mask, _ in held[i]]
    return [
        (mask, i * share, piece) for i, pieces in enumerate(held) for mask, piece in pieces
    ]


def direct_steps(own):
    masks = range(1, lax.axis_size("fsdp"))
    arrived = yield [(own, *swaps("fsdp", mask)) for mask in masks]
    return [(0, 0, own)] + [(mask, 0, piece) for mask, piece in zip(masks, arrived)]


def scatter_steps(parts, *orders, fold=0):
    index = lax.axis_index("fsdp")
    bits = len(orders[0])
    share = parts.shape[1] // len(orders)
    held = [
        parts[:, i * share : (i + 1) * share].reshape((2,) * bits + (share, parts.shape[2]))
        for i in range(len(orders))
    ]
    left = [list(range(bits))[::-1] for _ in orders]
    for step in range(bits):
        moves, keeps = [], []
        for i, order in enumerate(orders):
            axis = left[i].index(order[step])
            left[i].pop(axis)
            mine = (index >> order[step]) & 1
            send = lax.dynamic_index_in_dim(held[i], 1 - mine, axis, keepdims=False)
            keeps.append(lax.dynamic_index_in_dim(held[i], mine, axis, keepdims=False))
            moves.append((send, *swaps("fsdp", 1 << order[step])))
        arrived = yield moves
        held = [
            (keep.astype(F32) + got.astype(F32)).astype(BF16) for keep, got in zip(keeps, arrived)
        ]
    return jnp.concatenate(held, axis=fold)


def weave_steps(own, mine, other):
    count = lax.axis_size("ctx")
    line = count // 2
    place = lax.axis_index("ctx") // 2
    alike = own.shape == mine.shape[1:]
    forth = [(i, i + 2) for i in range(count - 2)]
    back = [(i, i - 2) for i in range(2, count)]
    ups, downs = [], []
    up, down, got = yield [
        (own, "ctx", forth), (own, "ctx", back), (other, *swaps("ctx", 1)),
    ]
    up_sum, down_sum = (up, down) if alike else (jnp.zeros_like(mine[0]),) * 2

    def block(target, added):
        target = jnp.clip(target, 0, line - 1)
        total = added.astype(F32)
        for half in (mine, got):
            total += lax.dynamic_index_in_dim(half, target, 0, keepdims=False).astype(F32)
        return total

    for step in range(2, line + 1):
        ups.append(up)
        downs.append(down)
        far = line + 1 - step
        up_sum = block(place + far, up_sum).astype(BF16)
        down_sum = block(place - far, down_sum).astype(BF16)
        if step == line:
            break
        if alike:
            up_sum = jnp.where(place >= step - 1, up, up_sum)
            down_sum = jnp.where(place <= line - step, down, down_sum)
            up_sum, down_sum = yield [(up_sum, "ctx", forth), (down_sum, "ctx", back)]
            up, down = up_sum, down_sum
        else:
            up, down, up_sum, down_sum = yield [
                (up, "ctx", [(i, j) for i, j in forth if i // 2 >= step - 1]),
                (down, "ctx", [(i, j) for i, j in back if i // 2 <= line - step]),
                (up_sum, "ctx", [(i, j) for i, j in forth if i // 2 < step - 1]),
                (down_sum, "ctx", [(i, j) for i, j in back if i // 2 > line - step]),
            ]

    def at_chip(chip):
        value = own
        for away in range(1, line):
            value = jnp.where(place == chip + away, ups[away - 1], value)
            value = jnp.where(place == chip - away, downs[away - 1], value)
        return value

    def swap_cores():
        blocks = jnp.stack([at_chip(chip) for chip in range(line)])
        (beside_blocks,) = yield [(blocks, *swaps("ctx", 1))]
        return blocks, beside_blocks

    def finish():
        last_up, last_down = yield [(up_sum, "ctx", forth), (down_sum, "ctx", back)]
        return block(place, last_up) + last_down.astype(F32)

    return Flow(swap_cores()), Flow(finish())


def total_steps(vector):
    for axis in ("ctx", "fsdp"):
        for bit in bits_of(axis):
            (got,) = yield [(vector, *swaps(axis, 1 << bit))]
            vector = vector + got
    return vector


def turn(values, cosine, sine):
    lane = lax.broadcasted_iota(jnp.int32, values.shape, 1) % HEAD_DIM
    half = ROT // 2
    partner = jnp.where(
        lane < half, pltpu.roll(values, LANES - half, 1), pltpu.roll(values, half, 1)
    )
    return values * cosine + partner * sine


def first_half(shape):
    return lax.broadcasted_iota(jnp.int32, shape, 1) < HEAD_DIM


def visible_range(ends_ref, step, tile):
    top = step * tile
    column = top + lax.broadcasted_iota(jnp.int32, (1, tile), 1)
    begin = jnp.zeros((1, tile), jnp.int32)
    first = jnp.int32(0)
    for sequence in range(ends_ref.shape[0]):
        end = ends_ref[sequence]
        begin = jnp.where(column >= end, jnp.maximum(begin, end), begin)
        first = jnp.where(top >= end, jnp.maximum(first, end), first)
    return column, begin, first // tile


def each_head(values, axis=1):
    half = lax.broadcasted_iota(jnp.int32, values.shape, axis) < HEAD_DIM
    zero = jnp.zeros_like(values)
    return [jnp.where(half, values, zero), jnp.where(half, zero, values)]


Q_LANES, K_LANES, V_LANES = (slice(i * LANES, (i + 1) * LANES) for i in range(3))
HEAD_ROWS = (slice(0, HEAD_DIM), slice(HEAD_DIM, LANES))


def each_block(place_ref, act):
    @pl.loop(0, place_ref.shape[0])
    def _(block):
        act(
            pl.ds(pl.multiple_of(block * BLK, BLK), BLK),
            pl.ds(pl.multiple_of(place_ref[block] * BLK, BLK), BLK),
        )


def part_lanes(pair, which):
    start = (3 * pair + which) * LANES
    return slice(start, start + LANES)


def forward_kernel(
    place_ref, ends_ref, lin_hbm, att_hbm, rows, summed_ref, lse_ref, values_t, att, sems
):
    tokens = rows.shape[0]
    tile = TILE
    pairs = rows.shape[1] // LANES // 3
    heads = 2 * pairs
    each_block(
        place_ref,
        lambda given, natural: pltpu.make_async_copy(
            lin_hbm.at[given], rows.at[natural], sems.at[0]
        ).start(),
    )
    pltpu.make_async_copy(lin_hbm, rows, sems.at[0]).wait()

    @pl.loop(0, tokens // tile)
    def _(step):
        part = pl.ds(pl.multiple_of(step * tile, tile), tile)
        for pair in range(pairs):
            lanes = slice(pair * LANES, (pair + 1) * LANES)
            values_t[lanes, part] = rows[part, part_lanes(pair, 2)].T

    @pl.loop(0, tokens // tile)
    def _(step):
        part = pl.ds(pl.multiple_of(step * tile, tile), tile)
        column, begin, low = visible_range(ends_ref, step, tile)
        queries = [
            query
            for pair in range(pairs)
            for query in each_head(rows[part, part_lanes(pair, 0)].T, 0)
        ]

        def combine(index, state):
            there = pl.ds(pl.multiple_of(index * tile, tile), tile)
            row = index * tile + lax.broadcasted_iota(jnp.int32, (tile, tile), 0)
            visible = (row <= column) & (row >= begin)
            result = []
            for head in range(heads):
                top, total, summed = state[head]
                key = rows[there, part_lanes(head // 2, 1)]
                scores = jnp.where(visible, dot_nn(key, queries[head]), -1e30)
                new_top = jnp.maximum(top, jnp.max(scores, axis=0, keepdims=True))
                weight = jnp.exp(scores - new_top)
                factor = jnp.exp(top - new_top)
                total = total * factor + jnp.sum(weight, axis=0, keepdims=True)
                here = slice(head * HEAD_DIM, (head + 1) * HEAD_DIM)
                summed = summed * factor + dot_nn(values_t[here, there], weight.astype(BF16))
                result.append((new_top, total, summed))
            return tuple(result)

        empty = (
            jnp.full((1, tile), -1e30, F32),
            jnp.zeros((1, tile), F32),
            jnp.zeros((HEAD_DIM, tile), F32),
        )
        state = lax.fori_loop(low, step + 1, combine, (empty,) * heads)
        for head in range(heads):
            top, total, summed = state[head]
            summed_ref[head * HEAD_DIM : (head + 1) * HEAD_DIM, part] = summed * (1.0 / total)
            lse_ref[head : head + 1, part] = top + jnp.log(total)
        for pair in range(pairs):
            lanes = slice(pair * LANES, (pair + 1) * LANES)
            att[part, lanes] = summed_ref[lanes, part].T.astype(BF16)

    each_block(
        place_ref,
        lambda given, natural: pltpu.make_async_copy(
            att.at[natural], att_hbm.at[given], sems.at[0]
        ).start(),
    )
    pltpu.make_async_copy(att, att_hbm, sems.at[0]).wait()


def backward_kernel(
    pair, place_ref, ends_ref, cos_ref, sin_ref, rows, summed_ref, lse_ref, grad_hbm, *refs
):
    mixed_hbm, grad, grad_t, keys_t, grad_k, grad_v, mixed, sems = refs[-8:]
    tokens = grad.shape[0]
    tile = TILE
    lanes = slice(pair * LANES, (pair + 1) * LANES)
    lanes3 = slice(3 * pair * LANES, 3 * (pair + 1) * LANES)
    each_block(
        place_ref,
        lambda given, natural: pltpu.make_async_copy(
            grad_hbm.at[given, lanes], grad.at[natural], sems.at[0]
        ).start(),
    )
    grad_k[...] = jnp.zeros_like(grad_k)
    grad_v[...] = jnp.zeros_like(grad_v)

    @pl.loop(0, tokens // tile)
    def _(step):
        part = pl.ds(pl.multiple_of(step * tile, tile), tile)
        keys_t[:, part] = rows[part, K_LANES].T

    pltpu.make_async_copy(grad_hbm.at[:, lanes], grad, sems.at[0]).wait()

    @pl.loop(0, tokens // tile)
    def _(step):
        part = pl.ds(pl.multiple_of(step * tile, tile), tile)
        column, begin, low = visible_range(ends_ref, step, tile)
        query, back = rows[part, Q_LANES], grad[part, :]
        back_t = back.T
        queries, queries_t = each_head(query), each_head(query.T, 0)
        backs, backs_t = each_head(back), each_head(back_t, 0)
        grad_t[...] = back_t.astype(F32)
        delta = [
            jnp.sum(summed_ref[here, part] * grad_t[here, :], axis=0, keepdims=True)
            for here in HEAD_ROWS
        ]
        lse = [lse_ref[2 * pair + head : 2 * pair + head + 1, part] for head in range(2)]

        def back_step(index, sums):
            there = pl.ds(pl.multiple_of(index * tile, tile), tile)
            row = index * tile + lax.broadcasted_iota(jnp.int32, (tile, tile), 0)
            visible = (row <= column) & (row >= begin)
            key, value = rows[there, K_LANES], rows[there, V_LANES]
            result, add_k, add_v = [], 0.0, 0.0
            for head in range(2):
                scores = jnp.where(visible, dot_nn(key, queries_t[head]), -1e30)
                weight = jnp.exp(scores - lse[head])
                grad_w = dot_nn(value, backs_t[head])
                grad_s = (weight * (grad_w - delta[head])).astype(BF16)
                add_k = add_k + dot_nn(grad_s, queries[head])
                add_v = add_v + dot_nn(weight.astype(BF16), backs[head])
                result.append(sums[head] + dot_nn(keys_t[HEAD_ROWS[head], there], grad_s))
            grad_k[there, :] += add_k
            grad_v[there, :] += add_v
            return tuple(result)

        sums = lax.fori_loop(low, step + 1, back_step, (jnp.zeros((HEAD_DIM, tile), F32),) * 2)
        grad_q = jnp.concatenate(sums, axis=0).T * HEAD_DIM ** (-0.5)
        mixed[part, Q_LANES] = turn(grad_q, cos_ref[part, :], -sin_ref[part, :]).astype(BF16)

    @pl.loop(0, tokens // tile)
    def _(step):
        part = pl.ds(pl.multiple_of(step * tile, tile), tile)
        turned = turn(grad_k[part, :], cos_ref[part, :], -sin_ref[part, :])
        mixed[part, K_LANES] = turned.astype(BF16)
        mixed[part, V_LANES] = grad_v[part, :].astype(BF16)

    each_block(
        place_ref,
        lambda given, natural: pltpu.make_async_copy(
            mixed.at[natural], mixed_hbm.at[given, lanes3], sems.at[0]
        ).start(),
    )
    pltpu.make_async_copy(mixed, mixed_hbm.at[:, lanes3], sems.at[0]).wait()


def turn_tables(position, ends):
    begin = jnp.max(jnp.where(position[:, None] >= ends[None, :], ends[None, :], 0), axis=1)
    within = (position - begin).astype(F32)
    half = ROT // 2
    lane = jnp.arange(LANES, dtype=jnp.int32) % HEAD_DIM
    frequency = 10000.0 ** (-(lane % half).astype(F32) * 2.0 / ROT)
    angles = within[:, None] * jnp.where(lane < ROT, frequency, 0.0)[None, :]
    return jnp.cos(angles), jnp.sin(angles) * jnp.where(lane < half, -1.0, 1.0)[None, :]


SMEM = pl.BlockSpec(memory_space=pltpu.SMEM)
VMEM = pl.BlockSpec(memory_space=pltpu.VMEM)
ANYWHERE = pl.BlockSpec(memory_space=pl.ANY)


def attention_forward(block_place, ends, linear):
    tokens, width3 = linear.shape
    width = width3 // 3
    return pl.pallas_call(
        forward_kernel,
        out_shape=(
            jax.ShapeDtypeStruct((tokens, width), BF16),
            jax.ShapeDtypeStruct((tokens, width3), BF16),
            jax.ShapeDtypeStruct((width, tokens), F32),
            jax.ShapeDtypeStruct((width // HEAD_DIM, tokens), F32),
        ),
        in_specs=[SMEM, SMEM, ANYWHERE],
        out_specs=(ANYWHERE, VMEM, VMEM, VMEM),
        scratch_shapes=[
            pltpu.VMEM((width, tokens), BF16),
            pltpu.VMEM((tokens, width), BF16),
            pltpu.SemaphoreType.DMA((1,)),
        ],
        compiler_params=pltpu.CompilerParams(vmem_limit_bytes=40 << 20),
        cost_estimate=pl.CostEstimate(
            flops=40 * 10**9, bytes_accessed=16 * 10**6, transcendentals=0
        ),
    )(block_place, ends, linear)


def attention_backward(pair, block_place, ends, tables, kept, grad_att, before):
    tokens, width = grad_att.shape
    return pl.pallas_call(
        functools.partial(backward_kernel, pair),
        out_shape=jax.ShapeDtypeStruct((tokens, 3 * width), BF16),
        grid=(1,),
        in_specs=[
            SMEM,
            SMEM,
            VMEM,
            VMEM,
            pl.BlockSpec((tokens, 3 * LANES), lambda i: (0, pair)),
            pl.BlockSpec((LANES, tokens), lambda i: (pair, 0)),
            VMEM,
        ]
        + [ANYWHERE] * (1 + len(before)),
        out_specs=ANYWHERE,
        input_output_aliases={8 + i: i for i in range(len(before))},
        scratch_shapes=[
            pltpu.VMEM((tokens, LANES), BF16),
            pltpu.VMEM((LANES, TILE), F32),
            pltpu.VMEM((LANES, tokens), BF16),
            pltpu.VMEM((tokens, LANES), F32),
            pltpu.VMEM((tokens, LANES), F32),
            pltpu.VMEM((tokens, 3 * LANES), BF16),
            pltpu.SemaphoreType.DMA((1,)),
        ],
        compiler_params=pltpu.CompilerParams(vmem_limit_bytes=40 << 20),
        cost_estimate=pl.CostEstimate(
            flops=20 * 10**9, bytes_accessed=8 * 10**6, transcendentals=0
        ),
    )(block_place, ends, *tables, *kept, grad_att, *before)


def row_call(kernel, where, rows, whole, assembled, outs, sums, flops, split=False):
    count = rows[0].shape[0]
    tiles = count // ROWS
    shards = lax.axis_size("fsdp")
    pieces = [piece for _, group in assembled for _, _, piece in group]
    height = sum(sum(piece.shape[0] for _, _, piece in group) for _, group in assembled)

    def body(at, *refs):
        inputs = refs[: len(rows) + len(whole)]
        sources = refs[len(inputs) : len(inputs) + len(pieces)]
        targets = refs[len(inputs) + len(pieces) : -2]
        buffer, sems = refs[-2:]

        @pl.when(pl.program_id(0) == 0)
        def _():
            copies, base = [], 0
            for shard_height, group in assembled:
                for mask, start, piece in group:
                    first = start if mask is None else (at[0] ^ mask) * shard_height + start
                    size = piece.shape[0]
                    target = buffer.at[pl.ds(pl.multiple_of(base + first, size), size)]
                    slot = len(copies)
                    copies.append(pltpu.make_async_copy(sources[slot], target, sems.at[slot]))
                base += sum(piece.shape[0] for _, _, piece in group)
            for copy in copies:
                copy.start()
            for copy in copies:
                copy.wait()

        if split:
            mine, other, *rest = targets

            def put(part, value):
                even = at[1] == 0
                half = value.shape[0] // 2
                first, second = value[:half], value[half:]
                mine[0, :, part] = jnp.where(even, first, second)
                other[0, :, part] = jnp.where(even, second, first)

            kernel(*inputs, buffer, put, *rest)
        else:
            kernel(*inputs, buffer, *targets)

    by_tile = lambda columns: pl.BlockSpec((ROWS, columns), lambda i, at: (i, 0))
    stay = lambda shape: pl.BlockSpec(shape, lambda i, at: (0, 0))
    moved = sum(item.size * item.dtype.itemsize for item in (*rows, *whole, *pieces))
    moved += sum(count * columns * jnp.dtype(kind).itemsize for columns, kind in outs)
    if split:
        ((columns, kind),) = outs
        out_shape = [jax.ShapeDtypeStruct((tiles, ROWS // 2, columns), kind)] * 2
        out_specs = [pl.BlockSpec((1, ROWS // 2, columns), lambda i, at: (i, 0, 0))] * 2
    else:
        out_shape = [jax.ShapeDtypeStruct((count, columns), kind) for columns, kind in outs]
        out_specs = [by_tile(columns) for columns, _ in outs]
    return pl.pallas_call(
        body,
        out_shape=out_shape + [jax.ShapeDtypeStruct(shape, F32) for shape in sums],
        grid_spec=pltpu.PrefetchScalarGridSpec(
            num_scalar_prefetch=1,
            grid=(tiles,),
            in_specs=[by_tile(item.shape[1]) for item in rows]
            + [stay(item.shape) for item in whole]
            + [ANYWHERE] * len(pieces),
            out_specs=out_specs + [stay(shape) for shape in sums],
            scratch_shapes=[
                pltpu.VMEM((height, pieces[0].shape[1]), BF16),
                pltpu.SemaphoreType.DMA((len(pieces),)),
            ],
        ),
        compiler_params=pltpu.CompilerParams(vmem_limit_bytes=56 << 20),
        cost_estimate=pl.CostEstimate(flops=flops, bytes_accessed=moved, transcendentals=0),
    )(where, *rows, *whole, *pieces)


def chunks_of(columns, size=256):
    return [slice(start, min(start + size, columns)) for start in range(0, columns, size)]


def standard(rows):
    values = rows.astype(F32)
    centred = values - jnp.mean(values, axis=1, keepdims=True)
    inv_std = lax.rsqrt(jnp.mean(centred * centred, axis=1, keepdims=True) + 1e-05)
    return centred * inv_std, inv_std


def enter_kernel(
    tokens, cosine, sine, gain, shift, bias, inner, normed_out, slope_out, active_out, linear_out
):
    for start in range(0, tokens.shape[0], 32):
        part = slice(start, start + 32)
        scaled, _ = standard(tokens[part, :])
        normed_out[part, :] = (scaled * gain[...] + shift[...]).astype(BF16)
    normed = normed_out[...]
    units = active_out.shape[1]
    for part in chunks_of(units):
        hidden = dot_nn(normed, inner[:, part]) + bias[:, part]
        square = hidden * hidden
        gate = 1.0 / (1.0 + jnp.exp(hidden * (-1.5957691216057308 - 0.07135481627260025 * square)))
        value = hidden * gate
        active_out[:, part] = value.astype(BF16)
        inner_slope = 1.5957691216057308 + 0.21406444881780073 * square
        slope_out[:, part] = (gate + (value - value * gate) * inner_slope).astype(BF16)
    for part in chunks_of(linear_out.shape[1], 3 * LANES):
        there = slice(units + part.start, units + part.stop)
        value = dot_nn(normed, inner[:, there]) + bias[:, there]
        query = turn(value[:, Q_LANES], cosine[...], sine[...]) * HEAD_DIM ** (-0.5)
        key = turn(value[:, K_LANES], cosine[...], sine[...])
        joined = jnp.concatenate([query, key, value[:, V_LANES]], axis=1)
        linear_out[:, part] = joined.astype(BF16)


def back_kernel(first, second, slope, weights, hidden_out, att_out, hidden_sum):
    @pl.when(pl.program_id(0) == 0)
    def _():
        hidden_sum[...] = jnp.zeros_like(hidden_sum)

    rows = jnp.concatenate([first[...], second[...]], axis=1)
    units = slope.shape[1]
    for part in chunks_of(units):
        grad = (dot_nt(rows, weights[part, :]) * slope[:, part]).astype(BF16)
        hidden_out[:, part] = grad
        hidden_sum[:, part] += jnp.sum(grad.astype(F32), axis=0, keepdims=True)
    for part in chunks_of(att_out.shape[1]):
        there = slice(units + part.start, units + part.stop)
        att_out[:, part] = dot_nt(rows, weights[there, :]).astype(BF16)


def leave_kernel(attended, active, weights, put):
    rows = jnp.concatenate([active[...], attended[...]], axis=1)
    for part in chunks_of(weights.shape[1], 512):
        put(part, dot_nn(rows, weights[:, part]).astype(BF16))


def norm_back_kernel(tokens, mixed, hidden, inner, put, gain_sum, shift_sum, mixed_sum):
    @pl.when(pl.program_id(0) == 0)
    def _():
        for total in (gain_sum, shift_sum, mixed_sum):
            total[...] = jnp.zeros_like(total)

    scaled, _ = standard(tokens[...])
    mixed_sum[...] += jnp.sum(mixed[...].astype(F32), axis=0, keepdims=True)
    rows = jnp.concatenate([hidden[...], mixed[...]], axis=1)
    for part in chunks_of(inner.shape[0], 512):
        grad = dot_nt(rows, inner[part, :])
        put(part, grad.astype(BF16))
        shift_sum[:, part] += jnp.sum(grad, axis=0, keepdims=True)
        gain_sum[:, part] += jnp.sum(grad * scaled[:, part], axis=0, keepdims=True)


def pick_kernel(plans, index_ref, *refs):
    *weights, target, tiles, sems = refs
    at = index_ref[0]
    count = plans[0][2]
    copies, late, slot, column = [], [], 0, 0
    for weight, (unit, order, _) in zip(weights, plans):
        if unit % LANES == 0:
            for place in order:
                first = pl.multiple_of((place * count + at) * unit, unit)
                copies.append(
                    (weight.at[:, pl.ds(first, unit)], target.at[:, column : column + unit])
                )
                column += unit
            continue
        for one, two in zip(order[::2], order[1::2]):
            for which, place in enumerate((one, two)):
                first = pl.multiple_of((place * count + at) // 2 * LANES, LANES)
                copies.append((weight.at[:, pl.ds(first, LANES)], tiles.at[slot, which]))
            late.append((slot, column))
            slot, column = slot + 1, column + LANES
    copies = [
        pltpu.make_async_copy(source, there, sems.at[i])
        for i, (source, there) in enumerate(copies)
    ]
    for copy in copies:
        copy.start()
    for copy in copies:
        copy.wait()
    for slot, column in late:
        first, second = tiles[slot, 0].astype(F32), tiles[slot, 1].astype(F32)
        odd = at % 2 == 1
        first = jnp.where(odd, pltpu.roll(first, HEAD_DIM, 1), first)
        second = jnp.where(odd, second, pltpu.roll(second, HEAD_DIM, 1))
        target[:, column : column + LANES] = jnp.where(
            first_half(first.shape), first, second
        ).astype(target.dtype)


def pick_columns(weights, units, orders, index, count):
    rows = weights[0].shape[0]
    width = sum(unit * len(order) for unit, order in zip(units, orders))
    narrow = [len(order) // 2 for unit, order in zip(units, orders) if unit % LANES]
    copies = sum(len(order) for order in orders)
    return pl.pallas_call(
        functools.partial(pick_kernel, [(unit, order, count) for unit, order in zip(units, orders)]),
        out_shape=jax.ShapeDtypeStruct((rows, width), weights[0].dtype),
        in_specs=[SMEM] + [ANYWHERE] * len(weights),
        out_specs=VMEM,
        scratch_shapes=[
            pltpu.VMEM((sum(narrow), 2, rows, LANES), weights[0].dtype),
            pltpu.SemaphoreType.DMA((copies,)),
        ],
        compiler_params=pltpu.CompilerParams(vmem_limit_bytes=32 << 20),
        cost_estimate=pl.CostEstimate(
            flops=0, bytes_accessed=4 * rows * width, transcendentals=0
        ),
    )(index.reshape(1), *weights)


def deal_kernel(unit, order, at_ref, mine, other, target, *rest):
    line = mine.shape[0]
    count = 2 * line
    even = at_ref[1] == 0

    def both_cores(chip, tile):
        one, two = mine[chip, :, tile], other[chip, :, tile]
        return jnp.where(even, one, two).astype(F32), jnp.where(even, two, one).astype(F32)

    for chip in range(line):
        for group, place in enumerate(order):
            start = (place * count + 2 * chip) * unit
            if unit % LANES == 0:
                values = both_cores(chip, slice(group * unit, (group + 1) * unit))
                for core, value in enumerate(values):
                    target[:, start + core * unit : start + (core + 1) * unit] = value
                continue
            first, second = both_cores(chip, slice(group // 2 * LANES, (group // 2 + 1) * LANES))
            if group % 2:
                first = pltpu.roll(first, HEAD_DIM, 1)
            else:
                second = pltpu.roll(second, HEAD_DIM, 1)
            target[:, start : start + LANES] = jnp.where(first_half(first.shape), first, second)
    for out in rest:
        chips = out.shape[0] // HEAD_DIM // 2
        tail = slice(len(order) * unit, mine.shape[2])
        for chip in range(chips):
            source = chip if chips == line else at_ref[0] * chips + chip
            for core, value in enumerate(both_cores(source, tail)):
                row = (2 * chip + core) * HEAD_DIM
                out[row : row + HEAD_DIM, :] = value


def deal_columns(mine, other, unit, order, where, with_out=False):
    line, rows, columns = mine.shape
    rows, columns = 2 * rows, columns // 2
    width = len(order) * unit
    step = HEAD_DIM
    steps = rows // step
    out_shape = [jax.ShapeDtypeStruct((rows, 2 * line * width), F32)]
    out_specs = [pl.BlockSpec((step, 2 * line * width), lambda i, at: (i, 0))]
    if with_out:
        out_shape.append(jax.ShapeDtypeStruct((rows, (columns - width) * (rows // step)), F32))
        out_specs.append(pl.BlockSpec((rows, columns - width), lambda i, at: (0, i)))
    return pl.pallas_call(
        functools.partial(deal_kernel, unit, order),
        out_shape=out_shape,
        grid_spec=pltpu.PrefetchScalarGridSpec(
            num_scalar_prefetch=1,
            grid=(rows // step,),
            in_specs=[
                pl.BlockSpec(
                    (line, step, columns),
                    lambda i, at: (0, i % (steps // 2), i // (steps // 2)),
                )
            ]
            * 2,
            out_specs=out_specs,
        ),
        compiler_params=pltpu.CompilerParams(vmem_limit_bytes=32 << 20),
        cost_estimate=pl.CostEstimate(
            flops=0, bytes_accessed=12 * rows * line * columns, transcendentals=0
        ),
    )(where, mine, other)


def join_kernel(turns, turn_ref, left, *refs):
    *pieces, target = refs
    width = left.shape[1]
    size = target.shape[1] - width
    target[:, :width] = left[...]
    keep = pl.program_id(0) % turns == turn_ref[0]
    for piece_index, piece in enumerate(pieces):
        for chunk in range(piece.shape[1] // size):
            value = piece[:, chunk * size : (chunk + 1) * size]
            if turns > 1:
                value = jnp.where(keep, value, jnp.zeros_like(value))
            row = (piece_index * (piece.shape[1] // size) + chunk) * HEAD_DIM
            target[row : row + HEAD_DIM, width:] = value


def join_terms(left, pieces, shards, turns, turn_index):
    rows = left.shape[0] // shards
    extra = sum(piece.shape[1] for piece in pieces) * HEAD_DIM // rows
    width = left.shape[1]
    return pl.pallas_call(
        functools.partial(join_kernel, turns),
        out_shape=jax.ShapeDtypeStruct((left.shape[0], width + extra), left.dtype),
        grid_spec=pltpu.PrefetchScalarGridSpec(
            num_scalar_prefetch=1,
            grid=(shards,),
            in_specs=[pl.BlockSpec((rows, width), lambda i, at: (i, 0))]
            + [
                pl.BlockSpec((HEAD_DIM, piece.shape[1]), lambda i, at: (i // turns, 0))
                for piece in pieces
            ],
            out_specs=pl.BlockSpec((rows, width + extra), lambda i, at: (i, 0)),
        ),
        cost_estimate=pl.CostEstimate(
            flops=0, bytes_accessed=4 * left.shape[0] * (width + extra), transcendentals=0
        ),
    )(turn_index.reshape(1), left, *pieces)


def side_kernel(*refs):
    *pieces, target = refs
    start = 0
    for piece in pieces:
        target[:, start : start + piece.shape[1]] = piece[...].astype(F32)
        start += piece.shape[1]


def side_by_side(*pieces):
    rows = pieces[0].shape[0]
    width = sum(piece.shape[1] for piece in pieces)
    return pl.pallas_call(
        side_kernel,
        out_shape=jax.ShapeDtypeStruct((rows, width), F32),
        grid=(rows // TILE,),
        in_specs=[pl.BlockSpec((TILE, piece.shape[1]), lambda i: (i, 0)) for piece in pieces],
        out_specs=pl.BlockSpec((TILE, width), lambda i: (i, 0)),
        cost_estimate=pl.CostEstimate(flops=0, bytes_accessed=6 * rows * width, transcendentals=0),
    )(*pieces)


def after(value, *others):
    return lax.optimization_barrier((value,) + others)[0]


def shards(
    tokens,
    block_place,
    seq_lengths,
    norm_gain,
    norm_bias,
    qkv_weight,
    qkv_bias,
    out_weight,
    out_bias,
    up_weight,
    up_bias,
    down_weight,
    down_bias,
    out_grad,
):
    ctx_count, ctx_index = lax.axis_size("ctx"), lax.axis_index("ctx")
    shard_count, shard_index = lax.axis_size("fsdp"), lax.axis_index("fsdp")
    own_tokens, own_grad = tokens[0], out_grad[0]
    own_rows, model_width = own_tokens.shape
    hidden_width = up_weight.shape[1]
    heads = model_width // HEAD_DIM
    own_heads = heads // ctx_count
    shard_heads = heads // shard_count
    unit = hidden_width // shard_count // ctx_count
    own_width = own_heads * HEAD_DIM
    head_turns = ctx_count // shard_heads
    low_first = list(bits_of("fsdp"))
    high_first = low_first[::-1]

    def pick(value, axis):
        return lax.dynamic_index_in_dim(value, ctx_index, axis, keepdims=False)

    half_width = model_width // 2
    pairs = own_heads // 2

    def section_order(slot):
        pair, rest = slot // 6, slot % 6
        return rest // 2 * own_heads + pair * 2 + rest % 2

    def by_ctx(value):
        return lax.all_gather(value, "ctx", axis=0, tiled=True)

    def as_row(value):
        return value.reshape(1, -1)

    token_count = ctx_count * own_rows
    units = shard_count * unit
    flops = 2 * token_count * model_width
    shard_rows = model_width // shard_count
    both = (low_first, high_first)
    qkv_order = [section_order(slot) for slot in range(3 * own_heads)]
    turn_index, head_slot = ctx_index // shard_heads, ctx_index % shard_heads
    where = jnp.stack([shard_index, ctx_index % 2]).astype(jnp.int32)

    all_tokens = by_ctx(own_tokens)
    own_inner = pick_columns(
        [up_weight, qkv_weight],
        [unit, HEAD_DIM],
        [list(range(shard_count)), qkv_order],
        ctx_index,
        ctx_count,
    )
    vectors = (norm_gain, norm_bias, qkv_bias, out_bias, up_bias, down_bias)
    inner_flow = Flow(gather_steps(own_inner, *both))
    vector_flow = Flow(direct_steps(jnp.concatenate(vectors).reshape(8, -1)))
    grad_first = by_ctx(after(own_grad[:, :half_width], own_inner))

    def prepare(down_weight, out_weight):
        own_down = pick(down_weight.reshape(ctx_count, unit, model_width), 0)
        own_out = lax.dynamic_index_in_dim(
            out_weight.reshape(shard_heads, HEAD_DIM, model_width), head_slot, 0, keepdims=False
        )
        return own_down, own_out

    def both_tables(ends, block_place):
        natural = jnp.arange(token_count, dtype=jnp.int32)
        given = (block_place[:, None] * BLK + jnp.arange(BLK, dtype=jnp.int32)).reshape(-1)
        return turn_tables(natural, ends), turn_tables(given, ends)

    ends = jnp.cumsum(seq_lengths[0]).astype(jnp.int32)
    own_down, own_out = beside(prepare, (down_weight, out_weight), [inner_flow, vector_flow])
    grad_second = by_ctx(after(own_grad[:, half_width:], own_down))
    natural_tables, given_tables = beside(both_tables, (ends, block_place), [inner_flow])
    while inner_flow.moves:
        own_down, own_out = beside(lambda *same: same, (own_down, own_out), [inner_flow])
    packed = jnp.stack([piece.reshape(-1) for _, _, piece in vector_flow.result])
    packed = jnp.concatenate(
        [lax.dynamic_index_in_dim(packed, shard_index ^ i, 0) for i in range(shard_count)]
    )
    cuts = [0]
    for vector in vectors:
        cuts.append(cuts[-1] + vector.shape[0])
    gain_all, shift_all, qkv_bias_all, out_bias_all, up_bias_all, down_bias_all = [
        packed[:, start:stop].reshape(-1).astype(F32) for start, stop in zip(cuts, cuts[1:])
    ]
    own_qkv_bias = pick(qkv_bias_all.reshape(3, pairs, 2, ctx_count, HEAD_DIM), 3)
    own_qkv_bias = jnp.transpose(own_qkv_bias, (1, 0, 2, 3)).reshape(-1)
    own_up_bias = pick(up_bias_all.reshape(shard_count, ctx_count, unit), 1).reshape(-1)
    inner_bias = jnp.concatenate([own_up_bias, own_qkv_bias])
    inner = (shard_rows, inner_flow.result)
    down_flow = Flow(direct_steps(own_down))
    out_flow = Flow(direct_steps(own_out))

    def enter(rows):
        return row_call(
            enter_kernel,
            where,
            [rows, *given_tables],
            [as_row(gain_all), as_row(shift_all), as_row(inner_bias)],
            [inner],
            [(model_width, BF16), (units, BF16), (units, BF16), (3 * own_width, BF16)],
            [],
            flops * (units + 3 * own_width),
        )

    normed, slope, active, linear = beside(enter, (all_tokens,), [down_flow])

    def down_terms(rows):
        return dot_tn(active, rows).astype(BF16).reshape(shard_count, unit, half_width)

    first_terms = down_terms(after(grad_first, active))
    first_flow = Flow(scatter_steps(first_terms, *both))
    attended, *kept = beside(
        lambda rows: attention_forward(block_place, ends, rows),
        (linear,),
        [first_flow, out_flow],
    )
    down = (unit, down_flow.result)
    out = (HEAD_DIM, out_flow.result)
    if head_turns > 1:
        out_all = jnp.stack([piece for _, _, piece in out_flow.result])
        out_all = jnp.concatenate(
            [
                lax.dynamic_index_in_dim(
                    out_all, shard_index ^ (i * head_turns + turn_index), 0, keepdims=False
                )
                for i in range(own_heads)
            ]
        )
        out = (own_width, [(None, 0, out_all)])
    second_terms = beside(down_terms, (after(grad_second, attended),), [first_flow])
    while first_flow.moves:
        second_terms = beside(lambda same: same, (second_terms,), [first_flow])
    second_flow = Flow(scatter_steps(second_terms, *both))

    def leave(rows):
        return row_call(
            leave_kernel,
            where,
            [rows, active],
            [],
            [down, out],
            [(model_width, BF16)],
            [],
            flops * (units + own_width),
            split=True,
        )

    def back(rows):
        return row_call(
            back_kernel,
            where,
            [grad_first, rows, slope],
            [],
            [down, out],
            [(units, BF16), (own_width, BF16)],
            [(1, units)],
            flops * (units + own_width),
        )

    grad_hidden, grad_att, hidden_sum = beside(
        back, (after(grad_second, first_flow.result),), [second_flow]
    )
    up_terms = beside(
        lambda rows: dot_tn(normed, rows).astype(BF16), (grad_hidden,), [second_flow]
    )
    while second_flow.moves:
        up_terms = beside(lambda same: same, (up_terms,), [second_flow])
    up_flow = Flow(scatter_steps(up_terms.reshape(shard_count, shard_rows, units), *both, fold=1))
    out_halves = beside(leave, (after(attended, second_flow.result),), [up_flow])
    down_total = tuple(by_ctx(flow.result) for flow in (first_flow, second_flow))
    grad_mixed, weave = (), None
    for pair in range(pairs):
        grad_mixed = (
            beside(
                lambda rows: attention_backward(
                    pair, block_place, ends, natural_tables, kept, rows, grad_mixed
                ),
                (after(grad_att, *out_halves, down_total[min(pair, 1)]),),
                [weave or up_flow],
            ),
        )
        while up_flow.moves and pair + 1 == pairs:
            out_halves = beside(lambda *same: same, tuple(out_halves), [up_flow])
        if not up_flow.moves and weave is None:
            weave = Flow(weave_steps(up_flow.result, *out_halves))
    (grad_mixed,) = grad_mixed

    def joint(rows):
        late = after(attended, rows)
        out_terms = [dot_tn(late, piece).astype(BF16) for piece in (grad_first, grad_second)]
        return join_terms(
            dot_tn(normed, rows).astype(BF16), out_terms, shard_count, head_turns, turn_index
        )

    joint_terms = beside(joint, (grad_mixed,), [weave])
    joint_flow = Flow(
        scatter_steps(joint_terms.reshape(shard_count, shard_rows, -1), *both, fold=1)
    )

    def norm_back(rows):
        return row_call(
            norm_back_kernel,
            where,
            [all_tokens, rows, grad_hidden],
            [],
            [inner],
            [(model_width, BF16)],
            [(1, model_width), (1, model_width), (1, 3 * own_width)],
            flops * (units + 3 * own_width),
            split=True,
        )

    mine, other, gain_sum, shift_sum, mixed_sum = beside(
        norm_back, (after(grad_mixed, joint_terms),), [joint_flow, weave]
    )

    def spread(value, count):
        value = value.reshape(count, 1, -1)
        whole = jnp.zeros((count, ctx_count, value.shape[2]), F32)
        return lax.dynamic_update_slice_in_dim(whole, value, ctx_index, 1).reshape(-1)

    grad_float = own_grad.astype(F32)
    mixed_sum = jnp.transpose(mixed_sum.reshape(pairs, 3, 2 * HEAD_DIM), (1, 0, 2))
    sums = (
        gain_sum.reshape(-1),
        shift_sum.reshape(-1),
        spread(mixed_sum, 3 * own_heads),
        jnp.sum(grad_float, axis=0),
        spread(hidden_sum, shard_count),
    )
    total_flow = Flow(total_steps(jnp.concatenate(sums)))
    at = jnp.stack([shard_index % head_turns, ctx_index % 2]).astype(jnp.int32)

    def nothing():
        return ()

    while weave.moves:
        beside(nothing, (), [weave])
    up_swap, out_finish = weave.result
    down_total = beside(side_by_side, down_total, [joint_flow, out_finish, up_swap])
    while joint_flow.moves:
        beside(nothing, (), [joint_flow])
    weave = Flow(weave_steps(joint_flow.result, mine, other))
    (up_dealt,) = beside(
        lambda *halves: deal_columns(*halves, unit, list(range(shard_count)), at),
        up_swap.result,
        [weave, total_flow],
    )
    while weave.moves:
        beside(nothing, (), [flow for flow in (weave, total_flow) if flow.moves])
    joint_swap, norm_finish = weave.result
    beside(
        nothing, (), [flow for flow in (joint_swap, total_flow) if flow.moves], late=[norm_finish]
    )
    qkv_dealt, out_dealt = beside(
        lambda *halves: deal_columns(*halves, HEAD_DIM, qkv_order, at, with_out=True),
        joint_swap.result,
        [flow for flow in (total_flow,) if flow.moves],
        early=[norm_finish],
    )
    out_sum, grad_normed = out_finish.result, norm_finish.result

    inputs = own_tokens.astype(F32)
    output = (inputs + out_sum + (out_bias_all + down_bias_all)).astype(BF16)

    scaled, inv_std = standard(own_tokens)
    grad_scaled = grad_normed * gain_all
    grad_input = inv_std * (
        grad_scaled
        - jnp.mean(grad_scaled, axis=1, keepdims=True)
        - scaled * jnp.mean(grad_scaled * scaled, axis=1, keepdims=True)
    )
    input_grad = (grad_float + grad_input).astype(BF16)

    while total_flow.moves:
        beside(nothing, (), [total_flow])
    total = total_flow.result
    own_sums, start = [], 0
    for item in sums:
        size = item.shape[0] // shard_count
        own_sums.append(lax.dynamic_slice_in_dim(total, start + shard_index * size, size))
        start += item.shape[0]
    gain_total, shift_total, qkv_bias_total, bias_total, up_bias_total = own_sums

    return (
        output[None],
        input_grad[None],
        gain_total,
        shift_total,
        qkv_dealt,
        qkv_bias_total,
        out_dealt,
        bias_total,
        up_dealt,
        up_bias_total,
        down_total,
        bias_total,
    )


def solution(mesh):
    in_specs = (
        P("fsdp", "ctx", None),
        P(),
        P("fsdp", None),
        P("fsdp"),
        P("fsdp"),
        P("fsdp", None),
        P("fsdp"),
        P("fsdp", None),
        P("fsdp"),
        P("fsdp", None),
        P("fsdp"),
        P("fsdp", None),
        P("fsdp"),
        P("fsdp", "ctx", None),
    )
    out_specs = (
        P("fsdp", "ctx", None),
        P("fsdp", "ctx", None),
        P("fsdp"),
        P("fsdp"),
        P("fsdp", None),
        P("fsdp"),
        P("fsdp", None),
        P("fsdp"),
        P("fsdp", None),
        P("fsdp"),
        P("fsdp", None),
        P("fsdp"),
    )
    return jax.shard_map(shards, mesh=mesh, in_specs=in_specs, out_specs=out_specs, check_vma=False)
```

```python
import functools

import jax
import jax.numpy as jnp
from jax import lax
from jax.experimental import pallas as pl
from jax.experimental.pallas import tpu as pltpu
from jax.sharding import PartitionSpec as P

HEAD_DIM = 64
ROT = 32
BLK = 16
TILE = 256
WIDE = 512
ROWS = 512
LANES = 128
F32 = jnp.float32
BF16 = jnp.bfloat16


def dot_nn(left, right):
    return lax.dot_general(left, right, (((1,), (0,)), ((), ())), preferred_element_type=F32)


def dot_nt(left, right):
    return lax.dot_general(left, right, (((1,), (1,)), ((), ())), preferred_element_type=F32)


def dot_tn(left, right):
    return lax.dot_general(left, right, (((0,), (0,)), ((), ())), preferred_element_type=F32)


def bits_of(axis):
    return range(lax.axis_size(axis).bit_length() - 1)


def swaps(axis, mask):
    return axis, [(i, i ^ mask) for i in range(lax.axis_size(axis))]


class Flow:
    def __init__(self, steps):
        self.steps = steps
        self.result = None
        self.moves = next(steps)

    def arrive(self, values):
        try:
            self.moves = self.steps.send(values)
        except StopIteration as stop:
            self.moves, self.result = [], stop.value


def beside(work, inputs, flows, late=(), early=()):
    starting = [*flows, *late]
    sends = [[value for value, _, _ in flow.moves] for flow in starting]
    inputs, sends = lax.optimization_barrier((inputs, sends))
    for flow, values in zip(starting, sends):
        flow.moving = [
            lax.ppermute(value, axis, pairs) for value, (_, axis, pairs) in zip(values, flow.moves)
        ]
    outputs = work(*inputs)
    ending = [*flows, *early]
    outputs, arrived = lax.optimization_barrier((outputs, [flow.moving for flow in ending]))
    for flow, values in zip(ending, arrived):
        flow.arrive(values)
    return outputs


def gather_steps(own, *orders):
    share = own.shape[0] // len(orders)
    held = [[(0, own[i * share : (i + 1) * share])] for i in range(len(orders))]
    for step in range(len(orders[0])):
        moves = [
            (piece, *swaps("fsdp", 1 << order[step]))
            for pieces, order in zip(held, orders)
            for _, piece in pieces
        ]
        arrived = iter((yield moves))
        for i, order in enumerate(orders):
            held[i] = held[i] + [(mask ^ (1 << order[step]), next(arrived)) for mask, _ in held[i]]
    return [
        (mask, i * share, piece) for i, pieces in enumerate(held) for mask, piece in pieces
    ]


def direct_steps(own):
    masks = range(1, lax.axis_size("fsdp"))
    arrived = yield [(own, *swaps("fsdp", mask)) for mask in masks]
    return [(0, 0, own)] + [(mask, 0, piece) for mask, piece in zip(masks, arrived)]


def scatter_steps(parts, *orders, fold=0):
    index = lax.axis_index("fsdp")
    bits = len(orders[0])
    share = parts.shape[1] // len(orders)
    held = [
        parts[:, i * share : (i + 1) * share].reshape((2,) * bits + (share, parts.shape[2]))
        for i in range(len(orders))
    ]
    left = [list(range(bits))[::-1] for _ in orders]
    for step in range(bits):
        moves, keeps = [], []
        for i, order in enumerate(orders):
            axis = left[i].index(order[step])
            left[i].pop(axis)
            mine = (index >> order[step]) & 1
            send = lax.dynamic_index_in_dim(held[i], 1 - mine, axis, keepdims=False)
            keeps.append(lax.dynamic_index_in_dim(held[i], mine, axis, keepdims=False))
            moves.append((send, *swaps("fsdp", 1 << order[step])))
        arrived = yield moves
        held = [
            (keep.astype(F32) + got.astype(F32)).astype(BF16) for keep, got in zip(keeps, arrived)
        ]
    return jnp.concatenate(held, axis=fold)


def weave_steps(own, mine, other):
    count = lax.axis_size("ctx")
    line = count // 2
    place = lax.axis_index("ctx") // 2
    alike = own.shape == mine.shape[1:]
    forth = [(i, i + 2) for i in range(count - 2)]
    back = [(i, i - 2) for i in range(2, count)]
    ups, downs = [], []
    up, down, got = yield [
        (own, "ctx", forth), (own, "ctx", back), (other, *swaps("ctx", 1)),
    ]
    up_sum, down_sum = (up, down) if alike else (jnp.zeros_like(mine[0]),) * 2

    def block(target, added):
        target = jnp.clip(target, 0, line - 1)
        total = added.astype(F32)
        for half in (mine, got):
            total += lax.dynamic_index_in_dim(half, target, 0, keepdims=False).astype(F32)
        return total

    for step in range(2, line + 1):
        ups.append(up)
        downs.append(down)
        far = line + 1 - step
        up_sum = block(place + far, up_sum).astype(BF16)
        down_sum = block(place - far, down_sum).astype(BF16)
        if step == line:
            break
        if alike:
            up_sum = jnp.where(place >= step - 1, up, up_sum)
            down_sum = jnp.where(place <= line - step, down, down_sum)
            up_sum, down_sum = yield [(up_sum, "ctx", forth), (down_sum, "ctx", back)]
            up, down = up_sum, down_sum
        else:
            up, down, up_sum, down_sum = yield [
                (up, "ctx", [(i, j) for i, j in forth if i // 2 >= step - 1]),
                (down, "ctx", [(i, j) for i, j in back if i // 2 <= line - step]),
                (up_sum, "ctx", [(i, j) for i, j in forth if i // 2 < step - 1]),
                (down_sum, "ctx", [(i, j) for i, j in back if i // 2 > line - step]),
            ]

    def at_chip(chip):
        value = own
        for away in range(1, line):
            value = jnp.where(place == chip + away, ups[away - 1], value)
            value = jnp.where(place == chip - away, downs[away - 1], value)
        return value

    def swap_cores():
        blocks = jnp.stack([at_chip(chip) for chip in range(line)])
        (beside_blocks,) = yield [(blocks, *swaps("ctx", 1))]
        return blocks, beside_blocks

    def finish():
        last_up, last_down = yield [(up_sum, "ctx", forth), (down_sum, "ctx", back)]
        return block(place, last_up) + last_down.astype(F32)

    return Flow(swap_cores()), Flow(finish())


def total_steps(vector):
    for axis in ("ctx", "fsdp"):
        for bit in bits_of(axis):
            (got,) = yield [(vector, *swaps(axis, 1 << bit))]
            vector = vector + got
    return vector


def turn(values, cosine, sine):
    lane = lax.broadcasted_iota(jnp.int32, values.shape, 1) % HEAD_DIM
    half = ROT // 2
    partner = jnp.where(
        lane < half, pltpu.roll(values, LANES - half, 1), pltpu.roll(values, half, 1)
    )
    return values * cosine + partner * sine


def first_half(shape):
    return lax.broadcasted_iota(jnp.int32, shape, 1) < HEAD_DIM


def visible_range(ends_ref, step, wide, tile):
    top = step * wide
    column = top + lax.broadcasted_iota(jnp.int32, (1, wide), 1)
    begin = jnp.zeros((1, wide), jnp.int32)
    first = jnp.int32(0)
    for sequence in range(ends_ref.shape[0]):
        end = ends_ref[sequence]
        begin = jnp.where(column >= end, jnp.maximum(begin, end), begin)
        first = jnp.where(top >= end, jnp.maximum(first, end), first)
    return column, begin, first // tile


def each_head(values, axis=1):
    half = lax.broadcasted_iota(jnp.int32, values.shape, axis) < HEAD_DIM
    zero = jnp.zeros_like(values)
    return [jnp.where(half, values, zero), jnp.where(half, zero, values)]


Q_LANES, K_LANES, V_LANES = (slice(i * LANES, (i + 1) * LANES) for i in range(3))
HEAD_ROWS = (slice(0, HEAD_DIM), slice(HEAD_DIM, LANES))


def each_block(place_ref, act):
    @pl.loop(0, place_ref.shape[0])
    def _(block):
        act(
            pl.ds(pl.multiple_of(block * BLK, BLK), BLK),
            pl.ds(pl.multiple_of(place_ref[block] * BLK, BLK), BLK),
        )


def part_lanes(pair, which):
    start = (3 * pair + which) * LANES
    return slice(start, start + LANES)


def forward_kernel(
    place_ref, ends_ref, lin_hbm, att_hbm, rows, summed_ref, lse_ref, values_t, att, sems
):
    tokens = rows.shape[0]
    tile, wide = TILE, WIDE
    pairs = rows.shape[1] // LANES // 3
    heads = 2 * pairs
    each_block(
        place_ref,
        lambda given, natural: pltpu.make_async_copy(
            lin_hbm.at[given], rows.at[natural], sems.at[0]
        ).start(),
    )
    pltpu.make_async_copy(lin_hbm, rows, sems.at[0]).wait()

    @pl.loop(0, tokens // tile)
    def _(step):
        part = pl.ds(pl.multiple_of(step * tile, tile), tile)
        for pair in range(pairs):
            lanes = slice(pair * LANES, (pair + 1) * LANES)
            values_t[lanes, part] = rows[part, part_lanes(pair, 2)].T

    @pl.loop(0, tokens // wide)
    def _(step):
        part = pl.ds(pl.multiple_of(step * wide, wide), wide)
        column, begin, low = visible_range(ends_ref, step, wide, tile)
        queries = [
            query
            for pair in range(pairs)
            for query in each_head(rows[part, part_lanes(pair, 0)].T, 0)
        ]

        def combine(index, state):
            there = pl.ds(pl.multiple_of(index * tile, tile), tile)
            row = index * tile + lax.broadcasted_iota(jnp.int32, (tile, wide), 0)
            visible = (row <= column) & (row >= begin)
            result = []
            for head in range(heads):
                top, total, summed = state[head]
                key = rows[there, part_lanes(head // 2, 1)]
                scores = jnp.where(visible, dot_nn(key, queries[head]), -1e30)
                new_top = jnp.maximum(top, jnp.max(scores, axis=0, keepdims=True))
                weight = jnp.exp(scores - new_top)
                factor = jnp.exp(top - new_top)
                total = total * factor + jnp.sum(weight, axis=0, keepdims=True)
                here = slice(head * HEAD_DIM, (head + 1) * HEAD_DIM)
                summed = summed * factor + dot_nn(values_t[here, there], weight.astype(BF16))
                result.append((new_top, total, summed))
            return tuple(result)

        empty = (
            jnp.full((1, wide), -1e30, F32),
            jnp.zeros((1, wide), F32),
            jnp.zeros((HEAD_DIM, wide), F32),
        )
        state = lax.fori_loop(low, (step + 1) * (wide // tile), combine, (empty,) * heads)
        for head in range(heads):
            top, total, summed = state[head]
            summed_ref[head * HEAD_DIM : (head + 1) * HEAD_DIM, part] = summed * (1.0 / total)
            lse_ref[head : head + 1, part] = top + jnp.log(total)
        for pair in range(pairs):
            lanes = slice(pair * LANES, (pair + 1) * LANES)
            att[part, lanes] = summed_ref[lanes, part].T.astype(BF16)

    each_block(
        place_ref,
        lambda given, natural: pltpu.make_async_copy(
            att.at[natural], att_hbm.at[given], sems.at[0]
        ).start(),
    )
    pltpu.make_async_copy(att, att_hbm, sems.at[0]).wait()


def backward_kernel(
    pair, place_ref, ends_ref, cos_ref, sin_ref, rows, summed_ref, lse_ref, grad_hbm, *refs
):
    mixed_hbm, grad, grad_t, keys_t, grad_k, grad_v, mixed, sems = refs[-8:]
    tokens = grad.shape[0]
    tile, wide = TILE, WIDE
    lanes = slice(pair * LANES, (pair + 1) * LANES)
    lanes3 = slice(3 * pair * LANES, 3 * (pair + 1) * LANES)
    each_block(
        place_ref,
        lambda given, natural: pltpu.make_async_copy(
            grad_hbm.at[given, lanes], grad.at[natural], sems.at[0]
        ).start(),
    )
    grad_k[...] = jnp.zeros_like(grad_k)
    grad_v[...] = jnp.zeros_like(grad_v)

    @pl.loop(0, tokens // tile)
    def _(step):
        part = pl.ds(pl.multiple_of(step * tile, tile), tile)
        keys_t[:, part] = rows[part, K_LANES].T

    pltpu.make_async_copy(grad_hbm.at[:, lanes], grad, sems.at[0]).wait()

    @pl.loop(0, tokens // wide)
    def _(step):
        part = pl.ds(pl.multiple_of(step * wide, wide), wide)
        column, begin, low = visible_range(ends_ref, step, wide, tile)
        query, back = rows[part, Q_LANES], grad[part, :]
        back_t = back.T
        queries, queries_t = each_head(query), each_head(query.T, 0)
        backs, backs_t = each_head(back), each_head(back_t, 0)
        grad_t[...] = back_t.astype(F32)
        delta = [
            jnp.sum(summed_ref[here, part] * grad_t[here, :], axis=0, keepdims=True)
            for here in HEAD_ROWS
        ]
        lse = [lse_ref[2 * pair + head : 2 * pair + head + 1, part] for head in range(2)]

        def back_step(index, sums):
            there = pl.ds(pl.multiple_of(index * tile, tile), tile)
            row = index * tile + lax.broadcasted_iota(jnp.int32, (tile, wide), 0)
            visible = (row <= column) & (row >= begin)
            key, value = rows[there, K_LANES], rows[there, V_LANES]
            result, add_k, add_v = [], 0.0, 0.0
            for head in range(2):
                scores = jnp.where(visible, dot_nn(key, queries_t[head]), -1e30)
                weight = jnp.exp(scores - lse[head])
                grad_w = dot_nn(value, backs_t[head])
                grad_s = (weight * (grad_w - delta[head])).astype(BF16)
                add_k = add_k + dot_nn(grad_s, queries[head])
                add_v = add_v + dot_nn(weight.astype(BF16), backs[head])
                result.append(sums[head] + dot_nn(keys_t[HEAD_ROWS[head], there], grad_s))
            grad_k[there, :] += add_k
            grad_v[there, :] += add_v
            return tuple(result)

        sums = lax.fori_loop(low, (step + 1) * (wide // tile), back_step, (jnp.zeros((HEAD_DIM, wide), F32),) * 2)
        grad_q = jnp.concatenate(sums, axis=0).T * HEAD_DIM ** (-0.5)
        mixed[part, Q_LANES] = turn(grad_q, cos_ref[part, :], -sin_ref[part, :]).astype(BF16)

    @pl.loop(0, tokens // tile)
    def _(step):
        part = pl.ds(pl.multiple_of(step * tile, tile), tile)
        turned = turn(grad_k[part, :], cos_ref[part, :], -sin_ref[part, :])
        mixed[part, K_LANES] = turned.astype(BF16)
        mixed[part, V_LANES] = grad_v[part, :].astype(BF16)

    each_block(
        place_ref,
        lambda given, natural: pltpu.make_async_copy(
            mixed.at[natural], mixed_hbm.at[given, lanes3], sems.at[0]
        ).start(),
    )
    pltpu.make_async_copy(mixed, mixed_hbm.at[:, lanes3], sems.at[0]).wait()


def turn_tables(position, ends):
    begin = jnp.max(jnp.where(position[:, None] >= ends[None, :], ends[None, :], 0), axis=1)
    within = (position - begin).astype(F32)
    half = ROT // 2
    lane = jnp.arange(LANES, dtype=jnp.int32) % HEAD_DIM
    frequency = 10000.0 ** (-(lane % half).astype(F32) * 2.0 / ROT)
    angles = within[:, None] * jnp.where(lane < ROT, frequency, 0.0)[None, :]
    return jnp.cos(angles), jnp.sin(angles) * jnp.where(lane < half, -1.0, 1.0)[None, :]


SMEM = pl.BlockSpec(memory_space=pltpu.SMEM)
VMEM = pl.BlockSpec(memory_space=pltpu.VMEM)
ANYWHERE = pl.BlockSpec(memory_space=pl.ANY)


def attention_forward(block_place, ends, linear):
    tokens, width3 = linear.shape
    width = width3 // 3
    return pl.pallas_call(
        forward_kernel,
        out_shape=(
            jax.ShapeDtypeStruct((tokens, width), BF16),
            jax.ShapeDtypeStruct((tokens, width3), BF16),
            jax.ShapeDtypeStruct((width, tokens), F32),
            jax.ShapeDtypeStruct((width // HEAD_DIM, tokens), F32),
        ),
        in_specs=[SMEM, SMEM, ANYWHERE],
        out_specs=(ANYWHERE, VMEM, VMEM, VMEM),
        scratch_shapes=[
            pltpu.VMEM((width, tokens), BF16),
            pltpu.VMEM((tokens, width), BF16),
            pltpu.SemaphoreType.DMA((1,)),
        ],
        compiler_params=pltpu.CompilerParams(vmem_limit_bytes=60 << 20),
        cost_estimate=pl.CostEstimate(
            flops=40 * 10**9, bytes_accessed=16 * 10**6, transcendentals=0
        ),
    )(block_place, ends, linear)


def attention_backward(pair, block_place, ends, tables, kept, grad_att, before):
    tokens, width = grad_att.shape
    return pl.pallas_call(
        functools.partial(backward_kernel, pair),
        out_shape=jax.ShapeDtypeStruct((tokens, 3 * width), BF16),
        grid=(1,),
        in_specs=[
            SMEM,
            SMEM,
            VMEM,
            VMEM,
            pl.BlockSpec((tokens, 3 * LANES), lambda i: (0, pair)),
            pl.BlockSpec((LANES, tokens), lambda i: (pair, 0)),
            VMEM,
        ]
        + [ANYWHERE] * (1 + len(before)),
        out_specs=ANYWHERE,
        input_output_aliases={8 + i: i for i in range(len(before))},
        scratch_shapes=[
            pltpu.VMEM((tokens, LANES), BF16),
            pltpu.VMEM((LANES, WIDE), F32),
            pltpu.VMEM((LANES, tokens), BF16),
            pltpu.VMEM((tokens, LANES), F32),
            pltpu.VMEM((tokens, LANES), F32),
            pltpu.VMEM((tokens, 3 * LANES), BF16),
            pltpu.SemaphoreType.DMA((1,)),
        ],
        compiler_params=pltpu.CompilerParams(vmem_limit_bytes=60 << 20),
        cost_estimate=pl.CostEstimate(
            flops=20 * 10**9, bytes_accessed=8 * 10**6, transcendentals=0
        ),
    )(block_place, ends, *tables, *kept, grad_att, *before)


def row_call(kernel, where, rows, whole, assembled, outs, sums, flops, split=False):
    count = rows[0].shape[0]
    tiles = count // ROWS
    shards = lax.axis_size("fsdp")
    pieces = [piece for _, group in assembled for _, _, piece in group]
    height = sum(sum(piece.shape[0] for _, _, piece in group) for _, group in assembled)

    def body(at, *refs):
        inputs = refs[: len(rows) + len(whole)]
        sources = refs[len(inputs) : len(inputs) + len(pieces)]
        targets = refs[len(inputs) + len(pieces) : -2]
        buffer, sems = refs[-2:]

        @pl.when(pl.program_id(0) == 0)
        def _():
            copies, base = [], 0
            for shard_height, group in assembled:
                for mask, start, piece in group:
                    first = start if mask is None else (at[0] ^ mask) * shard_height + start
                    size = piece.shape[0]
                    target = buffer.at[pl.ds(pl.multiple_of(base + first, size), size)]
                    slot = len(copies)
                    copies.append(pltpu.make_async_copy(sources[slot], target, sems.at[slot]))
                base += sum(piece.shape[0] for _, _, piece in group)
            for copy in copies:
                copy.start()
            for copy in copies:
                copy.wait()

        if split:
            mine, other, *rest = targets

            def put(part, value):
                even = at[1] == 0
                half = value.shape[0] // 2
                first, second = value[:half], value[half:]
                mine[0, :, part] = jnp.where(even, first, second)
                other[0, :, part] = jnp.where(even, second, first)

            kernel(*inputs, buffer, put, *rest)
        else:
            kernel(*inputs, buffer, *targets)

    by_tile = lambda columns: pl.BlockSpec((ROWS, columns), lambda i, at: (i, 0))
    stay = lambda shape: pl.BlockSpec(shape, lambda i, at: (0, 0))
    moved = sum(item.size * item.dtype.itemsize for item in (*rows, *whole, *pieces))
    moved += sum(count * columns * jnp.dtype(kind).itemsize for columns, kind in outs)
    if split:
        ((columns, kind),) = outs
        out_shape = [jax.ShapeDtypeStruct((tiles, ROWS // 2, columns), kind)] * 2
        out_specs = [pl.BlockSpec((1, ROWS // 2, columns), lambda i, at: (i, 0, 0))] * 2
    else:
        out_shape = [jax.ShapeDtypeStruct((count, columns), kind) for columns, kind in outs]
        out_specs = [by_tile(columns) for columns, _ in outs]
    return pl.pallas_call(
        body,
        out_shape=out_shape + [jax.ShapeDtypeStruct(shape, F32) for shape in sums],
        grid_spec=pltpu.PrefetchScalarGridSpec(
            num_scalar_prefetch=1,
            grid=(tiles,),
            in_specs=[by_tile(item.shape[1]) for item in rows]
            + [stay(item.shape) for item in whole]
            + [ANYWHERE] * len(pieces),
            out_specs=out_specs + [stay(shape) for shape in sums],
            scratch_shapes=[
                pltpu.VMEM((height, pieces[0].shape[1]), BF16),
                pltpu.SemaphoreType.DMA((len(pieces),)),
            ],
        ),
        compiler_params=pltpu.CompilerParams(vmem_limit_bytes=60 << 20),
        cost_estimate=pl.CostEstimate(flops=flops, bytes_accessed=moved, transcendentals=0),
    )(where, *rows, *whole, *pieces)


def chunks_of(columns, size=256):
    return [slice(start, min(start + size, columns)) for start in range(0, columns, size)]


def standard(rows):
    values = rows.astype(F32)
    centred = values - jnp.mean(values, axis=1, keepdims=True)
    inv_std = lax.rsqrt(jnp.mean(centred * centred, axis=1, keepdims=True) + 1e-05)
    return centred * inv_std, inv_std


def enter_kernel(
    tokens, cosine, sine, gain, shift, bias, inner, normed_out, slope_out, active_out, linear_out
):
    for start in range(0, tokens.shape[0], 32):
        part = slice(start, start + 32)
        scaled, _ = standard(tokens[part, :])
        normed_out[part, :] = (scaled * gain[...] + shift[...]).astype(BF16)
    normed = normed_out[...]
    units = active_out.shape[1]
    for part in chunks_of(units):
        hidden = dot_nn(normed, inner[:, part]) + bias[:, part]
        square = hidden * hidden
        gate = 1.0 / (1.0 + jnp.exp(hidden * (-1.5957691216057308 - 0.07135481627260025 * square)))
        value = hidden * gate
        active_out[:, part] = value.astype(BF16)
        inner_slope = 1.5957691216057308 + 0.21406444881780073 * square
        slope_out[:, part] = (gate + (value - value * gate) * inner_slope).astype(BF16)
    for part in chunks_of(linear_out.shape[1], 3 * LANES):
        there = slice(units + part.start, units + part.stop)
        value = dot_nn(normed, inner[:, there]) + bias[:, there]
        query = turn(value[:, Q_LANES], cosine[...], sine[...]) * HEAD_DIM ** (-0.5)
        key = turn(value[:, K_LANES], cosine[...], sine[...])
        joined = jnp.concatenate([query, key, value[:, V_LANES]], axis=1)
        linear_out[:, part] = joined.astype(BF16)


def back_kernel(first, second, slope, weights, hidden_out, att_out, hidden_sum):
    @pl.when(pl.program_id(0) == 0)
    def _():
        hidden_sum[...] = jnp.zeros_like(hidden_sum)

    rows = jnp.concatenate([first[...], second[...]], axis=1)
    units = slope.shape[1]
    for part in chunks_of(units):
        grad = (dot_nt(rows, weights[part, :]) * slope[:, part]).astype(BF16)
        hidden_out[:, part] = grad
        hidden_sum[:, part] += jnp.sum(grad.astype(F32), axis=0, keepdims=True)
    for part in chunks_of(att_out.shape[1]):
        there = slice(units + part.start, units + part.stop)
        att_out[:, part] = dot_nt(rows, weights[there, :]).astype(BF16)


def leave_kernel(attended, active, weights, put):
    rows = jnp.concatenate([active[...], attended[...]], axis=1)
    for part in chunks_of(weights.shape[1], 512):
        put(part, dot_nn(rows, weights[:, part]).astype(BF16))


def norm_back_kernel(tokens, mixed, hidden, inner, put, gain_sum, shift_sum, mixed_sum):
    @pl.when(pl.program_id(0) == 0)
    def _():
        for total in (gain_sum, shift_sum, mixed_sum):
            total[...] = jnp.zeros_like(total)

    scaled, _ = standard(tokens[...])
    mixed_sum[...] += jnp.sum(mixed[...].astype(F32), axis=0, keepdims=True)
    rows = jnp.concatenate([hidden[...], mixed[...]], axis=1)
    for part in chunks_of(inner.shape[0], 512):
        grad = dot_nt(rows, inner[part, :])
        put(part, grad.astype(BF16))
        shift_sum[:, part] += jnp.sum(grad, axis=0, keepdims=True)
        gain_sum[:, part] += jnp.sum(grad * scaled[:, part], axis=0, keepdims=True)


def pick_kernel(plans, index_ref, *refs):
    *weights, target, tiles, sems = refs
    at = index_ref[0]
    count = plans[0][2]
    copies, late, slot, column = [], [], 0, 0
    for weight, (unit, order, _) in zip(weights, plans):
        if unit % LANES == 0:
            for place in order:
                first = pl.multiple_of((place * count + at) * unit, unit)
                copies.append(
                    (weight.at[:, pl.ds(first, unit)], target.at[:, column : column + unit])
                )
                column += unit
            continue
        for one, two in zip(order[::2], order[1::2]):
            for which, place in enumerate((one, two)):
                first = pl.multiple_of((place * count + at) // 2 * LANES, LANES)
                copies.append((weight.at[:, pl.ds(first, LANES)], tiles.at[slot, which]))
            late.append((slot, column))
            slot, column = slot + 1, column + LANES
    copies = [
        pltpu.make_async_copy(source, there, sems.at[i])
        for i, (source, there) in enumerate(copies)
    ]
    for copy in copies:
        copy.start()
    for copy in copies:
        copy.wait()
    for slot, column in late:
        first, second = tiles[slot, 0].astype(F32), tiles[slot, 1].astype(F32)
        odd = at % 2 == 1
        first = jnp.where(odd, pltpu.roll(first, HEAD_DIM, 1), first)
        second = jnp.where(odd, second, pltpu.roll(second, HEAD_DIM, 1))
        target[:, column : column + LANES] = jnp.where(
            first_half(first.shape), first, second
        ).astype(target.dtype)


def pick_columns(weights, units, orders, index, count):
    rows = weights[0].shape[0]
    width = sum(unit * len(order) for unit, order in zip(units, orders))
    narrow = [len(order) // 2 for unit, order in zip(units, orders) if unit % LANES]
    copies = sum(len(order) for order in orders)
    return pl.pallas_call(
        functools.partial(pick_kernel, [(unit, order, count) for unit, order in zip(units, orders)]),
        out_shape=jax.ShapeDtypeStruct((rows, width), weights[0].dtype),
        in_specs=[SMEM] + [ANYWHERE] * len(weights),
        out_specs=VMEM,
        scratch_shapes=[
            pltpu.VMEM((sum(narrow), 2, rows, LANES), weights[0].dtype),
            pltpu.SemaphoreType.DMA((copies,)),
        ],
        compiler_params=pltpu.CompilerParams(vmem_limit_bytes=32 << 20),
        cost_estimate=pl.CostEstimate(
            flops=0, bytes_accessed=4 * rows * width, transcendentals=0
        ),
    )(index.reshape(1), *weights)


def deal_kernel(unit, order, at_ref, mine, other, target, *rest):
    line = mine.shape[0]
    count = 2 * line
    even = at_ref[1] == 0

    def both_cores(chip, tile):
        one, two = mine[chip, :, tile], other[chip, :, tile]
        return jnp.where(even, one, two).astype(F32), jnp.where(even, two, one).astype(F32)

    for chip in range(line):
        for group, place in enumerate(order):
            start = (place * count + 2 * chip) * unit
            if unit % LANES == 0:
                values = both_cores(chip, slice(group * unit, (group + 1) * unit))
                for core, value in enumerate(values):
                    target[:, start + core * unit : start + (core + 1) * unit] = value
                continue
            first, second = both_cores(chip, slice(group // 2 * LANES, (group // 2 + 1) * LANES))
            if group % 2:
                first = pltpu.roll(first, HEAD_DIM, 1)
            else:
                second = pltpu.roll(second, HEAD_DIM, 1)
            target[:, start : start + LANES] = jnp.where(first_half(first.shape), first, second)
    for out in rest:
        chips = out.shape[0] // HEAD_DIM // 2
        tail = slice(len(order) * unit, mine.shape[2])
        for chip in range(chips):
            source = chip if chips == line else at_ref[0] * chips + chip
            for core, value in enumerate(both_cores(source, tail)):
                row = (2 * chip + core) * HEAD_DIM
                out[row : row + HEAD_DIM, :] = value


def deal_columns(mine, other, unit, order, where, with_out=False):
    line, rows, columns = mine.shape
    rows, columns = 2 * rows, columns // 2
    width = len(order) * unit
    step = HEAD_DIM
    steps = rows // step
    out_shape = [jax.ShapeDtypeStruct((rows, 2 * line * width), F32)]
    out_specs = [pl.BlockSpec((step, 2 * line * width), lambda i, at: (i, 0))]
    if with_out:
        out_shape.append(jax.ShapeDtypeStruct((rows, (columns - width) * (rows // step)), F32))
        out_specs.append(pl.BlockSpec((rows, columns - width), lambda i, at: (0, i)))
    return pl.pallas_call(
        functools.partial(deal_kernel, unit, order),
        out_shape=out_shape,
        grid_spec=pltpu.PrefetchScalarGridSpec(
            num_scalar_prefetch=1,
            grid=(rows // step,),
            in_specs=[
                pl.BlockSpec(
                    (line, step, columns),
                    lambda i, at: (0, i % (steps // 2), i // (steps // 2)),
                )
            ]
            * 2,
            out_specs=out_specs,
        ),
        compiler_params=pltpu.CompilerParams(vmem_limit_bytes=32 << 20),
        cost_estimate=pl.CostEstimate(
            flops=0, bytes_accessed=12 * rows * line * columns, transcendentals=0
        ),
    )(where, mine, other)


def join_kernel(turns, turn_ref, left, *refs):
    *pieces, target = refs
    width = left.shape[1]
    size = target.shape[1] - width
    target[:, :width] = left[...]
    keep = pl.program_id(0) % turns == turn_ref[0]
    for piece_index, piece in enumerate(pieces):
        for chunk in range(piece.shape[1] // size):
            value = piece[:, chunk * size : (chunk + 1) * size]
            if turns > 1:
                value = jnp.where(keep, value, jnp.zeros_like(value))
            row = (piece_index * (piece.shape[1] // size) + chunk) * HEAD_DIM
            target[row : row + HEAD_DIM, width:] = value


def join_terms(left, pieces, shards, turns, turn_index):
    rows = left.shape[0] // shards
    extra = sum(piece.shape[1] for piece in pieces) * HEAD_DIM // rows
    width = left.shape[1]
    return pl.pallas_call(
        functools.partial(join_kernel, turns),
        out_shape=jax.ShapeDtypeStruct((left.shape[0], width + extra), left.dtype),
        grid_spec=pltpu.PrefetchScalarGridSpec(
            num_scalar_prefetch=1,
            grid=(shards,),
            in_specs=[pl.BlockSpec((rows, width), lambda i, at: (i, 0))]
            + [
                pl.BlockSpec((HEAD_DIM, piece.shape[1]), lambda i, at: (i // turns, 0))
                for piece in pieces
            ],
            out_specs=pl.BlockSpec((rows, width + extra), lambda i, at: (i, 0)),
        ),
        cost_estimate=pl.CostEstimate(
            flops=0, bytes_accessed=4 * left.shape[0] * (width + extra), transcendentals=0
        ),
    )(turn_index.reshape(1), left, *pieces)


def side_kernel(*refs):
    *pieces, target = refs
    start = 0
    for piece in pieces:
        target[:, start : start + piece.shape[1]] = piece[...].astype(F32)
        start += piece.shape[1]


def side_by_side(*pieces):
    rows = pieces[0].shape[0]
    width = sum(piece.shape[1] for piece in pieces)
    return pl.pallas_call(
        side_kernel,
        out_shape=jax.ShapeDtypeStruct((rows, width), F32),
        grid=(rows // TILE,),
        in_specs=[pl.BlockSpec((TILE, piece.shape[1]), lambda i: (i, 0)) for piece in pieces],
        out_specs=pl.BlockSpec((TILE, width), lambda i: (i, 0)),
        cost_estimate=pl.CostEstimate(flops=0, bytes_accessed=6 * rows * width, transcendentals=0),
    )(*pieces)


def after(value, *others):
    return lax.optimization_barrier((value,) + others)[0]


def shards(
    tokens,
    block_place,
    seq_lengths,
    norm_gain,
    norm_bias,
    qkv_weight,
    qkv_bias,
    out_weight,
    out_bias,
    up_weight,
    up_bias,
    down_weight,
    down_bias,
    out_grad,
):
    ctx_count, ctx_index = lax.axis_size("ctx"), lax.axis_index("ctx")
    shard_count, shard_index = lax.axis_size("fsdp"), lax.axis_index("fsdp")
    own_tokens, own_grad = tokens[0], out_grad[0]
    own_rows, model_width = own_tokens.shape
    hidden_width = up_weight.shape[1]
    heads = model_width // HEAD_DIM
    own_heads = heads // ctx_count
    shard_heads = heads // shard_count
    unit = hidden_width // shard_count // ctx_count
    own_width = own_heads * HEAD_DIM
    head_turns = ctx_count // shard_heads
    low_first = list(bits_of("fsdp"))
    high_first = low_first[::-1]

    def pick(value, axis):
        return lax.dynamic_index_in_dim(value, ctx_index, axis, keepdims=False)

    half_width = model_width // 2
    pairs = own_heads // 2

    def section_order(slot):
        pair, rest = slot // 6, slot % 6
        return rest // 2 * own_heads + pair * 2 + rest % 2

    def by_ctx(value):
        return lax.all_gather(value, "ctx", axis=0, tiled=True)

    def as_row(value):
        return value.reshape(1, -1)

    token_count = ctx_count * own_rows
    units = shard_count * unit
    flops = 2 * token_count * model_width
    shard_rows = model_width // shard_count
    both = (low_first, high_first)
    qkv_order = [section_order(slot) for slot in range(3 * own_heads)]
    turn_index, head_slot = ctx_index // shard_heads, ctx_index % shard_heads
    where = jnp.stack([shard_index, ctx_index % 2]).astype(jnp.int32)

    all_tokens = by_ctx(own_tokens)
    own_inner = pick_columns(
        [up_weight, qkv_weight],
        [unit, HEAD_DIM],
        [list(range(shard_count)), qkv_order],
        ctx_index,
        ctx_count,
    )
    vectors = (norm_gain, norm_bias, qkv_bias, out_bias, up_bias, down_bias)
    inner_flow = Flow(gather_steps(own_inner, *both))
    vector_flow = Flow(direct_steps(jnp.concatenate(vectors).reshape(8, -1)))
    grad_first = by_ctx(after(own_grad[:, :half_width], own_inner))

    def prepare(down_weight, out_weight):
        own_down = pick(down_weight.reshape(ctx_count, unit, model_width), 0)
        own_out = lax.dynamic_index_in_dim(
            out_weight.reshape(shard_heads, HEAD_DIM, model_width), head_slot, 0, keepdims=False
        )
        return own_down, own_out

    def both_tables(ends, block_place):
        natural = jnp.arange(token_count, dtype=jnp.int32)
        given = (block_place[:, None] * BLK + jnp.arange(BLK, dtype=jnp.int32)).reshape(-1)
        return turn_tables(natural, ends), turn_tables(given, ends)

    ends = jnp.cumsum(seq_lengths[0]).astype(jnp.int32)
    own_down, own_out = beside(prepare, (down_weight, out_weight), [inner_flow, vector_flow])
    grad_second = by_ctx(after(own_grad[:, half_width:], own_down))
    natural_tables, given_tables = beside(both_tables, (ends, block_place), [inner_flow])
    while inner_flow.moves:
        own_down, own_out = beside(lambda *same: same, (own_down, own_out), [inner_flow])
    packed = jnp.stack([piece.reshape(-1) for _, _, piece in vector_flow.result])
    packed = jnp.concatenate(
        [lax.dynamic_index_in_dim(packed, shard_index ^ i, 0) for i in range(shard_count)]
    )
    cuts = [0]
    for vector in vectors:
        cuts.append(cuts[-1] + vector.shape[0])
    gain_all, shift_all, qkv_bias_all, out_bias_all, up_bias_all, down_bias_all = [
        packed[:, start:stop].reshape(-1).astype(F32) for start, stop in zip(cuts, cuts[1:])
    ]
    own_qkv_bias = pick(qkv_bias_all.reshape(3, pairs, 2, ctx_count, HEAD_DIM), 3)
    own_qkv_bias = jnp.transpose(own_qkv_bias, (1, 0, 2, 3)).reshape(-1)
    own_up_bias = pick(up_bias_all.reshape(shard_count, ctx_count, unit), 1).reshape(-1)
    inner_bias = jnp.concatenate([own_up_bias, own_qkv_bias])
    inner = (shard_rows, inner_flow.result)
    down_flow = Flow(direct_steps(own_down))
    out_flow = Flow(direct_steps(own_out))

    def enter(rows):
        return row_call(
            enter_kernel,
            where,
            [rows, *given_tables],
            [as_row(gain_all), as_row(shift_all), as_row(inner_bias)],
            [inner],
            [(model_width, BF16), (units, BF16), (units, BF16), (3 * own_width, BF16)],
            [],
            flops * (units + 3 * own_width),
        )

    normed, slope, active, linear = beside(enter, (all_tokens,), [down_flow])

    def down_terms(rows):
        return dot_tn(active, rows).astype(BF16).reshape(shard_count, unit, half_width)

    first_terms = down_terms(after(grad_first, active))
    first_flow = Flow(scatter_steps(first_terms, *both))
    attended, *kept = beside(
        lambda rows: attention_forward(block_place, ends, rows),
        (linear,),
        [first_flow, out_flow],
    )
    down = (unit, down_flow.result)
    out = (HEAD_DIM, out_flow.result)
    if head_turns > 1:
        out_all = jnp.stack([piece for _, _, piece in out_flow.result])
        out_all = jnp.concatenate(
            [
                lax.dynamic_index_in_dim(
                    out_all, shard_index ^ (i * head_turns + turn_index), 0, keepdims=False
                )
                for i in range(own_heads)
            ]
        )
        out = (own_width, [(None, 0, out_all)])
    second_terms = beside(down_terms, (after(grad_second, attended),), [first_flow])
    while first_flow.moves:
        second_terms = beside(lambda same: same, (second_terms,), [first_flow])
    second_flow = Flow(scatter_steps(second_terms, *both))

    def leave(rows):
        return row_call(
            leave_kernel,
            where,
            [rows, active],
            [],
            [down, out],
            [(model_width, BF16)],
            [],
            flops * (units + own_width),
            split=True,
        )

    def back(rows):
        return row_call(
            back_kernel,
            where,
            [grad_first, rows, slope],
            [],
            [down, out],
            [(units, BF16), (own_width, BF16)],
            [(1, units)],
            flops * (units + own_width),
        )

    grad_hidden, grad_att, hidden_sum = beside(
        back, (after(grad_second, first_flow.result),), [second_flow]
    )
    up_terms = beside(
        lambda rows: dot_tn(normed, rows).astype(BF16), (grad_hidden,), [second_flow]
    )
    while second_flow.moves:
        up_terms = beside(lambda same: same, (up_terms,), [second_flow])
    up_flow = Flow(scatter_steps(up_terms.reshape(shard_count, shard_rows, units), *both, fold=1))
    out_halves = beside(leave, (after(attended, second_flow.result),), [up_flow])
    down_total = tuple(by_ctx(flow.result) for flow in (first_flow, second_flow))
    grad_mixed, weave = (), None
    for pair in range(pairs):
        grad_mixed = (
            beside(
                lambda rows: attention_backward(
                    pair, block_place, ends, natural_tables, kept, rows, grad_mixed
                ),
                (after(grad_att, *out_halves, down_total[min(pair, 1)]),),
                [weave or up_flow],
            ),
        )
        while up_flow.moves and pair + 1 == pairs:
            out_halves = beside(lambda *same: same, tuple(out_halves), [up_flow])
        if not up_flow.moves and weave is None:
            weave = Flow(weave_steps(up_flow.result, *out_halves))
    (grad_mixed,) = grad_mixed

    def joint(rows):
        late = after(attended, rows)
        out_terms = [dot_tn(late, piece).astype(BF16) for piece in (grad_first, grad_second)]
        return join_terms(
            dot_tn(normed, rows).astype(BF16), out_terms, shard_count, head_turns, turn_index
        )

    joint_terms = beside(joint, (grad_mixed,), [weave])
    joint_flow = Flow(
        scatter_steps(joint_terms.reshape(shard_count, shard_rows, -1), *both, fold=1)
    )

    def norm_back(rows):
        return row_call(
            norm_back_kernel,
            where,
            [all_tokens, rows, grad_hidden],
            [],
            [inner],
            [(model_width, BF16)],
            [(1, model_width), (1, model_width), (1, 3 * own_width)],
            flops * (units + 3 * own_width),
            split=True,
        )

    mine, other, gain_sum, shift_sum, mixed_sum = beside(
        norm_back, (after(grad_mixed, joint_terms),), [joint_flow, weave]
    )

    def spread(value, count):
        value = value.reshape(count, 1, -1)
        whole = jnp.zeros((count, ctx_count, value.shape[2]), F32)
        return lax.dynamic_update_slice_in_dim(whole, value, ctx_index, 1).reshape(-1)

    grad_float = own_grad.astype(F32)
    mixed_sum = jnp.transpose(mixed_sum.reshape(pairs, 3, 2 * HEAD_DIM), (1, 0, 2))
    sums = (
        gain_sum.reshape(-1),
        shift_sum.reshape(-1),
        spread(mixed_sum, 3 * own_heads),
        jnp.sum(grad_float, axis=0),
        spread(hidden_sum, shard_count),
    )
    total_flow = Flow(total_steps(jnp.concatenate(sums)))
    at = jnp.stack([shard_index % head_turns, ctx_index % 2]).astype(jnp.int32)

    def nothing():
        return ()

    while weave.moves:
        beside(nothing, (), [weave])
    up_swap, out_finish = weave.result
    down_total = beside(side_by_side, down_total, [joint_flow, out_finish])
    while joint_flow.moves:
        beside(nothing, (), [joint_flow])
    weave = Flow(weave_steps(joint_flow.result, mine, other))
    beside(nothing, (), [weave, total_flow])
    beside(nothing, (), [flow for flow in (weave, total_flow, up_swap) if flow.moves])
    (up_dealt,) = beside(
        lambda *halves: deal_columns(*halves, unit, list(range(shard_count)), at),
        up_swap.result,
        [flow for flow in (weave, total_flow) if flow.moves],
    )
    while weave.moves:
        beside(nothing, (), [flow for flow in (weave, total_flow) if flow.moves])
    joint_swap, norm_finish = weave.result
    beside(
        nothing, (), [flow for flow in (joint_swap, total_flow) if flow.moves], late=[norm_finish]
    )
    qkv_dealt, out_dealt = beside(
        lambda *halves: deal_columns(*halves, HEAD_DIM, qkv_order, at, with_out=True),
        joint_swap.result,
        [flow for flow in (total_flow,) if flow.moves],
        early=[norm_finish],
    )
    out_sum, grad_normed = out_finish.result, norm_finish.result

    inputs = own_tokens.astype(F32)
    output = (inputs + out_sum + (out_bias_all + down_bias_all)).astype(BF16)

    scaled, inv_std = standard(own_tokens)
    grad_scaled = grad_normed * gain_all
    grad_input = inv_std * (
        grad_scaled
        - jnp.mean(grad_scaled, axis=1, keepdims=True)
        - scaled * jnp.mean(grad_scaled * scaled, axis=1, keepdims=True)
    )
    input_grad = (grad_float + grad_input).astype(BF16)

    while total_flow.moves:
        beside(nothing, (), [total_flow])
    total = total_flow.result
    own_sums, start = [], 0
    for item in sums:
        size = item.shape[0] // shard_count
        own_sums.append(lax.dynamic_slice_in_dim(total, start + shard_index * size, size))
        start += item.shape[0]
    gain_total, shift_total, qkv_bias_total, bias_total, up_bias_total = own_sums

    return (
        output[None],
        input_grad[None],
        gain_total,
        shift_total,
        qkv_dealt,
        qkv_bias_total,
        out_dealt,
        bias_total,
        up_dealt,
        up_bias_total,
        down_total,
        bias_total,
    )


def solution(mesh):
    in_specs = (
        P("fsdp", "ctx", None),
        P(),
        P("fsdp", None),
        P("fsdp"),
        P("fsdp"),
        P("fsdp", None),
        P("fsdp"),
        P("fsdp", None),
        P("fsdp"),
        P("fsdp", None),
        P("fsdp"),
        P("fsdp", None),
        P("fsdp"),
        P("fsdp", "ctx", None),
    )
    out_specs = (
        P("fsdp", "ctx", None),
        P("fsdp", "ctx", None),
        P("fsdp"),
        P("fsdp"),
        P("fsdp", None),
        P("fsdp"),
        P("fsdp", None),
        P("fsdp"),
        P("fsdp", None),
        P("fsdp"),
        P("fsdp", None),
        P("fsdp"),
    )
    return jax.shard_map(shards, mesh=mesh, in_specs=in_specs, out_specs=out_specs, check_vma=False)
```

```python
import functools

import jax
import jax.numpy as jnp
from jax import lax
from jax.experimental import pallas as pl
from jax.experimental.pallas import tpu as pltpu
from jax.sharding import PartitionSpec as P

HEAD_DIM = 64
ROT = 32
BLK = 16
TILE = 256
WIDE = 512
ROWS = 512
LANES = 128
F32 = jnp.float32
BF16 = jnp.bfloat16


def dot_nn(left, right):
    return lax.dot_general(left, right, (((1,), (0,)), ((), ())), preferred_element_type=F32)


def dot_nt(left, right):
    return lax.dot_general(left, right, (((1,), (1,)), ((), ())), preferred_element_type=F32)


def dot_tn(left, right):
    return lax.dot_general(left, right, (((0,), (0,)), ((), ())), preferred_element_type=F32)


def bits_of(axis):
    return range(lax.axis_size(axis).bit_length() - 1)


def swaps(axis, mask):
    return axis, [(i, i ^ mask) for i in range(lax.axis_size(axis))]


class Flow:
    def __init__(self, steps):
        self.steps = steps
        self.result = None
        self.moves = next(steps)

    def arrive(self, values):
        try:
            self.moves = self.steps.send(values)
        except StopIteration as stop:
            self.moves, self.result = [], stop.value


def beside(work, inputs, flows, late=(), early=()):
    starting = [*flows, *late]
    sends = [[value for value, _, _ in flow.moves] for flow in starting]
    inputs, sends = lax.optimization_barrier((inputs, sends))
    for flow, values in zip(starting, sends):
        flow.moving = [
            lax.ppermute(value, axis, pairs) for value, (_, axis, pairs) in zip(values, flow.moves)
        ]
    outputs = work(*inputs)
    ending = [*flows, *early]
    outputs, arrived = lax.optimization_barrier((outputs, [flow.moving for flow in ending]))
    for flow, values in zip(ending, arrived):
        flow.arrive(values)
    return outputs


def gather_steps(own, *orders):
    share = own.shape[0] // len(orders)
    held = [[(0, own[i * share : (i + 1) * share])] for i in range(len(orders))]
    for step in range(len(orders[0])):
        moves = [
            (piece, *swaps("fsdp", 1 << order[step]))
            for pieces, order in zip(held, orders)
            for _, piece in pieces
        ]
        arrived = iter((yield moves))
        for i, order in enumerate(orders):
            held[i] = held[i] + [(mask ^ (1 << order[step]), next(arrived)) for mask, _ in held[i]]
    return [
        (mask, i * share, piece) for i, pieces in enumerate(held) for mask, piece in pieces
    ]


def direct_steps(own):
    masks = range(1, lax.axis_size("fsdp"))
    arrived = yield [(own, *swaps("fsdp", mask)) for mask in masks]
    return [(0, 0, own)] + [(mask, 0, piece) for mask, piece in zip(masks, arrived)]


def scatter_steps(parts, *orders, fold=0):
    index = lax.axis_index("fsdp")
    bits = len(orders[0])
    share = parts.shape[1] // len(orders)
    held = [
        parts[:, i * share : (i + 1) * share].reshape((2,) * bits + (share, parts.shape[2]))
        for i in range(len(orders))
    ]
    left = [list(range(bits))[::-1] for _ in orders]
    for step in range(bits):
        moves, keeps = [], []
        for i, order in enumerate(orders):
            axis = left[i].index(order[step])
            left[i].pop(axis)
            mine = (index >> order[step]) & 1
            send = lax.dynamic_index_in_dim(held[i], 1 - mine, axis, keepdims=False)
            keeps.append(lax.dynamic_index_in_dim(held[i], mine, axis, keepdims=False))
            moves.append((send, *swaps("fsdp", 1 << order[step])))
        arrived = yield moves
        held = [
            (keep.astype(F32) + got.astype(F32)).astype(BF16) for keep, got in zip(keeps, arrived)
        ]
    return jnp.concatenate(held, axis=fold)


def swap_steps(value, kept=None):
    (got,) = yield [(value, *swaps("ctx", 1))]
    return value if kept is None else kept, got


def add_pair(mine, got):
    return (mine.astype(F32) + got.astype(F32)).astype(BF16)


def weave_steps(own, held, shape):
    count = lax.axis_size("ctx")
    line = count // 2
    place = lax.axis_index("ctx") // 2
    alike = own.shape == shape[1:]
    forth = [(i, i + 2) for i in range(count - 2)]
    back = [(i, i - 2) for i in range(2, count)]
    ups, downs = [], []
    up, down = yield [(own, "ctx", forth), (own, "ctx", back)]
    up_sum, down_sum = (up, down) if alike else (jnp.zeros(shape[1:], BF16),) * 2

    def block(target, added):
        target = jnp.clip(target, 0, line - 1)
        part = lax.dynamic_index_in_dim(held[0], target, 0, keepdims=False)
        return part.astype(F32) + added.astype(F32)

    for step in range(2, line + 1):
        ups.append(up)
        downs.append(down)
        far = line + 1 - step
        up_sum = block(place + far, up_sum).astype(BF16)
        down_sum = block(place - far, down_sum).astype(BF16)
        if step == line:
            break
        if alike:
            up_sum = jnp.where(place >= step - 1, up, up_sum)
            down_sum = jnp.where(place <= line - step, down, down_sum)
            up_sum, down_sum = yield [(up_sum, "ctx", forth), (down_sum, "ctx", back)]
            up, down = up_sum, down_sum
        else:
            up, down, up_sum, down_sum = yield [
                (up, "ctx", [(i, j) for i, j in forth if i // 2 >= step - 1]),
                (down, "ctx", [(i, j) for i, j in back if i // 2 <= line - step]),
                (up_sum, "ctx", [(i, j) for i, j in forth if i // 2 < step - 1]),
                (down_sum, "ctx", [(i, j) for i, j in back if i // 2 > line - step]),
            ]

    def finish():
        last_up, last_down = yield [(up_sum, "ctx", forth), (down_sum, "ctx", back)]
        return block(place, last_up) + last_down.astype(F32)

    return (own, ups, downs), Flow(finish())


def in_order(own, ups, downs):
    place = lax.axis_index("ctx") // 2
    blocks = []
    for chip in range(len(ups) + 1):
        value = own
        for away, (up, down) in enumerate(zip(ups, downs), 1):
            value = jnp.where(place == chip + away, up, value)
            value = jnp.where(place == chip - away, down, value)
        blocks.append(value)
    return jnp.stack(blocks)


def total_steps(vector):
    for axis in ("ctx", "fsdp"):
        for bit in bits_of(axis):
            (got,) = yield [(vector, *swaps(axis, 1 << bit))]
            vector = vector + got
    return vector


def turn(values, cosine, sine):
    lane = lax.broadcasted_iota(jnp.int32, values.shape, 1) % HEAD_DIM
    half = ROT // 2
    partner = jnp.where(
        lane < half, pltpu.roll(values, LANES - half, 1), pltpu.roll(values, half, 1)
    )
    return values * cosine + partner * sine


def first_half(shape):
    return lax.broadcasted_iota(jnp.int32, shape, 1) < HEAD_DIM


def visible_range(ends_ref, step, wide, tile):
    top = step * wide
    column = top + lax.broadcasted_iota(jnp.int32, (1, wide), 1)
    begin = jnp.zeros((1, wide), jnp.int32)
    first = jnp.int32(0)
    for sequence in range(ends_ref.shape[0]):
        end = ends_ref[sequence]
        begin = jnp.where(column >= end, jnp.maximum(begin, end), begin)
        first = jnp.where(top >= end, jnp.maximum(first, end), first)
    return column, begin, first // tile


def each_head(values, axis=1):
    half = lax.broadcasted_iota(jnp.int32, values.shape, axis) < HEAD_DIM
    zero = jnp.zeros_like(values)
    return [jnp.where(half, values, zero), jnp.where(half, zero, values)]


Q_LANES, K_LANES, V_LANES = (slice(i * LANES, (i + 1) * LANES) for i in range(3))
HEAD_ROWS = (slice(0, HEAD_DIM), slice(HEAD_DIM, LANES))


def each_block(place_ref, act):
    @pl.loop(0, place_ref.shape[0])
    def _(block):
        act(
            pl.ds(pl.multiple_of(block * BLK, BLK), BLK),
            pl.ds(pl.multiple_of(place_ref[block] * BLK, BLK), BLK),
        )


def part_lanes(pair, which):
    start = (3 * pair + which) * LANES
    return slice(start, start + LANES)


def forward_kernel(
    place_ref, ends_ref, lin_hbm, att_hbm, rows, summed_ref, lse_ref, values_t, att, sems
):
    tokens = rows.shape[0]
    tile, wide = TILE, WIDE
    pairs = rows.shape[1] // LANES // 3
    heads = 2 * pairs
    each_block(
        place_ref,
        lambda given, natural: pltpu.make_async_copy(
            lin_hbm.at[given], rows.at[natural], sems.at[0]
        ).start(),
    )
    pltpu.make_async_copy(lin_hbm, rows, sems.at[0]).wait()

    @pl.loop(0, tokens // tile)
    def _(step):
        part = pl.ds(pl.multiple_of(step * tile, tile), tile)
        for pair in range(pairs):
            lanes = slice(pair * LANES, (pair + 1) * LANES)
            values_t[lanes, part] = rows[part, part_lanes(pair, 2)].T

    @pl.loop(0, tokens // wide)
    def _(step):
        part = pl.ds(pl.multiple_of(step * wide, wide), wide)
        column, begin, low = visible_range(ends_ref, step, wide, tile)
        queries = [
            query
            for pair in range(pairs)
            for query in each_head(rows[part, part_lanes(pair, 0)].T, 0)
        ]

        def combine(index, state):
            there = pl.ds(pl.multiple_of(index * tile, tile), tile)
            row = index * tile + lax.broadcasted_iota(jnp.int32, (tile, wide), 0)
            visible = (row <= column) & (row >= begin)
            result = []
            for head in range(heads):
                top, total, summed = state[head]
                key = rows[there, part_lanes(head // 2, 1)]
                scores = jnp.where(visible, dot_nn(key, queries[head]), -1e30)
                new_top = jnp.maximum(top, jnp.max(scores, axis=0, keepdims=True))
                weight = jnp.exp(scores - new_top)
                factor = jnp.exp(top - new_top)
                total = total * factor + jnp.sum(weight, axis=0, keepdims=True)
                here = slice(head * HEAD_DIM, (head + 1) * HEAD_DIM)
                summed = summed * factor + dot_nn(values_t[here, there], weight.astype(BF16))
                result.append((new_top, total, summed))
            return tuple(result)

        empty = (
            jnp.full((1, wide), -1e30, F32),
            jnp.zeros((1, wide), F32),
            jnp.zeros((HEAD_DIM, wide), F32),
        )
        state = lax.fori_loop(low, (step + 1) * (wide // tile), combine, (empty,) * heads)
        for head in range(heads):
            top, total, summed = state[head]
            summed_ref[head * HEAD_DIM : (head + 1) * HEAD_DIM, part] = summed * (1.0 / total)
            lse_ref[head : head + 1, part] = top + jnp.log(total)
        for pair in range(pairs):
            lanes = slice(pair * LANES, (pair + 1) * LANES)
            att[part, lanes] = summed_ref[lanes, part].T.astype(BF16)

    each_block(
        place_ref,
        lambda given, natural: pltpu.make_async_copy(
            att.at[natural], att_hbm.at[given], sems.at[0]
        ).start(),
    )
    pltpu.make_async_copy(att, att_hbm, sems.at[0]).wait()


def backward_kernel(
    pair, place_ref, ends_ref, cos_ref, sin_ref, rows, summed_ref, lse_ref, grad_hbm, *refs
):
    mixed_hbm, grad, grad_t, keys_t, grad_k, grad_v, mixed, sems = refs[-8:]
    tokens = grad.shape[0]
    tile, wide = TILE, WIDE
    lanes = slice(pair * LANES, (pair + 1) * LANES)
    lanes3 = slice(3 * pair * LANES, 3 * (pair + 1) * LANES)
    each_block(
        place_ref,
        lambda given, natural: pltpu.make_async_copy(
            grad_hbm.at[given, lanes], grad.at[natural], sems.at[0]
        ).start(),
    )
    grad_k[...] = jnp.zeros_like(grad_k)
    grad_v[...] = jnp.zeros_like(grad_v)

    @pl.loop(0, tokens // tile)
    def _(step):
        part = pl.ds(pl.multiple_of(step * tile, tile), tile)
        keys_t[:, part] = rows[part, K_LANES].T

    pltpu.make_async_copy(grad_hbm.at[:, lanes], grad, sems.at[0]).wait()

    @pl.loop(0, tokens // wide)
    def _(step):
        part = pl.ds(pl.multiple_of(step * wide, wide), wide)
        column, begin, low = visible_range(ends_ref, step, wide, tile)
        query, back = rows[part, Q_LANES], grad[part, :]
        back_t = back.T
        queries, queries_t = each_head(query), each_head(query.T, 0)
        backs, backs_t = each_head(back), each_head(back_t, 0)
        grad_t[...] = back_t.astype(F32)
        delta = [
            jnp.sum(summed_ref[here, part] * grad_t[here, :], axis=0, keepdims=True)
            for here in HEAD_ROWS
        ]
        lse = [lse_ref[2 * pair + head : 2 * pair + head + 1, part] for head in range(2)]

        def back_step(index, sums):
            there = pl.ds(pl.multiple_of(index * tile, tile), tile)
            row = index * tile + lax.broadcasted_iota(jnp.int32, (tile, wide), 0)
            visible = (row <= column) & (row >= begin)
            key, value = rows[there, K_LANES], rows[there, V_LANES]
            result, add_k, add_v = [], 0.0, 0.0
            for head in range(2):
                scores = jnp.where(visible, dot_nn(key, queries_t[head]), -1e30)
                weight = jnp.exp(scores - lse[head])
                grad_w = dot_nn(value, backs_t[head])
                grad_s = (weight * (grad_w - delta[head])).astype(BF16)
                add_k = add_k + dot_nn(grad_s, queries[head])
                add_v = add_v + dot_nn(weight.astype(BF16), backs[head])
                result.append(sums[head] + dot_nn(keys_t[HEAD_ROWS[head], there], grad_s))
            grad_k[there, :] += add_k
            grad_v[there, :] += add_v
            return tuple(result)

        sums = lax.fori_loop(low, (step + 1) * (wide // tile), back_step, (jnp.zeros((HEAD_DIM, wide), F32),) * 2)
        grad_q = jnp.concatenate(sums, axis=0).T * HEAD_DIM ** (-0.5)
        mixed[part, Q_LANES] = turn(grad_q, cos_ref[part, :], -sin_ref[part, :]).astype(BF16)

    @pl.loop(0, tokens // tile)
    def _(step):
        part = pl.ds(pl.multiple_of(step * tile, tile), tile)
        turned = turn(grad_k[part, :], cos_ref[part, :], -sin_ref[part, :])
        mixed[part, K_LANES] = turned.astype(BF16)
        mixed[part, V_LANES] = grad_v[part, :].astype(BF16)

    each_block(
        place_ref,
        lambda given, natural: pltpu.make_async_copy(
            mixed.at[natural], mixed_hbm.at[given, lanes3], sems.at[0]
        ).start(),
    )
    pltpu.make_async_copy(mixed, mixed_hbm.at[:, lanes3], sems.at[0]).wait()


def turn_tables(position, ends):
    begin = jnp.max(jnp.where(position[:, None] >= ends[None, :], ends[None, :], 0), axis=1)
    within = (position - begin).astype(F32)
    half = ROT // 2
    lane = jnp.arange(LANES, dtype=jnp.int32) % HEAD_DIM
    frequency = 10000.0 ** (-(lane % half).astype(F32) * 2.0 / ROT)
    angles = within[:, None] * jnp.where(lane < ROT, frequency, 0.0)[None, :]
    return jnp.cos(angles), jnp.sin(angles) * jnp.where(lane < half, -1.0, 1.0)[None, :]


SMEM = pl.BlockSpec(memory_space=pltpu.SMEM)
VMEM = pl.BlockSpec(memory_space=pltpu.VMEM)
ANYWHERE = pl.BlockSpec(memory_space=pl.ANY)


def attention_forward(block_place, ends, linear):
    tokens, width3 = linear.shape
    width = width3 // 3
    return pl.pallas_call(
        forward_kernel,
        out_shape=(
            jax.ShapeDtypeStruct((tokens, width), BF16),
            jax.ShapeDtypeStruct((tokens, width3), BF16),
            jax.ShapeDtypeStruct((width, tokens), F32),
            jax.ShapeDtypeStruct((width // HEAD_DIM, tokens), F32),
        ),
        in_specs=[SMEM, SMEM, ANYWHERE],
        out_specs=(ANYWHERE, VMEM, VMEM, VMEM),
        scratch_shapes=[
            pltpu.VMEM((width, tokens), BF16),
            pltpu.VMEM((tokens, width), BF16),
            pltpu.SemaphoreType.DMA((1,)),
        ],
        compiler_params=pltpu.CompilerParams(vmem_limit_bytes=60 << 20),
        cost_estimate=pl.CostEstimate(
            flops=40 * 10**9, bytes_accessed=16 * 10**6, transcendentals=0
        ),
    )(block_place, ends, linear)


def attention_backward(pair, block_place, ends, tables, kept, grad_att, before):
    tokens, width = grad_att.shape
    return pl.pallas_call(
        functools.partial(backward_kernel, pair),
        out_shape=jax.ShapeDtypeStruct((tokens, 3 * width), BF16),
        grid=(1,),
        in_specs=[
            SMEM,
            SMEM,
            VMEM,
            VMEM,
            pl.BlockSpec((tokens, 3 * LANES), lambda i: (0, pair)),
            pl.BlockSpec((LANES, tokens), lambda i: (pair, 0)),
            VMEM,
        ]
        + [ANYWHERE] * (1 + len(before)),
        out_specs=ANYWHERE,
        input_output_aliases={8 + i: i for i in range(len(before))},
        scratch_shapes=[
            pltpu.VMEM((tokens, LANES), BF16),
            pltpu.VMEM((LANES, WIDE), F32),
            pltpu.VMEM((LANES, tokens), BF16),
            pltpu.VMEM((tokens, LANES), F32),
            pltpu.VMEM((tokens, LANES), F32),
            pltpu.VMEM((tokens, 3 * LANES), BF16),
            pltpu.SemaphoreType.DMA((1,)),
        ],
        compiler_params=pltpu.CompilerParams(vmem_limit_bytes=60 << 20),
        cost_estimate=pl.CostEstimate(
            flops=20 * 10**9, bytes_accessed=8 * 10**6, transcendentals=0
        ),
    )(block_place, ends, *tables, *kept, grad_att, *before)


def row_call(kernel, where, rows, whole, assembled, outs, sums, flops, split=False):
    count = rows[0].shape[0]
    tiles = count // ROWS
    shards = lax.axis_size("fsdp")
    pieces = [piece for _, group in assembled for _, _, piece in group]
    height = sum(sum(piece.shape[0] for _, _, piece in group) for _, group in assembled)

    def body(at, *refs):
        inputs = refs[: len(rows) + len(whole)]
        sources = refs[len(inputs) : len(inputs) + len(pieces)]
        targets = refs[len(inputs) + len(pieces) : -2]
        buffer, sems = refs[-2:]

        @pl.when(pl.program_id(0) == 0)
        def _():
            copies, base = [], 0
            for shard_height, group in assembled:
                for mask, start, piece in group:
                    first = start if mask is None else (at[0] ^ mask) * shard_height + start
                    size = piece.shape[0]
                    target = buffer.at[pl.ds(pl.multiple_of(base + first, size), size)]
                    slot = len(copies)
                    copies.append(pltpu.make_async_copy(sources[slot], target, sems.at[slot]))
                base += sum(piece.shape[0] for _, _, piece in group)
            for copy in copies:
                copy.start()
            for copy in copies:
                copy.wait()

        if split:
            mine, other, *rest = targets

            def put(part, value):
                even = at[1] == 0
                half = value.shape[0] // 2
                first, second = value[:half], value[half:]
                mine[0, :, part] = jnp.where(even, first, second)
                other[0, :, part] = jnp.where(even, second, first)

            kernel(*inputs, buffer, put, *rest)
        else:
            kernel(*inputs, buffer, *targets)

    by_tile = lambda columns: pl.BlockSpec((ROWS, columns), lambda i, at: (i, 0))
    stay = lambda shape: pl.BlockSpec(shape, lambda i, at: (0, 0))
    moved = sum(item.size * item.dtype.itemsize for item in (*rows, *whole, *pieces))
    moved += sum(count * columns * jnp.dtype(kind).itemsize for columns, kind in outs)
    if split:
        ((columns, kind),) = outs
        out_shape = [jax.ShapeDtypeStruct((tiles, ROWS // 2, columns), kind)] * 2
        out_specs = [pl.BlockSpec((1, ROWS // 2, columns), lambda i, at: (i, 0, 0))] * 2
    else:
        out_shape = [jax.ShapeDtypeStruct((count, columns), kind) for columns, kind in outs]
        out_specs = [by_tile(columns) for columns, _ in outs]
    return pl.pallas_call(
        body,
        out_shape=out_shape + [jax.ShapeDtypeStruct(shape, F32) for shape in sums],
        grid_spec=pltpu.PrefetchScalarGridSpec(
            num_scalar_prefetch=1,
            grid=(tiles,),
            in_specs=[by_tile(item.shape[1]) for item in rows]
            + [stay(item.shape) for item in whole]
            + [ANYWHERE] * len(pieces),
            out_specs=out_specs + [stay(shape) for shape in sums],
            scratch_shapes=[
                pltpu.VMEM((height, pieces[0].shape[1]), BF16),
                pltpu.SemaphoreType.DMA((len(pieces),)),
            ],
        ),
        compiler_params=pltpu.CompilerParams(vmem_limit_bytes=60 << 20),
        cost_estimate=pl.CostEstimate(flops=flops, bytes_accessed=moved, transcendentals=0),
    )(where, *rows, *whole, *pieces)


def chunks_of(columns, size=256):
    return [slice(start, min(start + size, columns)) for start in range(0, columns, size)]


def standard(rows):
    values = rows.astype(F32)
    centred = values - jnp.mean(values, axis=1, keepdims=True)
    inv_std = lax.rsqrt(jnp.mean(centred * centred, axis=1, keepdims=True) + 1e-05)
    return centred * inv_std, inv_std


def enter_kernel(
    tokens, cosine, sine, gain, shift, bias, inner, normed_out, slope_out, active_out, linear_out
):
    for start in range(0, tokens.shape[0], 32):
        part = slice(start, start + 32)
        scaled, _ = standard(tokens[part, :])
        normed_out[part, :] = (scaled * gain[...] + shift[...]).astype(BF16)
    normed = normed_out[...]
    units = active_out.shape[1]
    for part in chunks_of(units):
        hidden = dot_nn(normed, inner[:, part]) + bias[:, part]
        square = hidden * hidden
        gate = 1.0 / (1.0 + jnp.exp(hidden * (-1.5957691216057308 - 0.07135481627260025 * square)))
        value = hidden * gate
        active_out[:, part] = value.astype(BF16)
        inner_slope = 1.5957691216057308 + 0.21406444881780073 * square
        slope_out[:, part] = (gate + (value - value * gate) * inner_slope).astype(BF16)
    for part in chunks_of(linear_out.shape[1], 3 * LANES):
        there = slice(units + part.start, units + part.stop)
        value = dot_nn(normed, inner[:, there]) + bias[:, there]
        query = turn(value[:, Q_LANES], cosine[...], sine[...]) * HEAD_DIM ** (-0.5)
        key = turn(value[:, K_LANES], cosine[...], sine[...])
        joined = jnp.concatenate([query, key, value[:, V_LANES]], axis=1)
        linear_out[:, part] = joined.astype(BF16)


def back_kernel(first, second, slope, weights, hidden_out, att_out, hidden_sum):
    @pl.when(pl.program_id(0) == 0)
    def _():
        hidden_sum[...] = jnp.zeros_like(hidden_sum)

    rows = jnp.concatenate([first[...], second[...]], axis=1)
    units = slope.shape[1]
    for part in chunks_of(units):
        grad = (dot_nt(rows, weights[part, :]) * slope[:, part]).astype(BF16)
        hidden_out[:, part] = grad
        hidden_sum[:, part] += jnp.sum(grad.astype(F32), axis=0, keepdims=True)
    for part in chunks_of(att_out.shape[1]):
        there = slice(units + part.start, units + part.stop)
        att_out[:, part] = dot_nt(rows, weights[there, :]).astype(BF16)


def leave_kernel(attended, active, weights, put):
    rows = jnp.concatenate([active[...], attended[...]], axis=1)
    for part in chunks_of(weights.shape[1], 512):
        put(part, dot_nn(rows, weights[:, part]).astype(BF16))


def norm_back_kernel(tokens, mixed, hidden, inner, put, gain_sum, shift_sum, mixed_sum):
    @pl.when(pl.program_id(0) == 0)
    def _():
        for total in (gain_sum, shift_sum, mixed_sum):
            total[...] = jnp.zeros_like(total)

    scaled, _ = standard(tokens[...])
    mixed_sum[...] += jnp.sum(mixed[...].astype(F32), axis=0, keepdims=True)
    rows = jnp.concatenate([hidden[...], mixed[...]], axis=1)
    for part in chunks_of(inner.shape[0], 512):
        grad = dot_nt(rows, inner[part, :])
        put(part, grad.astype(BF16))
        shift_sum[:, part] += jnp.sum(grad, axis=0, keepdims=True)
        gain_sum[:, part] += jnp.sum(grad * scaled[:, part], axis=0, keepdims=True)


def pick_kernel(plans, index_ref, *refs):
    *weights, target, tiles, sems = refs
    at = index_ref[0]
    count = plans[0][2]
    copies, late, slot, column = [], [], 0, 0
    for weight, (unit, order, _) in zip(weights, plans):
        if unit % LANES == 0:
            for place in order:
                first = pl.multiple_of((place * count + at) * unit, unit)
                copies.append(
                    (weight.at[:, pl.ds(first, unit)], target.at[:, column : column + unit])
                )
                column += unit
            continue
        for one, two in zip(order[::2], order[1::2]):
            for which, place in enumerate((one, two)):
                first = pl.multiple_of((place * count + at) // 2 * LANES, LANES)
                copies.append((weight.at[:, pl.ds(first, LANES)], tiles.at[slot, which]))
            late.append((slot, column))
            slot, column = slot + 1, column + LANES
    copies = [
        pltpu.make_async_copy(source, there, sems.at[i])
        for i, (source, there) in enumerate(copies)
    ]
    for copy in copies:
        copy.start()
    for copy in copies:
        copy.wait()
    for slot, column in late:
        first, second = tiles[slot, 0].astype(F32), tiles[slot, 1].astype(F32)
        odd = at % 2 == 1
        first = jnp.where(odd, pltpu.roll(first, HEAD_DIM, 1), first)
        second = jnp.where(odd, second, pltpu.roll(second, HEAD_DIM, 1))
        target[:, column : column + LANES] = jnp.where(
            first_half(first.shape), first, second
        ).astype(target.dtype)


def pick_columns(weights, units, orders, index, count):
    rows = weights[0].shape[0]
    width = sum(unit * len(order) for unit, order in zip(units, orders))
    narrow = [len(order) // 2 for unit, order in zip(units, orders) if unit % LANES]
    copies = sum(len(order) for order in orders)
    return pl.pallas_call(
        functools.partial(pick_kernel, [(unit, order, count) for unit, order in zip(units, orders)]),
        out_shape=jax.ShapeDtypeStruct((rows, width), weights[0].dtype),
        in_specs=[SMEM] + [ANYWHERE] * len(weights),
        out_specs=VMEM,
        scratch_shapes=[
            pltpu.VMEM((sum(narrow), 2, rows, LANES), weights[0].dtype),
            pltpu.SemaphoreType.DMA((copies,)),
        ],
        compiler_params=pltpu.CompilerParams(vmem_limit_bytes=32 << 20),
        cost_estimate=pl.CostEstimate(
            flops=0, bytes_accessed=4 * rows * width, transcendentals=0
        ),
    )(index.reshape(1), *weights)


def deal_kernel(unit, order, at_ref, mine, other, target, *rest):
    line = mine.shape[0]
    count = 2 * line
    even = at_ref[1] == 0

    def both_cores(chip, tile):
        one, two = mine[chip, :, tile], other[chip, :, tile]
        return jnp.where(even, one, two).astype(F32), jnp.where(even, two, one).astype(F32)

    for chip in range(line):
        for group, place in enumerate(order):
            start = (place * count + 2 * chip) * unit
            if unit % LANES == 0:
                values = both_cores(chip, slice(group * unit, (group + 1) * unit))
                for core, value in enumerate(values):
                    target[:, start + core * unit : start + (core + 1) * unit] = value
                continue
            first, second = both_cores(chip, slice(group // 2 * LANES, (group // 2 + 1) * LANES))
            if group % 2:
                first = pltpu.roll(first, HEAD_DIM, 1)
            else:
                second = pltpu.roll(second, HEAD_DIM, 1)
            target[:, start : start + LANES] = jnp.where(first_half(first.shape), first, second)
    for out in rest:
        chips = out.shape[0] // HEAD_DIM // 2
        tail = slice(len(order) * unit, mine.shape[2])
        for chip in range(chips):
            source = chip if chips == line else at_ref[0] * chips + chip
            for core, value in enumerate(both_cores(source, tail)):
                row = (2 * chip + core) * HEAD_DIM
                out[row : row + HEAD_DIM, :] = value


def deal_columns(mine, other, unit, order, where, with_out=False):
    line, rows, columns = mine.shape
    rows, columns = 2 * rows, columns // 2
    width = len(order) * unit
    step = HEAD_DIM
    steps = rows // step
    out_shape = [jax.ShapeDtypeStruct((rows, 2 * line * width), F32)]
    out_specs = [pl.BlockSpec((step, 2 * line * width), lambda i, at: (i, 0))]
    if with_out:
        out_shape.append(jax.ShapeDtypeStruct((rows, (columns - width) * (rows // step)), F32))
        out_specs.append(pl.BlockSpec((rows, columns - width), lambda i, at: (0, i)))
    return pl.pallas_call(
        functools.partial(deal_kernel, unit, order),
        out_shape=out_shape,
        grid_spec=pltpu.PrefetchScalarGridSpec(
            num_scalar_prefetch=1,
            grid=(rows // step,),
            in_specs=[
                pl.BlockSpec(
                    (line, step, columns),
                    lambda i, at: (0, i % (steps // 2), i // (steps // 2)),
                )
            ]
            * 2,
            out_specs=out_specs,
        ),
        compiler_params=pltpu.CompilerParams(vmem_limit_bytes=32 << 20),
        cost_estimate=pl.CostEstimate(
            flops=0, bytes_accessed=12 * rows * line * columns, transcendentals=0
        ),
    )(where, mine, other)


def join_kernel(turns, turn_ref, left, *refs):
    *pieces, target = refs
    width = left.shape[1]
    size = target.shape[1] - width
    target[:, :width] = left[...]
    keep = pl.program_id(0) % turns == turn_ref[0]
    for piece_index, piece in enumerate(pieces):
        for chunk in range(piece.shape[1] // size):
            value = piece[:, chunk * size : (chunk + 1) * size]
            if turns > 1:
                value = jnp.where(keep, value, jnp.zeros_like(value))
            row = (piece_index * (piece.shape[1] // size) + chunk) * HEAD_DIM
            target[row : row + HEAD_DIM, width:] = value


def join_terms(left, pieces, shards, turns, turn_index):
    rows = left.shape[0] // shards
    extra = sum(piece.shape[1] for piece in pieces) * HEAD_DIM // rows
    width = left.shape[1]
    return pl.pallas_call(
        functools.partial(join_kernel, turns),
        out_shape=jax.ShapeDtypeStruct((left.shape[0], width + extra), left.dtype),
        grid_spec=pltpu.PrefetchScalarGridSpec(
            num_scalar_prefetch=1,
            grid=(shards,),
            in_specs=[pl.BlockSpec((rows, width), lambda i, at: (i, 0))]
            + [
                pl.BlockSpec((HEAD_DIM, piece.shape[1]), lambda i, at: (i // turns, 0))
                for piece in pieces
            ],
            out_specs=pl.BlockSpec((rows, width + extra), lambda i, at: (i, 0)),
        ),
        cost_estimate=pl.CostEstimate(
            flops=0, bytes_accessed=4 * left.shape[0] * (width + extra), transcendentals=0
        ),
    )(turn_index.reshape(1), left, *pieces)


def side_kernel(*refs):
    *pieces, target = refs
    start = 0
    for piece in pieces:
        target[:, start : start + piece.shape[1]] = piece[...].astype(F32)
        start += piece.shape[1]


def side_by_side(*pieces):
    rows = pieces[0].shape[0]
    width = sum(piece.shape[1] for piece in pieces)
    return pl.pallas_call(
        side_kernel,
        out_shape=jax.ShapeDtypeStruct((rows, width), F32),
        grid=(rows // TILE,),
        in_specs=[pl.BlockSpec((TILE, piece.shape[1]), lambda i: (i, 0)) for piece in pieces],
        out_specs=pl.BlockSpec((TILE, width), lambda i: (i, 0)),
        cost_estimate=pl.CostEstimate(flops=0, bytes_accessed=6 * rows * width, transcendentals=0),
    )(*pieces)


def after(value, *others):
    return lax.optimization_barrier((value,) + others)[0]


def shards(
    tokens,
    block_place,
    seq_lengths,
    norm_gain,
    norm_bias,
    qkv_weight,
    qkv_bias,
    out_weight,
    out_bias,
    up_weight,
    up_bias,
    down_weight,
    down_bias,
    out_grad,
):
    ctx_count, ctx_index = lax.axis_size("ctx"), lax.axis_index("ctx")
    shard_count, shard_index = lax.axis_size("fsdp"), lax.axis_index("fsdp")
    own_tokens, own_grad = tokens[0], out_grad[0]
    own_rows, model_width = own_tokens.shape
    hidden_width = up_weight.shape[1]
    heads = model_width // HEAD_DIM
    own_heads = heads // ctx_count
    shard_heads = heads // shard_count
    unit = hidden_width // shard_count // ctx_count
    own_width = own_heads * HEAD_DIM
    head_turns = ctx_count // shard_heads
    low_first = list(bits_of("fsdp"))
    high_first = low_first[::-1]

    def pick(value, axis):
        return lax.dynamic_index_in_dim(value, ctx_index, axis, keepdims=False)

    half_width = model_width // 2
    pairs = own_heads // 2

    def section_order(slot):
        pair, rest = slot // 6, slot % 6
        return rest // 2 * own_heads + pair * 2 + rest % 2

    def by_ctx(value):
        return lax.all_gather(value, "ctx", axis=0, tiled=True)

    def as_row(value):
        return value.reshape(1, -1)

    token_count = ctx_count * own_rows
    units = shard_count * unit
    flops = 2 * token_count * model_width
    shard_rows = model_width // shard_count
    both = (low_first, high_first)
    qkv_order = [section_order(slot) for slot in range(3 * own_heads)]
    turn_index, head_slot = ctx_index // shard_heads, ctx_index % shard_heads
    where = jnp.stack([shard_index, ctx_index % 2]).astype(jnp.int32)

    all_tokens = by_ctx(own_tokens)
    own_inner = pick_columns(
        [up_weight, qkv_weight],
        [unit, HEAD_DIM],
        [list(range(shard_count)), qkv_order],
        ctx_index,
        ctx_count,
    )
    vectors = (norm_gain, norm_bias, qkv_bias, out_bias, up_bias, down_bias)
    inner_flow = Flow(gather_steps(own_inner, *both))
    vector_flow = Flow(direct_steps(jnp.concatenate(vectors).reshape(8, -1)))
    grad_first = by_ctx(after(own_grad[:, :half_width], own_inner))

    def prepare(down_weight, out_weight):
        own_down = pick(down_weight.reshape(ctx_count, unit, model_width), 0)
        own_out = lax.dynamic_index_in_dim(
            out_weight.reshape(shard_heads, HEAD_DIM, model_width), head_slot, 0, keepdims=False
        )
        return own_down, own_out

    def both_tables(ends, block_place):
        natural = jnp.arange(token_count, dtype=jnp.int32)
        given = (block_place[:, None] * BLK + jnp.arange(BLK, dtype=jnp.int32)).reshape(-1)
        return turn_tables(natural, ends), turn_tables(given, ends)

    ends = jnp.cumsum(seq_lengths[0]).astype(jnp.int32)
    own_down, own_out = beside(prepare, (down_weight, out_weight), [inner_flow, vector_flow])
    grad_second = by_ctx(after(own_grad[:, half_width:], own_down))
    natural_tables, given_tables = beside(both_tables, (ends, block_place), [inner_flow])
    while inner_flow.moves:
        own_down, own_out = beside(lambda *same: same, (own_down, own_out), [inner_flow])
    packed = jnp.stack([piece.reshape(-1) for _, _, piece in vector_flow.result])
    packed = jnp.concatenate(
        [lax.dynamic_index_in_dim(packed, shard_index ^ i, 0) for i in range(shard_count)]
    )
    cuts = [0]
    for vector in vectors:
        cuts.append(cuts[-1] + vector.shape[0])
    gain_all, shift_all, qkv_bias_all, out_bias_all, up_bias_all, down_bias_all = [
        packed[:, start:stop].reshape(-1).astype(F32) for start, stop in zip(cuts, cuts[1:])
    ]
    own_qkv_bias = pick(qkv_bias_all.reshape(3, pairs, 2, ctx_count, HEAD_DIM), 3)
    own_qkv_bias = jnp.transpose(own_qkv_bias, (1, 0, 2, 3)).reshape(-1)
    own_up_bias = pick(up_bias_all.reshape(shard_count, ctx_count, unit), 1).reshape(-1)
    inner_bias = jnp.concatenate([own_up_bias, own_qkv_bias])
    inner = (shard_rows, inner_flow.result)
    down_flow = Flow(direct_steps(own_down))
    out_flow = Flow(direct_steps(own_out))

    def enter(rows):
        return row_call(
            enter_kernel,
            where,
            [rows, *given_tables],
            [as_row(gain_all), as_row(shift_all), as_row(inner_bias)],
            [inner],
            [(model_width, BF16), (units, BF16), (units, BF16), (3 * own_width, BF16)],
            [],
            flops * (units + 3 * own_width),
        )

    normed, slope, active, linear = beside(enter, (all_tokens,), [down_flow])

    def down_terms(rows):
        return dot_tn(active, rows).astype(BF16).reshape(shard_count, unit, half_width)

    first_terms = down_terms(after(grad_first, active))
    first_flow = Flow(scatter_steps(first_terms, *both))
    attended, *kept = beside(
        lambda rows: attention_forward(block_place, ends, rows),
        (linear,),
        [first_flow, out_flow],
    )
    down = (unit, down_flow.result)
    out = (HEAD_DIM, out_flow.result)
    if head_turns > 1:
        out_all = jnp.stack([piece for _, _, piece in out_flow.result])
        out_all = jnp.concatenate(
            [
                lax.dynamic_index_in_dim(
                    out_all, shard_index ^ (i * head_turns + turn_index), 0, keepdims=False
                )
                for i in range(own_heads)
            ]
        )
        out = (own_width, [(None, 0, out_all)])
    second_terms = beside(down_terms, (after(grad_second, attended),), [first_flow])
    while first_flow.moves:
        second_terms = beside(lambda same: same, (second_terms,), [first_flow])
    second_flow = Flow(scatter_steps(second_terms, *both))

    def leave(rows):
        return row_call(
            leave_kernel,
            where,
            [rows, active],
            [],
            [down, out],
            [(model_width, BF16)],
            [],
            flops * (units + own_width),
            split=True,
        )

    def back(rows):
        return row_call(
            back_kernel,
            where,
            [grad_first, rows, slope],
            [],
            [down, out],
            [(units, BF16), (own_width, BF16)],
            [(1, units)],
            flops * (units + own_width),
        )

    grad_hidden, grad_att, hidden_sum = beside(
        back, (after(grad_second, first_flow.result),), [second_flow]
    )
    up_terms = beside(
        lambda rows: dot_tn(normed, rows).astype(BF16), (grad_hidden,), [second_flow]
    )
    while second_flow.moves:
        up_terms = beside(lambda same: same, (up_terms,), [second_flow])
    up_flow = Flow(scatter_steps(up_terms.reshape(shard_count, shard_rows, units), *both, fold=1))
    out_halves = beside(leave, (after(attended, second_flow.result),), [up_flow])
    core_flow = Flow(swap_steps(out_halves[1], out_halves[0]))
    held = []
    down_total = tuple(by_ctx(flow.result) for flow in (first_flow, second_flow))
    grad_mixed, weave = (), None
    for pair in range(pairs):

        def backward(rows, *halves):
            if halves:
                held.append(add_pair(*halves))
            result = attention_backward(
                pair, block_place, ends, natural_tables, kept, rows, grad_mixed
            )
            return [result, *held]

        rows = after(grad_att, *out_halves, down_total[min(pair, 1)])
        halves = core_flow.result if weave else ()
        flows = [weave] if weave else [flow for flow in (up_flow, core_flow) if flow.moves]
        grad_mixed = (beside(backward, (rows, *halves), flows)[0],)
        while up_flow.moves and pair + 1 == pairs:
            out_halves = beside(lambda *same: same, tuple(out_halves), [up_flow])
        if not up_flow.moves and weave is None:
            weave = Flow(weave_steps(up_flow.result, held, out_halves[0].shape))
    if not held:
        held.append(add_pair(*core_flow.result))
    (grad_mixed,) = grad_mixed

    def joint(rows):
        late = after(attended, rows)
        out_terms = [dot_tn(late, piece).astype(BF16) for piece in (grad_first, grad_second)]
        return join_terms(
            dot_tn(normed, rows).astype(BF16), out_terms, shard_count, head_turns, turn_index
        )

    joint_terms = beside(joint, (grad_mixed,), [weave])
    joint_flow = Flow(
        scatter_steps(joint_terms.reshape(shard_count, shard_rows, -1), *both, fold=1)
    )

    def norm_back(rows):
        return row_call(
            norm_back_kernel,
            where,
            [all_tokens, rows, grad_hidden],
            [],
            [inner],
            [(model_width, BF16)],
            [(1, model_width), (1, model_width), (1, 3 * own_width)],
            flops * (units + 3 * own_width),
            split=True,
        )

    mine, other, gain_sum, shift_sum, mixed_sum = beside(
        norm_back, (after(grad_mixed, joint_terms),), [joint_flow, weave]
    )

    def spread(value, count):
        value = value.reshape(count, 1, -1)
        whole = jnp.zeros((count, ctx_count, value.shape[2]), F32)
        return lax.dynamic_update_slice_in_dim(whole, value, ctx_index, 1).reshape(-1)

    grad_float = own_grad.astype(F32)
    mixed_sum = jnp.transpose(mixed_sum.reshape(pairs, 3, 2 * HEAD_DIM), (1, 0, 2))
    sums = (
        gain_sum.reshape(-1),
        shift_sum.reshape(-1),
        spread(mixed_sum, 3 * own_heads),
        jnp.sum(grad_float, axis=0),
        spread(hidden_sum, shard_count),
    )
    total_flow = Flow(total_steps(jnp.concatenate(sums)))
    at = jnp.stack([shard_index % head_turns, ctx_index % 2]).astype(jnp.int32)

    def nothing():
        return ()

    while weave.moves:
        beside(nothing, (), [weave])
    up_blocks, out_finish = weave.result
    core_flow = Flow(swap_steps(other, mine))
    down_total = beside(side_by_side, down_total, [joint_flow, core_flow], late=[out_finish])
    while joint_flow.moves:
        beside(nothing, (), [joint_flow])
    held = []
    weave = Flow(weave_steps(joint_flow.result, held, mine.shape))

    def order_and_add(blocks, halves):
        held.append(add_pair(*halves))
        return in_order(*blocks), held[0]

    up_blocks, _ = beside(
        order_and_add, (up_blocks, core_flow.result), [weave, total_flow], early=[out_finish]
    )
    up_swap = Flow(swap_steps(up_blocks))
    beside(nothing, (), [flow for flow in (weave, total_flow, up_swap) if flow.moves])
    (up_dealt,) = beside(
        lambda *halves: deal_columns(*halves, unit, list(range(shard_count)), at),
        up_swap.result,
        [flow for flow in (weave, total_flow) if flow.moves],
    )
    while weave.moves:
        beside(nothing, (), [flow for flow in (weave, total_flow) if flow.moves])
    joint_blocks, norm_finish = weave.result
    joint_swap = Flow(swap_steps(in_order(*joint_blocks)))
    beside(
        nothing, (), [flow for flow in (joint_swap, total_flow) if flow.moves], late=[norm_finish]
    )
    qkv_dealt, out_dealt = beside(
        lambda *halves: deal_columns(*halves, HEAD_DIM, qkv_order, at, with_out=True),
        joint_swap.result,
        [flow for flow in (total_flow,) if flow.moves],
        early=[norm_finish],
    )
    out_sum, grad_normed = out_finish.result, norm_finish.result

    inputs = own_tokens.astype(F32)
    output = (inputs + out_sum + (out_bias_all + down_bias_all)).astype(BF16)

    scaled, inv_std = standard(own_tokens)
    grad_scaled = grad_normed * gain_all
    grad_input = inv_std * (
        grad_scaled
        - jnp.mean(grad_scaled, axis=1, keepdims=True)
        - scaled * jnp.mean(grad_scaled * scaled, axis=1, keepdims=True)
    )
    input_grad = (grad_float + grad_input).astype(BF16)

    while total_flow.moves:
        beside(nothing, (), [total_flow])
    total = total_flow.result
    own_sums, start = [], 0
    for item in sums:
        size = item.shape[0] // shard_count
        own_sums.append(lax.dynamic_slice_in_dim(total, start + shard_index * size, size))
        start += item.shape[0]
    gain_total, shift_total, qkv_bias_total, bias_total, up_bias_total = own_sums

    return (
        output[None],
        input_grad[None],
        gain_total,
        shift_total,
        qkv_dealt,
        qkv_bias_total,
        out_dealt,
        bias_total,
        up_dealt,
        up_bias_total,
        down_total,
        bias_total,
    )


def solution(mesh):
    in_specs = (
        P("fsdp", "ctx", None),
        P(),
        P("fsdp", None),
        P("fsdp"),
        P("fsdp"),
        P("fsdp", None),
        P("fsdp"),
        P("fsdp", None),
        P("fsdp"),
        P("fsdp", None),
        P("fsdp"),
        P("fsdp", None),
        P("fsdp"),
        P("fsdp", "ctx", None),
    )
    out_specs = (
        P("fsdp", "ctx", None),
        P("fsdp", "ctx", None),
        P("fsdp"),
        P("fsdp"),
        P("fsdp", None),
        P("fsdp"),
        P("fsdp", None),
        P("fsdp"),
        P("fsdp", None),
        P("fsdp"),
        P("fsdp", None),
        P("fsdp"),
    )
    return jax.shard_map(shards, mesh=mesh, in_specs=in_specs, out_specs=out_specs, check_vma=False)
```

```python
import functools

import jax
import jax.numpy as jnp
from jax import lax
from jax.experimental import pallas as pl
from jax.experimental.pallas import tpu as pltpu
from jax.sharding import PartitionSpec as P

HEAD_DIM = 64
ROT = 32
BLK = 16
TILE = 512
WIDE = 512
ROWS = 512
LANES = 128
F32 = jnp.float32
BF16 = jnp.bfloat16


def dot_nn(left, right):
    return lax.dot_general(left, right, (((1,), (0,)), ((), ())), preferred_element_type=F32)


def dot_nt(left, right):
    return lax.dot_general(left, right, (((1,), (1,)), ((), ())), preferred_element_type=F32)


def dot_tn(left, right):
    return lax.dot_general(left, right, (((0,), (0,)), ((), ())), preferred_element_type=F32)


def bits_of(axis):
    return range(lax.axis_size(axis).bit_length() - 1)


def swaps(axis, mask):
    return axis, [(i, i ^ mask) for i in range(lax.axis_size(axis))]


class Flow:
    def __init__(self, steps):
        self.steps = steps
        self.result = None
        self.moves = next(steps)

    def arrive(self, values):
        try:
            self.moves = self.steps.send(values)
        except StopIteration as stop:
            self.moves, self.result = [], stop.value


def beside(work, inputs, flows, late=(), early=()):
    starting = [*flows, *late]
    sends = [[value for value, _, _ in flow.moves] for flow in starting]
    inputs, sends = lax.optimization_barrier((inputs, sends))
    for flow, values in zip(starting, sends):
        flow.moving = [
            lax.ppermute(value, axis, pairs) for value, (_, axis, pairs) in zip(values, flow.moves)
        ]
    outputs = work(*inputs)
    ending = [*flows, *early]
    outputs, arrived = lax.optimization_barrier((outputs, [flow.moving for flow in ending]))
    for flow, values in zip(ending, arrived):
        flow.arrive(values)
    return outputs


def gather_steps(own, *orders):
    share = own.shape[0] // len(orders)
    held = [[(0, own[i * share : (i + 1) * share])] for i in range(len(orders))]
    for step in range(len(orders[0])):
        moves = [
            (piece, *swaps("fsdp", 1 << order[step]))
            for pieces, order in zip(held, orders)
            for _, piece in pieces
        ]
        arrived = iter((yield moves))
        for i, order in enumerate(orders):
            held[i] = held[i] + [(mask ^ (1 << order[step]), next(arrived)) for mask, _ in held[i]]
    return [
        (mask, i * share, piece) for i, pieces in enumerate(held) for mask, piece in pieces
    ]


def direct_steps(own):
    masks = range(1, lax.axis_size("fsdp"))
    arrived = yield [(own, *swaps("fsdp", mask)) for mask in masks]
    return [(0, 0, own)] + [(mask, 0, piece) for mask, piece in zip(masks, arrived)]


def scatter_steps(parts, *orders, fold=0):
    index = lax.axis_index("fsdp")
    bits = len(orders[0])
    share = parts.shape[1] // len(orders)
    held = [
        parts[:, i * share : (i + 1) * share].reshape((2,) * bits + (share, parts.shape[2]))
        for i in range(len(orders))
    ]
    left = [list(range(bits))[::-1] for _ in orders]
    for step in range(bits):
        moves, keeps = [], []
        for i, order in enumerate(orders):
            axis = left[i].index(order[step])
            left[i].pop(axis)
            mine = (index >> order[step]) & 1
            send = lax.dynamic_index_in_dim(held[i], 1 - mine, axis, keepdims=False)
            keeps.append(lax.dynamic_index_in_dim(held[i], mine, axis, keepdims=False))
            moves.append((send, *swaps("fsdp", 1 << order[step])))
        arrived = yield moves
        held = [
            (keep.astype(F32) + got.astype(F32)).astype(BF16) for keep, got in zip(keeps, arrived)
        ]
    return jnp.concatenate(held, axis=fold)


def swap_steps(value, kept=None):
    (got,) = yield [(value, *swaps("ctx", 1))]
    return value if kept is None else kept, got


def add_pair(mine, got):
    return (mine.astype(F32) + got.astype(F32)).astype(BF16)


def weave_steps(own, held, shape):
    count = lax.axis_size("ctx")
    line = count // 2
    place = lax.axis_index("ctx") // 2
    alike = own.shape == shape[1:]
    forth = [(i, i + 2) for i in range(count - 2)]
    back = [(i, i - 2) for i in range(2, count)]
    ups, downs = [], []
    up, down = yield [(own, "ctx", forth), (own, "ctx", back)]
    up_sum, down_sum = (up, down) if alike else (jnp.zeros(shape[1:], BF16),) * 2

    def block(target, added):
        target = jnp.clip(target, 0, line - 1)
        part = lax.dynamic_index_in_dim(held[0], target, 0, keepdims=False)
        return part.astype(F32) + added.astype(F32)

    for step in range(2, line + 1):
        ups.append(up)
        downs.append(down)
        far = line + 1 - step
        up_sum = block(place + far, up_sum).astype(BF16)
        down_sum = block(place - far, down_sum).astype(BF16)
        if step == line:
            break
        if alike:
            up_sum = jnp.where(place >= step - 1, up, up_sum)
            down_sum = jnp.where(place <= line - step, down, down_sum)
            up_sum, down_sum = yield [(up_sum, "ctx", forth), (down_sum, "ctx", back)]
            up, down = up_sum, down_sum
        else:
            up, down, up_sum, down_sum = yield [
                (up, "ctx", [(i, j) for i, j in forth if i // 2 >= step - 1]),
                (down, "ctx", [(i, j) for i, j in back if i // 2 <= line - step]),
                (up_sum, "ctx", [(i, j) for i, j in forth if i // 2 < step - 1]),
                (down_sum, "ctx", [(i, j) for i, j in back if i // 2 > line - step]),
            ]

    def finish():
        last_up, last_down = yield [(up_sum, "ctx", forth), (down_sum, "ctx", back)]
        return block(place, last_up) + last_down.astype(F32)

    return (own, ups, downs), Flow(finish())


def in_order(own, ups, downs):
    place = lax.axis_index("ctx") // 2
    blocks = []
    for chip in range(len(ups) + 1):
        value = own
        for away, (up, down) in enumerate(zip(ups, downs), 1):
            value = jnp.where(place == chip + away, up, value)
            value = jnp.where(place == chip - away, down, value)
        blocks.append(value)
    return jnp.stack(blocks)


def total_steps(vector):
    for axis in ("ctx", "fsdp"):
        for bit in bits_of(axis):
            (got,) = yield [(vector, *swaps(axis, 1 << bit))]
            vector = vector + got
    return vector


def turn(values, cosine, sine):
    lane = lax.broadcasted_iota(jnp.int32, values.shape, 1) % HEAD_DIM
    half = ROT // 2
    partner = jnp.where(
        lane < half, pltpu.roll(values, LANES - half, 1), pltpu.roll(values, half, 1)
    )
    return values * cosine + partner * sine


def first_half(shape):
    return lax.broadcasted_iota(jnp.int32, shape, 1) < HEAD_DIM


def visible_range(ends_ref, step, wide, tile):
    top = step * wide
    column = top + lax.broadcasted_iota(jnp.int32, (1, wide), 1)
    begin = jnp.zeros((1, wide), jnp.int32)
    first = jnp.int32(0)
    for sequence in range(ends_ref.shape[0]):
        end = ends_ref[sequence]
        begin = jnp.where(column >= end, jnp.maximum(begin, end), begin)
        first = jnp.where(top >= end, jnp.maximum(first, end), first)
    return column, begin, first // tile


def each_head(values, axis=1):
    half = lax.broadcasted_iota(jnp.int32, values.shape, axis) < HEAD_DIM
    zero = jnp.zeros_like(values)
    return [jnp.where(half, values, zero), jnp.where(half, zero, values)]


Q_LANES, K_LANES, V_LANES = (slice(i * LANES, (i + 1) * LANES) for i in range(3))
HEAD_ROWS = (slice(0, HEAD_DIM), slice(HEAD_DIM, LANES))


def each_block(place_ref, act):
    @pl.loop(0, place_ref.shape[0])
    def _(block):
        act(
            pl.ds(pl.multiple_of(block * BLK, BLK), BLK),
            pl.ds(pl.multiple_of(place_ref[block] * BLK, BLK), BLK),
        )


def part_lanes(pair, which):
    start = (3 * pair + which) * LANES
    return slice(start, start + LANES)


def forward_kernel(
    place_ref, ends_ref, lin_hbm, att_hbm, rows, summed_ref, lse_ref, values_t, att, sems
):
    tokens = rows.shape[0]
    tile, wide = TILE, WIDE
    pairs = rows.shape[1] // LANES // 3
    heads = 2 * pairs
    each_block(
        place_ref,
        lambda given, natural: pltpu.make_async_copy(
            lin_hbm.at[given], rows.at[natural], sems.at[0]
        ).start(),
    )
    pltpu.make_async_copy(lin_hbm, rows, sems.at[0]).wait()

    @pl.loop(0, tokens // tile)
    def _(step):
        part = pl.ds(pl.multiple_of(step * tile, tile), tile)
        for pair in range(pairs):
            lanes = slice(pair * LANES, (pair + 1) * LANES)
            values_t[lanes, part] = rows[part, part_lanes(pair, 2)].T

    @pl.loop(0, tokens // wide)
    def _(step):
        part = pl.ds(pl.multiple_of(step * wide, wide), wide)
        column, begin, low = visible_range(ends_ref, step, wide, tile)
        queries = [
            query
            for pair in range(pairs)
            for query in each_head(rows[part, part_lanes(pair, 0)].T, 0)
        ]

        def combine(index, state):
            there = pl.ds(pl.multiple_of(index * tile, tile), tile)
            row = index * tile + lax.broadcasted_iota(jnp.int32, (tile, wide), 0)
            visible = (row <= column) & (row >= begin)
            result = []
            for head in range(heads):
                top, total, summed = state[head]
                key = rows[there, part_lanes(head // 2, 1)]
                scores = jnp.where(visible, dot_nn(key, queries[head]), -1e30)
                new_top = jnp.maximum(top, jnp.max(scores, axis=0, keepdims=True))
                weight = jnp.exp(scores - new_top)
                factor = jnp.exp(top - new_top)
                total = total * factor + jnp.sum(weight, axis=0, keepdims=True)
                here = slice(head * HEAD_DIM, (head + 1) * HEAD_DIM)
                summed = summed * factor + dot_nn(values_t[here, there], weight.astype(BF16))
                result.append((new_top, total, summed))
            return tuple(result)

        empty = (
            jnp.full((1, wide), -1e30, F32),
            jnp.zeros((1, wide), F32),
            jnp.zeros((HEAD_DIM, wide), F32),
        )
        state = lax.fori_loop(low, (step + 1) * (wide // tile), combine, (empty,) * heads)
        for head in range(heads):
            top, total, summed = state[head]
            summed_ref[head * HEAD_DIM : (head + 1) * HEAD_DIM, part] = summed * (1.0 / total)
            lse_ref[head : head + 1, part] = top + jnp.log(total)
        for pair in range(pairs):
            lanes = slice(pair * LANES, (pair + 1) * LANES)
            att[part, lanes] = summed_ref[lanes, part].T.astype(BF16)

    each_block(
        place_ref,
        lambda given, natural: pltpu.make_async_copy(
            att.at[natural], att_hbm.at[given], sems.at[0]
        ).start(),
    )
    pltpu.make_async_copy(att, att_hbm, sems.at[0]).wait()


def backward_kernel(
    pair, place_ref, ends_ref, cos_ref, sin_ref, rows, summed_ref, lse_ref, grad_hbm, *refs
):
    mixed_hbm, grad, grad_t, keys_t, grad_k, grad_v, mixed, sems = refs[-8:]
    tokens = grad.shape[0]
    tile, wide = TILE, WIDE
    lanes = slice(pair * LANES, (pair + 1) * LANES)
    lanes3 = slice(3 * pair * LANES, 3 * (pair + 1) * LANES)
    each_block(
        place_ref,
        lambda given, natural: pltpu.make_async_copy(
            grad_hbm.at[given, lanes], grad.at[natural], sems.at[0]
        ).start(),
    )
    grad_k[...] = jnp.zeros_like(grad_k)
    grad_v[...] = jnp.zeros_like(grad_v)

    @pl.loop(0, tokens // tile)
    def _(step):
        part = pl.ds(pl.multiple_of(step * tile, tile), tile)
        keys_t[:, part] = rows[part, K_LANES].T

    pltpu.make_async_copy(grad_hbm.at[:, lanes], grad, sems.at[0]).wait()

    @pl.loop(0, tokens // wide)
    def _(step):
        part = pl.ds(pl.multiple_of(step * wide, wide), wide)
        column, begin, low = visible_range(ends_ref, step, wide, tile)
        query, back = rows[part, Q_LANES], grad[part, :]
        back_t = back.T
        queries, queries_t = each_head(query), each_head(query.T, 0)
        backs, backs_t = each_head(back), each_head(back_t, 0)
        grad_t[...] = back_t.astype(F32)
        delta = [
            jnp.sum(summed_ref[here, part] * grad_t[here, :], axis=0, keepdims=True)
            for here in HEAD_ROWS
        ]
        lse = [lse_ref[2 * pair + head : 2 * pair + head + 1, part] for head in range(2)]

        def back_step(index, sums):
            there = pl.ds(pl.multiple_of(index * tile, tile), tile)
            row = index * tile + lax.broadcasted_iota(jnp.int32, (tile, wide), 0)
            visible = (row <= column) & (row >= begin)
            key, value = rows[there, K_LANES], rows[there, V_LANES]
            result, add_k, add_v = [], 0.0, 0.0
            for head in range(2):
                scores = jnp.where(visible, dot_nn(key, queries_t[head]), -1e30)
                weight = jnp.exp(scores - lse[head])
                grad_w = dot_nn(value, backs_t[head])
                grad_s = (weight * (grad_w - delta[head])).astype(BF16)
                add_k = add_k + dot_nn(grad_s, queries[head])
                add_v = add_v + dot_nn(weight.astype(BF16), backs[head])
                result.append(sums[head] + dot_nn(keys_t[HEAD_ROWS[head], there], grad_s))
            grad_k[there, :] += add_k
            grad_v[there, :] += add_v
            return tuple(result)

        sums = lax.fori_loop(low, (step + 1) * (wide // tile), back_step, (jnp.zeros((HEAD_DIM, wide), F32),) * 2)
        grad_q = jnp.concatenate(sums, axis=0).T * HEAD_DIM ** (-0.5)
        mixed[part, Q_LANES] = turn(grad_q, cos_ref[part, :], -sin_ref[part, :]).astype(BF16)

    @pl.loop(0, tokens // tile)
    def _(step):
        part = pl.ds(pl.multiple_of(step * tile, tile), tile)
        turned = turn(grad_k[part, :], cos_ref[part, :], -sin_ref[part, :])
        mixed[part, K_LANES] = turned.astype(BF16)
        mixed[part, V_LANES] = grad_v[part, :].astype(BF16)

    each_block(
        place_ref,
        lambda given, natural: pltpu.make_async_copy(
            mixed.at[natural], mixed_hbm.at[given, lanes3], sems.at[0]
        ).start(),
    )
    pltpu.make_async_copy(mixed, mixed_hbm.at[:, lanes3], sems.at[0]).wait()


def turn_tables(position, ends):
    begin = jnp.max(jnp.where(position[:, None] >= ends[None, :], ends[None, :], 0), axis=1)
    within = (position - begin).astype(F32)
    half = ROT // 2
    lane = jnp.arange(LANES, dtype=jnp.int32) % HEAD_DIM
    frequency = 10000.0 ** (-(lane % half).astype(F32) * 2.0 / ROT)
    angles = within[:, None] * jnp.where(lane < ROT, frequency, 0.0)[None, :]
    return jnp.cos(angles), jnp.sin(angles) * jnp.where(lane < half, -1.0, 1.0)[None, :]


SMEM = pl.BlockSpec(memory_space=pltpu.SMEM)
VMEM = pl.BlockSpec(memory_space=pltpu.VMEM)
ANYWHERE = pl.BlockSpec(memory_space=pl.ANY)


def attention_forward(block_place, ends, linear):
    tokens, width3 = linear.shape
    width = width3 // 3
    return pl.pallas_call(
        forward_kernel,
        out_shape=(
            jax.ShapeDtypeStruct((tokens, width), BF16),
            jax.ShapeDtypeStruct((tokens, width3), BF16),
            jax.ShapeDtypeStruct((width, tokens), F32),
            jax.ShapeDtypeStruct((width // HEAD_DIM, tokens), F32),
        ),
        in_specs=[SMEM, SMEM, ANYWHERE],
        out_specs=(ANYWHERE, VMEM, VMEM, VMEM),
        scratch_shapes=[
            pltpu.VMEM((width, tokens), BF16),
            pltpu.VMEM((tokens, width), BF16),
            pltpu.SemaphoreType.DMA((1,)),
        ],
        compiler_params=pltpu.CompilerParams(vmem_limit_bytes=60 << 20),
        cost_estimate=pl.CostEstimate(
            flops=40 * 10**9, bytes_accessed=16 * 10**6, transcendentals=0
        ),
    )(block_place, ends, linear)


def attention_backward(pair, block_place, ends, tables, kept, grad_att, before):
    tokens, width = grad_att.shape
    return pl.pallas_call(
        functools.partial(backward_kernel, pair),
        out_shape=jax.ShapeDtypeStruct((tokens, 3 * width), BF16),
        grid=(1,),
        in_specs=[
            SMEM,
            SMEM,
            VMEM,
            VMEM,
            pl.BlockSpec((tokens, 3 * LANES), lambda i: (0, pair)),
            pl.BlockSpec((LANES, tokens), lambda i: (pair, 0)),
            VMEM,
        ]
        + [ANYWHERE] * (1 + len(before)),
        out_specs=ANYWHERE,
        input_output_aliases={8 + i: i for i in range(len(before))},
        scratch_shapes=[
            pltpu.VMEM((tokens, LANES), BF16),
            pltpu.VMEM((LANES, WIDE), F32),
            pltpu.VMEM((LANES, tokens), BF16),
            pltpu.VMEM((tokens, LANES), F32),
            pltpu.VMEM((tokens, LANES), F32),
            pltpu.VMEM((tokens, 3 * LANES), BF16),
            pltpu.SemaphoreType.DMA((1,)),
        ],
        compiler_params=pltpu.CompilerParams(vmem_limit_bytes=60 << 20),
        cost_estimate=pl.CostEstimate(
            flops=20 * 10**9, bytes_accessed=8 * 10**6, transcendentals=0
        ),
    )(block_place, ends, *tables, *kept, grad_att, *before)


def row_call(kernel, where, rows, whole, assembled, outs, sums, flops, split=False):
    count = rows[0].shape[0]
    tiles = count // ROWS
    shards = lax.axis_size("fsdp")
    pieces = [piece for _, group in assembled for _, _, piece in group]
    height = sum(sum(piece.shape[0] for _, _, piece in group) for _, group in assembled)

    def body(at, *refs):
        inputs = refs[: len(rows) + len(whole)]
        sources = refs[len(inputs) : len(inputs) + len(pieces)]
        targets = refs[len(inputs) + len(pieces) : -2]
        buffer, sems = refs[-2:]

        @pl.when(pl.program_id(0) == 0)
        def _():
            copies, base = [], 0
            for shard_height, group in assembled:
                for mask, start, piece in group:
                    first = start if mask is None else (at[0] ^ mask) * shard_height + start
                    size = piece.shape[0]
                    target = buffer.at[pl.ds(pl.multiple_of(base + first, size), size)]
                    slot = len(copies)
                    copies.append(pltpu.make_async_copy(sources[slot], target, sems.at[slot]))
                base += sum(piece.shape[0] for _, _, piece in group)
            for copy in copies:
                copy.start()
            for copy in copies:
                copy.wait()

        if split:
            mine, other, *rest = targets

            def put(part, value):
                even = at[1] == 0
                half = value.shape[0] // 2
                first, second = value[:half], value[half:]
                mine[0, :, part] = jnp.where(even, first, second)
                other[0, :, part] = jnp.where(even, second, first)

            kernel(*inputs, buffer, put, *rest)
        else:
            kernel(*inputs, buffer, *targets)

    by_tile = lambda columns: pl.BlockSpec((ROWS, columns), lambda i, at: (i, 0))
    stay = lambda shape: pl.BlockSpec(shape, lambda i, at: (0, 0))
    moved = sum(item.size * item.dtype.itemsize for item in (*rows, *whole, *pieces))
    moved += sum(count * columns * jnp.dtype(kind).itemsize for columns, kind in outs)
    if split:
        ((columns, kind),) = outs
        out_shape = [jax.ShapeDtypeStruct((tiles, ROWS // 2, columns), kind)] * 2
        out_specs = [pl.BlockSpec((1, ROWS // 2, columns), lambda i, at: (i, 0, 0))] * 2
    else:
        out_shape = [jax.ShapeDtypeStruct((count, columns), kind) for columns, kind in outs]
        out_specs = [by_tile(columns) for columns, _ in outs]
    return pl.pallas_call(
        body,
        out_shape=out_shape + [jax.ShapeDtypeStruct(shape, F32) for shape in sums],
        grid_spec=pltpu.PrefetchScalarGridSpec(
            num_scalar_prefetch=1,
            grid=(tiles,),
            in_specs=[by_tile(item.shape[1]) for item in rows]
            + [stay(item.shape) for item in whole]
            + [ANYWHERE] * len(pieces),
            out_specs=out_specs + [stay(shape) for shape in sums],
            scratch_shapes=[
                pltpu.VMEM((height, pieces[0].shape[1]), BF16),
                pltpu.SemaphoreType.DMA((len(pieces),)),
            ],
        ),
        compiler_params=pltpu.CompilerParams(vmem_limit_bytes=60 << 20),
        cost_estimate=pl.CostEstimate(flops=flops, bytes_accessed=moved, transcendentals=0),
    )(where, *rows, *whole, *pieces)


def chunks_of(columns, size=256):
    return [slice(start, min(start + size, columns)) for start in range(0, columns, size)]


def standard(rows):
    values = rows.astype(F32)
    centred = values - jnp.mean(values, axis=1, keepdims=True)
    inv_std = lax.rsqrt(jnp.mean(centred * centred, axis=1, keepdims=True) + 1e-05)
    return centred * inv_std, inv_std


def enter_kernel(
    tokens, cosine, sine, gain, shift, bias, inner, normed_out, slope_out, active_out, linear_out
):
    for start in range(0, tokens.shape[0], 32):
        part = slice(start, start + 32)
        scaled, _ = standard(tokens[part, :])
        normed_out[part, :] = (scaled * gain[...] + shift[...]).astype(BF16)
    normed = normed_out[...]
    units = active_out.shape[1]
    for part in chunks_of(units):
        hidden = dot_nn(normed, inner[:, part]) + bias[:, part]
        square = hidden * hidden
        gate = 1.0 / (1.0 + jnp.exp(hidden * (-1.5957691216057308 - 0.07135481627260025 * square)))
        value = hidden * gate
        active_out[:, part] = value.astype(BF16)
        inner_slope = 1.5957691216057308 + 0.21406444881780073 * square
        slope_out[:, part] = (gate + (value - value * gate) * inner_slope).astype(BF16)
    for part in chunks_of(linear_out.shape[1], 3 * LANES):
        there = slice(units + part.start, units + part.stop)
        value = dot_nn(normed, inner[:, there]) + bias[:, there]
        query = turn(value[:, Q_LANES], cosine[...], sine[...]) * HEAD_DIM ** (-0.5)
        key = turn(value[:, K_LANES], cosine[...], sine[...])
        joined = jnp.concatenate([query, key, value[:, V_LANES]], axis=1)
        linear_out[:, part] = joined.astype(BF16)


def back_kernel(first, second, slope, weights, hidden_out, att_out, hidden_sum):
    @pl.when(pl.program_id(0) == 0)
    def _():
        hidden_sum[...] = jnp.zeros_like(hidden_sum)

    rows = jnp.concatenate([first[...], second[...]], axis=1)
    units = slope.shape[1]
    for part in chunks_of(units):
        grad = (dot_nt(rows, weights[part, :]) * slope[:, part]).astype(BF16)
        hidden_out[:, part] = grad
        hidden_sum[:, part] += jnp.sum(grad.astype(F32), axis=0, keepdims=True)
    for part in chunks_of(att_out.shape[1]):
        there = slice(units + part.start, units + part.stop)
        att_out[:, part] = dot_nt(rows, weights[there, :]).astype(BF16)


def leave_kernel(attended, active, weights, put):
    rows = jnp.concatenate([active[...], attended[...]], axis=1)
    for part in chunks_of(weights.shape[1], 512):
        put(part, dot_nn(rows, weights[:, part]).astype(BF16))


def norm_back_kernel(tokens, mixed, hidden, inner, put, gain_sum, shift_sum, mixed_sum):
    @pl.when(pl.program_id(0) == 0)
    def _():
        for total in (gain_sum, shift_sum, mixed_sum):
            total[...] = jnp.zeros_like(total)

    scaled, _ = standard(tokens[...])
    mixed_sum[...] += jnp.sum(mixed[...].astype(F32), axis=0, keepdims=True)
    rows = jnp.concatenate([hidden[...], mixed[...]], axis=1)
    for part in chunks_of(inner.shape[0], 512):
        grad = dot_nt(rows, inner[part, :])
        put(part, grad.astype(BF16))
        shift_sum[:, part] += jnp.sum(grad, axis=0, keepdims=True)
        gain_sum[:, part] += jnp.sum(grad * scaled[:, part], axis=0, keepdims=True)


def pick_kernel(plans, index_ref, *refs):
    *weights, target, tiles, sems = refs
    at = index_ref[0]
    count = plans[0][2]
    copies, late, slot, column = [], [], 0, 0
    for weight, (unit, order, _) in zip(weights, plans):
        if unit % LANES == 0:
            for place in order:
                first = pl.multiple_of((place * count + at) * unit, unit)
                copies.append(
                    (weight.at[:, pl.ds(first, unit)], target.at[:, column : column + unit])
                )
                column += unit
            continue
        for one, two in zip(order[::2], order[1::2]):
            for which, place in enumerate((one, two)):
                first = pl.multiple_of((place * count + at) // 2 * LANES, LANES)
                copies.append((weight.at[:, pl.ds(first, LANES)], tiles.at[slot, which]))
            late.append((slot, column))
            slot, column = slot + 1, column + LANES
    copies = [
        pltpu.make_async_copy(source, there, sems.at[i])
        for i, (source, there) in enumerate(copies)
    ]
    for copy in copies:
        copy.start()
    for copy in copies:
        copy.wait()
    for slot, column in late:
        first, second = tiles[slot, 0].astype(F32), tiles[slot, 1].astype(F32)
        odd = at % 2 == 1
        first = jnp.where(odd, pltpu.roll(first, HEAD_DIM, 1), first)
        second = jnp.where(odd, second, pltpu.roll(second, HEAD_DIM, 1))
        target[:, column : column + LANES] = jnp.where(
            first_half(first.shape), first, second
        ).astype(target.dtype)


def pick_columns(weights, units, orders, index, count):
    rows = weights[0].shape[0]
    width = sum(unit * len(order) for unit, order in zip(units, orders))
    narrow = [len(order) // 2 for unit, order in zip(units, orders) if unit % LANES]
    copies = sum(len(order) for order in orders)
    return pl.pallas_call(
        functools.partial(pick_kernel, [(unit, order, count) for unit, order in zip(units, orders)]),
        out_shape=jax.ShapeDtypeStruct((rows, width), weights[0].dtype),
        in_specs=[SMEM] + [ANYWHERE] * len(weights),
        out_specs=VMEM,
        scratch_shapes=[
            pltpu.VMEM((sum(narrow), 2, rows, LANES), weights[0].dtype),
            pltpu.SemaphoreType.DMA((copies,)),
        ],
        compiler_params=pltpu.CompilerParams(vmem_limit_bytes=32 << 20),
        cost_estimate=pl.CostEstimate(
            flops=0, bytes_accessed=4 * rows * width, transcendentals=0
        ),
    )(index.reshape(1), *weights)


def deal_kernel(unit, order, at_ref, mine, other, target, *rest):
    line = mine.shape[0]
    count = 2 * line
    even = at_ref[1] == 0

    def both_cores(chip, tile):
        one, two = mine[chip, :, tile], other[chip, :, tile]
        return jnp.where(even, one, two).astype(F32), jnp.where(even, two, one).astype(F32)

    for chip in range(line):
        for group, place in enumerate(order):
            start = (place * count + 2 * chip) * unit
            if unit % LANES == 0:
                values = both_cores(chip, slice(group * unit, (group + 1) * unit))
                for core, value in enumerate(values):
                    target[:, start + core * unit : start + (core + 1) * unit] = value
                continue
            first, second = both_cores(chip, slice(group // 2 * LANES, (group // 2 + 1) * LANES))
            if group % 2:
                first = pltpu.roll(first, HEAD_DIM, 1)
            else:
                second = pltpu.roll(second, HEAD_DIM, 1)
            target[:, start : start + LANES] = jnp.where(first_half(first.shape), first, second)
    for out in rest:
        chips = out.shape[0] // HEAD_DIM // 2
        tail = slice(len(order) * unit, mine.shape[2])
        for chip in range(chips):
            source = chip if chips == line else at_ref[0] * chips + chip
            for core, value in enumerate(both_cores(source, tail)):
                row = (2 * chip + core) * HEAD_DIM
                out[row : row + HEAD_DIM, :] = value


def deal_columns(mine, other, unit, order, where, with_out=False):
    line, rows, columns = mine.shape
    rows, columns = 2 * rows, columns // 2
    width = len(order) * unit
    step = HEAD_DIM
    steps = rows // step
    out_shape = [jax.ShapeDtypeStruct((rows, 2 * line * width), F32)]
    out_specs = [pl.BlockSpec((step, 2 * line * width), lambda i, at: (i, 0))]
    if with_out:
        out_shape.append(jax.ShapeDtypeStruct((rows, (columns - width) * (rows // step)), F32))
        out_specs.append(pl.BlockSpec((rows, columns - width), lambda i, at: (0, i)))
    return pl.pallas_call(
        functools.partial(deal_kernel, unit, order),
        out_shape=out_shape,
        grid_spec=pltpu.PrefetchScalarGridSpec(
            num_scalar_prefetch=1,
            grid=(rows // step,),
            in_specs=[
                pl.BlockSpec(
                    (line, step, columns),
                    lambda i, at: (0, i % (steps // 2), i // (steps // 2)),
                )
            ]
            * 2,
            out_specs=out_specs,
        ),
        compiler_params=pltpu.CompilerParams(vmem_limit_bytes=32 << 20),
        cost_estimate=pl.CostEstimate(
            flops=0, bytes_accessed=12 * rows * line * columns, transcendentals=0
        ),
    )(where, mine, other)


def join_kernel(turns, turn_ref, left, *refs):
    *pieces, target = refs
    width = left.shape[1]
    size = target.shape[1] - width
    target[:, :width] = left[...]
    keep = pl.program_id(0) % turns == turn_ref[0]
    for piece_index, piece in enumerate(pieces):
        for chunk in range(piece.shape[1] // size):
            value = piece[:, chunk * size : (chunk + 1) * size]
            if turns > 1:
                value = jnp.where(keep, value, jnp.zeros_like(value))
            row = (piece_index * (piece.shape[1] // size) + chunk) * HEAD_DIM
            target[row : row + HEAD_DIM, width:] = value


def join_terms(left, pieces, shards, turns, turn_index):
    rows = left.shape[0] // shards
    extra = sum(piece.shape[1] for piece in pieces) * HEAD_DIM // rows
    width = left.shape[1]
    return pl.pallas_call(
        functools.partial(join_kernel, turns),
        out_shape=jax.ShapeDtypeStruct((left.shape[0], width + extra), left.dtype),
        grid_spec=pltpu.PrefetchScalarGridSpec(
            num_scalar_prefetch=1,
            grid=(shards,),
            in_specs=[pl.BlockSpec((rows, width), lambda i, at: (i, 0))]
            + [
                pl.BlockSpec((HEAD_DIM, piece.shape[1]), lambda i, at: (i // turns, 0))
                for piece in pieces
            ],
            out_specs=pl.BlockSpec((rows, width + extra), lambda i, at: (i, 0)),
        ),
        cost_estimate=pl.CostEstimate(
            flops=0, bytes_accessed=4 * left.shape[0] * (width + extra), transcendentals=0
        ),
    )(turn_index.reshape(1), left, *pieces)


def side_kernel(*refs):
    *pieces, target = refs
    start = 0
    for piece in pieces:
        target[:, start : start + piece.shape[1]] = piece[...].astype(F32)
        start += piece.shape[1]


def side_by_side(*pieces):
    rows = pieces[0].shape[0]
    width = sum(piece.shape[1] for piece in pieces)
    return pl.pallas_call(
        side_kernel,
        out_shape=jax.ShapeDtypeStruct((rows, width), F32),
        grid=(rows // TILE,),
        in_specs=[pl.BlockSpec((TILE, piece.shape[1]), lambda i: (i, 0)) for piece in pieces],
        out_specs=pl.BlockSpec((TILE, width), lambda i: (i, 0)),
        cost_estimate=pl.CostEstimate(flops=0, bytes_accessed=6 * rows * width, transcendentals=0),
    )(*pieces)


def after(value, *others):
    return lax.optimization_barrier((value,) + others)[0]


def shards(
    tokens,
    block_place,
    seq_lengths,
    norm_gain,
    norm_bias,
    qkv_weight,
    qkv_bias,
    out_weight,
    out_bias,
    up_weight,
    up_bias,
    down_weight,
    down_bias,
    out_grad,
):
    ctx_count, ctx_index = lax.axis_size("ctx"), lax.axis_index("ctx")
    shard_count, shard_index = lax.axis_size("fsdp"), lax.axis_index("fsdp")
    own_tokens, own_grad = tokens[0], out_grad[0]
    own_rows, model_width = own_tokens.shape
    hidden_width = up_weight.shape[1]
    heads = model_width // HEAD_DIM
    own_heads = heads // ctx_count
    shard_heads = heads // shard_count
    unit = hidden_width // shard_count // ctx_count
    own_width = own_heads * HEAD_DIM
    head_turns = ctx_count // shard_heads
    low_first = list(bits_of("fsdp"))
    high_first = low_first[::-1]

    def pick(value, axis):
        return lax.dynamic_index_in_dim(value, ctx_index, axis, keepdims=False)

    half_width = model_width // 2
    pairs = own_heads // 2

    def section_order(slot):
        pair, rest = slot // 6, slot % 6
        return rest // 2 * own_heads + pair * 2 + rest % 2

    def by_ctx(value):
        return lax.all_gather(value, "ctx", axis=0, tiled=True)

    def as_row(value):
        return value.reshape(1, -1)

    token_count = ctx_count * own_rows
    units = shard_count * unit
    flops = 2 * token_count * model_width
    shard_rows = model_width // shard_count
    both = (low_first, high_first)
    qkv_order = [section_order(slot) for slot in range(3 * own_heads)]
    turn_index, head_slot = ctx_index // shard_heads, ctx_index % shard_heads
    where = jnp.stack([shard_index, ctx_index % 2]).astype(jnp.int32)

    all_tokens = by_ctx(own_tokens)
    own_inner = pick_columns(
        [up_weight, qkv_weight],
        [unit, HEAD_DIM],
        [list(range(shard_count)), qkv_order],
        ctx_index,
        ctx_count,
    )
    vectors = (norm_gain, norm_bias, qkv_bias, out_bias, up_bias, down_bias)
    inner_flow = Flow(gather_steps(own_inner, *both))
    vector_flow = Flow(direct_steps(jnp.concatenate(vectors).reshape(8, -1)))
    grad_first = by_ctx(after(own_grad[:, :half_width], own_inner))

    def prepare(down_weight, out_weight):
        own_down = pick(down_weight.reshape(ctx_count, unit, model_width), 0)
        own_out = lax.dynamic_index_in_dim(
            out_weight.reshape(shard_heads, HEAD_DIM, model_width), head_slot, 0, keepdims=False
        )
        return own_down, own_out

    def both_tables(ends, block_place):
        natural = jnp.arange(token_count, dtype=jnp.int32)
        given = (block_place[:, None] * BLK + jnp.arange(BLK, dtype=jnp.int32)).reshape(-1)
        return turn_tables(natural, ends), turn_tables(given, ends)

    ends = jnp.cumsum(seq_lengths[0]).astype(jnp.int32)
    own_down, own_out = beside(prepare, (down_weight, out_weight), [inner_flow, vector_flow])
    grad_second = by_ctx(after(own_grad[:, half_width:], own_down))
    natural_tables, given_tables = beside(both_tables, (ends, block_place), [inner_flow])
    while inner_flow.moves:
        own_down, own_out = beside(lambda *same: same, (own_down, own_out), [inner_flow])
    packed = jnp.stack([piece.reshape(-1) for _, _, piece in vector_flow.result])
    packed = jnp.concatenate(
        [lax.dynamic_index_in_dim(packed, shard_index ^ i, 0) for i in range(shard_count)]
    )
    cuts = [0]
    for vector in vectors:
        cuts.append(cuts[-1] + vector.shape[0])
    gain_all, shift_all, qkv_bias_all, out_bias_all, up_bias_all, down_bias_all = [
        packed[:, start:stop].reshape(-1).astype(F32) for start, stop in zip(cuts, cuts[1:])
    ]
    own_qkv_bias = pick(qkv_bias_all.reshape(3, pairs, 2, ctx_count, HEAD_DIM), 3)
    own_qkv_bias = jnp.transpose(own_qkv_bias, (1, 0, 2, 3)).reshape(-1)
    own_up_bias = pick(up_bias_all.reshape(shard_count, ctx_count, unit), 1).reshape(-1)
    inner_bias = jnp.concatenate([own_up_bias, own_qkv_bias])
    inner = (shard_rows, inner_flow.result)
    down_flow = Flow(direct_steps(own_down))
    out_flow = Flow(direct_steps(own_out))

    def enter(rows):
        return row_call(
            enter_kernel,
            where,
            [rows, *given_tables],
            [as_row(gain_all), as_row(shift_all), as_row(inner_bias)],
            [inner],
            [(model_width, BF16), (units, BF16), (units, BF16), (3 * own_width, BF16)],
            [],
            flops * (units + 3 * own_width),
        )

    normed, slope, active, linear = beside(enter, (all_tokens,), [down_flow])

    def down_terms(rows):
        return dot_tn(active, rows).astype(BF16).reshape(shard_count, unit, half_width)

    first_terms = down_terms(after(grad_first, active))
    first_flow = Flow(scatter_steps(first_terms, *both))
    attended, *kept = beside(
        lambda rows: attention_forward(block_place, ends, rows),
        (linear,),
        [first_flow, out_flow],
    )
    down = (unit, down_flow.result)
    out = (HEAD_DIM, out_flow.result)
    if head_turns > 1:
        out_all = jnp.stack([piece for _, _, piece in out_flow.result])
        out_all = jnp.concatenate(
            [
                lax.dynamic_index_in_dim(
                    out_all, shard_index ^ (i * head_turns + turn_index), 0, keepdims=False
                )
                for i in range(own_heads)
            ]
        )
        out = (own_width, [(None, 0, out_all)])
    second_terms = beside(down_terms, (after(grad_second, attended),), [first_flow])
    while first_flow.moves:
        second_terms = beside(lambda same: same, (second_terms,), [first_flow])
    second_flow = Flow(scatter_steps(second_terms, *both))

    def leave(rows):
        return row_call(
            leave_kernel,
            where,
            [rows, active],
            [],
            [down, out],
            [(model_width, BF16)],
            [],
            flops * (units + own_width),
            split=True,
        )

    def back(rows):
        return row_call(
            back_kernel,
            where,
            [grad_first, rows, slope],
            [],
            [down, out],
            [(units, BF16), (own_width, BF16)],
            [(1, units)],
            flops * (units + own_width),
        )

    grad_hidden, grad_att, hidden_sum = beside(
        back, (after(grad_second, first_flow.result),), [second_flow]
    )
    up_terms = beside(
        lambda rows: dot_tn(normed, rows).astype(BF16), (grad_hidden,), [second_flow]
    )
    while second_flow.moves:
        up_terms = beside(lambda same: same, (up_terms,), [second_flow])
    up_flow = Flow(scatter_steps(up_terms.reshape(shard_count, shard_rows, units), *both, fold=1))
    out_halves = beside(leave, (after(attended, second_flow.result),), [up_flow])
    core_flow = Flow(swap_steps(out_halves[1], out_halves[0]))
    held = []
    down_total = tuple(by_ctx(flow.result) for flow in (first_flow, second_flow))
    grad_mixed, weave = (), None
    for pair in range(pairs):

        def backward(rows, *halves):
            if halves:
                held.append(add_pair(*halves))
            result = attention_backward(
                pair, block_place, ends, natural_tables, kept, rows, grad_mixed
            )
            return [result, *held]

        rows = after(grad_att, *out_halves, down_total[min(pair, 1)])
        halves = core_flow.result if weave else ()
        flows = [weave] if weave else [flow for flow in (up_flow, core_flow) if flow.moves]
        grad_mixed = (beside(backward, (rows, *halves), flows)[0],)
        while up_flow.moves and pair + 1 == pairs:
            out_halves = beside(lambda *same: same, tuple(out_halves), [up_flow])
        if not up_flow.moves and weave is None:
            weave = Flow(weave_steps(up_flow.result, held, out_halves[0].shape))
    if not held:
        held.append(add_pair(*core_flow.result))
    (grad_mixed,) = grad_mixed

    def joint(rows):
        late = after(attended, rows)
        out_terms = [dot_tn(late, piece).astype(BF16) for piece in (grad_first, grad_second)]
        return join_terms(
            dot_tn(normed, rows).astype(BF16), out_terms, shard_count, head_turns, turn_index
        )

    joint_terms = beside(joint, (grad_mixed,), [weave])
    joint_flow = Flow(
        scatter_steps(joint_terms.reshape(shard_count, shard_rows, -1), *both, fold=1)
    )

    def norm_back(rows):
        return row_call(
            norm_back_kernel,
            where,
            [all_tokens, rows, grad_hidden],
            [],
            [inner],
            [(model_width, BF16)],
            [(1, model_width), (1, model_width), (1, 3 * own_width)],
            flops * (units + 3 * own_width),
            split=True,
        )

    mine, other, gain_sum, shift_sum, mixed_sum = beside(
        norm_back, (after(grad_mixed, joint_terms),), [weave, joint_flow]
    )

    def spread(value, count):
        value = value.reshape(count, 1, -1)
        whole = jnp.zeros((count, ctx_count, value.shape[2]), F32)
        return lax.dynamic_update_slice_in_dim(whole, value, ctx_index, 1).reshape(-1)

    grad_float = own_grad.astype(F32)
    mixed_sum = jnp.transpose(mixed_sum.reshape(pairs, 3, 2 * HEAD_DIM), (1, 0, 2))
    sums = (
        gain_sum.reshape(-1),
        shift_sum.reshape(-1),
        spread(mixed_sum, 3 * own_heads),
        jnp.sum(grad_float, axis=0),
        spread(hidden_sum, shard_count),
    )
    total_flow = Flow(total_steps(jnp.concatenate(sums)))
    at = jnp.stack([shard_index % head_turns, ctx_index % 2]).astype(jnp.int32)

    def nothing():
        return ()

    while weave.moves:
        beside(nothing, (), [weave])
    up_blocks, out_finish = weave.result
    core_flow = Flow(swap_steps(other, mine))
    down_total = beside(side_by_side, down_total, [joint_flow, core_flow], late=[out_finish])
    while joint_flow.moves:
        beside(nothing, (), [joint_flow])
    held = []
    weave = Flow(weave_steps(joint_flow.result, held, mine.shape))

    def order_and_add(blocks, halves):
        held.append(add_pair(*halves))
        return in_order(*blocks), held[0]

    up_blocks, _ = beside(
        order_and_add, (up_blocks, core_flow.result), [weave, total_flow], early=[out_finish]
    )
    up_swap = Flow(swap_steps(up_blocks))
    beside(nothing, (), [flow for flow in (weave, total_flow, up_swap) if flow.moves])
    (up_dealt,) = beside(
        lambda *halves: deal_columns(*halves, unit, list(range(shard_count)), at),
        up_swap.result,
        [flow for flow in (weave, total_flow) if flow.moves],
    )
    while weave.moves:
        beside(nothing, (), [flow for flow in (weave, total_flow) if flow.moves])
    joint_blocks, norm_finish = weave.result
    joint_blocks = beside(
        in_order, joint_blocks, [flow for flow in (total_flow,) if flow.moves], late=[norm_finish]
    )
    joint_swap = Flow(swap_steps(joint_blocks))
    beside(nothing, (), [flow for flow in (joint_swap, total_flow) if flow.moves])
    qkv_dealt, out_dealt = beside(
        lambda *halves: deal_columns(*halves, HEAD_DIM, qkv_order, at, with_out=True),
        joint_swap.result,
        [flow for flow in (total_flow,) if flow.moves],
        early=[norm_finish],
    )
    out_sum, grad_normed = out_finish.result, norm_finish.result

    inputs = own_tokens.astype(F32)
    output = (inputs + out_sum + (out_bias_all + down_bias_all)).astype(BF16)

    scaled, inv_std = standard(own_tokens)
    grad_scaled = grad_normed * gain_all
    grad_input = inv_std * (
        grad_scaled
        - jnp.mean(grad_scaled, axis=1, keepdims=True)
        - scaled * jnp.mean(grad_scaled * scaled, axis=1, keepdims=True)
    )
    input_grad = (grad_float + grad_input).astype(BF16)

    while total_flow.moves:
        beside(nothing, (), [total_flow])
    total = total_flow.result
    own_sums, start = [], 0
    for item in sums:
        size = item.shape[0] // shard_count
        own_sums.append(lax.dynamic_slice_in_dim(total, start + shard_index * size, size))
        start += item.shape[0]
    gain_total, shift_total, qkv_bias_total, bias_total, up_bias_total = own_sums

    return (
        output[None],
        input_grad[None],
        gain_total,
        shift_total,
        qkv_dealt,
        qkv_bias_total,
        out_dealt,
        bias_total,
        up_dealt,
        up_bias_total,
        down_total,
        bias_total,
    )


def solution(mesh):
    in_specs = (
        P("fsdp", "ctx", None),
        P(),
        P("fsdp", None),
        P("fsdp"),
        P("fsdp"),
        P("fsdp", None),
        P("fsdp"),
        P("fsdp", None),
        P("fsdp"),
        P("fsdp", None),
        P("fsdp"),
        P("fsdp", None),
        P("fsdp"),
        P("fsdp", "ctx", None),
    )
    out_specs = (
        P("fsdp", "ctx", None),
        P("fsdp", "ctx", None),
        P("fsdp"),
        P("fsdp"),
        P("fsdp", None),
        P("fsdp"),
        P("fsdp", None),
        P("fsdp"),
        P("fsdp", None),
        P("fsdp"),
        P("fsdp", None),
        P("fsdp"),
    )
    return jax.shard_map(shards, mesh=mesh, in_specs=in_specs, out_specs=out_specs, check_vma=False)
```

```python
import functools

import jax
import jax.numpy as jnp
from jax import lax
from jax.experimental import pallas as pl
from jax.experimental.pallas import tpu as pltpu
from jax.sharding import PartitionSpec as P

HEAD_DIM = 64
ROT = 32
BLK = 16
TILE = 512
WIDE = 512
ROWS = 512
LANES = 128
F32 = jnp.float32
BF16 = jnp.bfloat16


def dot_nn(left, right):
    return lax.dot_general(left, right, (((1,), (0,)), ((), ())), preferred_element_type=F32)


def dot_nt(left, right):
    return lax.dot_general(left, right, (((1,), (1,)), ((), ())), preferred_element_type=F32)


def dot_tn(left, right):
    return lax.dot_general(left, right, (((0,), (0,)), ((), ())), preferred_element_type=F32)


def bits_of(axis):
    return range(lax.axis_size(axis).bit_length() - 1)


def swaps(axis, mask):
    return axis, [(i, i ^ mask) for i in range(lax.axis_size(axis))]


class Flow:
    def __init__(self, steps):
        self.steps = steps
        self.result = None
        self.moves = next(steps)

    def arrive(self, values):
        try:
            self.moves = self.steps.send(values)
        except StopIteration as stop:
            self.moves, self.result = [], stop.value


def beside(work, inputs, flows, late=(), early=()):
    starting = [*flows, *late]
    sends = [[value for value, _, _ in flow.moves] for flow in starting]
    inputs, sends = lax.optimization_barrier((inputs, sends))
    for flow, values in zip(starting, sends):
        flow.moving = [
            lax.ppermute(value, axis, pairs) for value, (_, axis, pairs) in zip(values, flow.moves)
        ]
    outputs = work(*inputs)
    ending = [*flows, *early]
    outputs, arrived = lax.optimization_barrier((outputs, [flow.moving for flow in ending]))
    for flow, values in zip(ending, arrived):
        flow.arrive(values)
    return outputs


def gather_steps(own, *orders):
    share = own.shape[0] // len(orders)
    held = [[(0, own[i * share : (i + 1) * share])] for i in range(len(orders))]
    for step in range(len(orders[0])):
        moves = [
            (piece, *swaps("fsdp", 1 << order[step]))
            for pieces, order in zip(held, orders)
            for _, piece in pieces
        ]
        arrived = iter((yield moves))
        for i, order in enumerate(orders):
            held[i] = held[i] + [(mask ^ (1 << order[step]), next(arrived)) for mask, _ in held[i]]
    return [
        (mask, i * share, piece) for i, pieces in enumerate(held) for mask, piece in pieces
    ]


def direct_steps(own):
    masks = range(1, lax.axis_size("fsdp"))
    arrived = yield [(own, *swaps("fsdp", mask)) for mask in masks]
    return [(0, 0, own)] + [(mask, 0, piece) for mask, piece in zip(masks, arrived)]


def scatter_steps(parts, *orders, fold=0):
    index = lax.axis_index("fsdp")
    bits = len(orders[0])
    share = parts.shape[1] // len(orders)
    held = [
        parts[:, i * share : (i + 1) * share].reshape((2,) * bits + (share, parts.shape[2]))
        for i in range(len(orders))
    ]
    left = [list(range(bits))[::-1] for _ in orders]
    for step in range(bits):
        moves, keeps = [], []
        for i, order in enumerate(orders):
            axis = left[i].index(order[step])
            left[i].pop(axis)
            mine = (index >> order[step]) & 1
            send = lax.dynamic_index_in_dim(held[i], 1 - mine, axis, keepdims=False)
            keeps.append(lax.dynamic_index_in_dim(held[i], mine, axis, keepdims=False))
            moves.append((send, *swaps("fsdp", 1 << order[step])))
        arrived = yield moves
        held = [
            (keep.astype(F32) + got.astype(F32)).astype(BF16) for keep, got in zip(keeps, arrived)
        ]
    return jnp.concatenate(held, axis=fold)


def swap_steps(value, kept=None):
    (got,) = yield [(value, *swaps("ctx", 1))]
    return value if kept is None else kept, got


def add_pair(mine, got):
    return (mine.astype(F32) + got.astype(F32)).astype(BF16)


def weave_steps(own, held, shape):
    count = lax.axis_size("ctx")
    line = count // 2
    place = lax.axis_index("ctx") // 2
    alike = own.shape == shape[1:]
    forth = [(i, i + 2) for i in range(count - 2)]
    back = [(i, i - 2) for i in range(2, count)]
    ups, downs = [], []
    up, down = yield [(own, "ctx", forth), (own, "ctx", back)]
    up_sum, down_sum = (up, down) if alike else (jnp.zeros(shape[1:], BF16),) * 2

    def block(target, added):
        target = jnp.clip(target, 0, line - 1)
        part = lax.dynamic_index_in_dim(held[0], target, 0, keepdims=False)
        return part.astype(F32) + added.astype(F32)

    for step in range(2, line + 1):
        ups.append(up)
        downs.append(down)
        far = line + 1 - step
        up_sum = block(place + far, up_sum).astype(BF16)
        down_sum = block(place - far, down_sum).astype(BF16)
        if step == line:
            break
        if alike:
            up_sum = jnp.where(place >= step - 1, up, up_sum)
            down_sum = jnp.where(place <= line - step, down, down_sum)
            up_sum, down_sum = yield [(up_sum, "ctx", forth), (down_sum, "ctx", back)]
            up, down = up_sum, down_sum
        else:
            up, down, up_sum, down_sum = yield [
                (up, "ctx", [(i, j) for i, j in forth if i // 2 >= step - 1]),
                (down, "ctx", [(i, j) for i, j in back if i // 2 <= line - step]),
                (up_sum, "ctx", [(i, j) for i, j in forth if i // 2 < step - 1]),
                (down_sum, "ctx", [(i, j) for i, j in back if i // 2 > line - step]),
            ]

    def finish():
        last_up, last_down = yield [(up_sum, "ctx", forth), (down_sum, "ctx", back)]
        return block(place, last_up) + last_down.astype(F32)

    return (own, ups, downs), Flow(finish())


def in_order(own, ups, downs):
    place = lax.axis_index("ctx") // 2
    blocks = []
    for chip in range(len(ups) + 1):
        value = own
        for away, (up, down) in enumerate(zip(ups, downs), 1):
            value = jnp.where(place == chip + away, up, value)
            value = jnp.where(place == chip - away, down, value)
        blocks.append(value)
    return jnp.stack(blocks)


def total_steps(vector):
    for axis in ("ctx", "fsdp"):
        for bit in bits_of(axis):
            (got,) = yield [(vector, *swaps(axis, 1 << bit))]
            vector = vector + got
    return vector


def turn(values, cosine, sine):
    lane = lax.broadcasted_iota(jnp.int32, values.shape, 1) % HEAD_DIM
    half = ROT // 2
    partner = jnp.where(
        lane < half, pltpu.roll(values, LANES - half, 1), pltpu.roll(values, half, 1)
    )
    return values * cosine + partner * sine


def first_half(shape):
    return lax.broadcasted_iota(jnp.int32, shape, 1) < HEAD_DIM


def visible_range(ends_ref, step, wide, tile):
    top = step * wide
    column = top + lax.broadcasted_iota(jnp.int32, (1, wide), 1)
    begin = jnp.zeros((1, wide), jnp.int32)
    first = jnp.int32(0)
    for sequence in range(ends_ref.shape[0]):
        end = ends_ref[sequence]
        begin = jnp.where(column >= end, jnp.maximum(begin, end), begin)
        first = jnp.where(top >= end, jnp.maximum(first, end), first)
    return column, begin, first // tile


def each_head(values, axis=1):
    half = lax.broadcasted_iota(jnp.int32, values.shape, axis) < HEAD_DIM
    zero = jnp.zeros_like(values)
    return [jnp.where(half, values, zero), jnp.where(half, zero, values)]


Q_LANES, K_LANES, V_LANES = (slice(i * LANES, (i + 1) * LANES) for i in range(3))
HEAD_ROWS = (slice(0, HEAD_DIM), slice(HEAD_DIM, LANES))


def each_block(place_ref, act):
    @pl.loop(0, place_ref.shape[0])
    def _(block):
        act(
            pl.ds(pl.multiple_of(block * BLK, BLK), BLK),
            pl.ds(pl.multiple_of(place_ref[block] * BLK, BLK), BLK),
        )


def part_lanes(pair, which):
    start = (3 * pair + which) * LANES
    return slice(start, start + LANES)


def forward_kernel(
    place_ref, ends_ref, lin_hbm, att_hbm, rows, summed_ref, lse_ref, values_t, att, sems
):
    tokens = rows.shape[0]
    tile, wide = TILE, WIDE
    pairs = rows.shape[1] // LANES // 3
    heads = 2 * pairs
    each_block(
        place_ref,
        lambda given, natural: pltpu.make_async_copy(
            lin_hbm.at[given], rows.at[natural], sems.at[0]
        ).start(),
    )
    pltpu.make_async_copy(lin_hbm, rows, sems.at[0]).wait()

    @pl.loop(0, tokens // tile)
    def _(step):
        part = pl.ds(pl.multiple_of(step * tile, tile), tile)
        for pair in range(pairs):
            lanes = slice(pair * LANES, (pair + 1) * LANES)
            values_t[lanes, part] = rows[part, part_lanes(pair, 2)].T

    @pl.loop(0, tokens // wide)
    def _(step):
        part = pl.ds(pl.multiple_of(step * wide, wide), wide)
        column, begin, low = visible_range(ends_ref, step, wide, tile)
        queries = [
            query
            for pair in range(pairs)
            for query in each_head(rows[part, part_lanes(pair, 0)].T, 0)
        ]

        def combine(index, state):
            there = pl.ds(pl.multiple_of(index * tile, tile), tile)
            row = index * tile + lax.broadcasted_iota(jnp.int32, (tile, wide), 0)
            visible = (row <= column) & (row >= begin)
            result = []
            for head in range(heads):
                top, total, summed = state[head]
                key = rows[there, part_lanes(head // 2, 1)]
                scores = jnp.where(visible, dot_nn(key, queries[head]), -1e30)
                new_top = jnp.maximum(top, jnp.max(scores, axis=0, keepdims=True))
                weight = jnp.exp(scores - new_top)
                factor = jnp.exp(top - new_top)
                total = total * factor + jnp.sum(weight, axis=0, keepdims=True)
                here = slice(head * HEAD_DIM, (head + 1) * HEAD_DIM)
                summed = summed * factor + dot_nn(values_t[here, there], weight.astype(BF16))
                result.append((new_top, total, summed))
            return tuple(result)

        empty = (
            jnp.full((1, wide), -1e30, F32),
            jnp.zeros((1, wide), F32),
            jnp.zeros((HEAD_DIM, wide), F32),
        )
        state = lax.fori_loop(low, (step + 1) * (wide // tile), combine, (empty,) * heads)
        for head in range(heads):
            top, total, summed = state[head]
            summed_ref[head * HEAD_DIM : (head + 1) * HEAD_DIM, part] = summed * (1.0 / total)
            lse_ref[head : head + 1, part] = top + jnp.log(total)
        for pair in range(pairs):
            lanes = slice(pair * LANES, (pair + 1) * LANES)
            att[part, lanes] = summed_ref[lanes, part].T.astype(BF16)

    each_block(
        place_ref,
        lambda given, natural: pltpu.make_async_copy(
            att.at[natural], att_hbm.at[given], sems.at[0]
        ).start(),
    )
    pltpu.make_async_copy(att, att_hbm, sems.at[0]).wait()


def backward_kernel(
    pair, place_ref, ends_ref, cos_ref, sin_ref, rows, summed_ref, lse_ref, grad_hbm, *refs
):
    mixed_hbm, grad, grad_t, keys_t, grad_k, grad_v, mixed, sems = refs[-8:]
    tokens = grad.shape[0]
    tile, wide = TILE, WIDE
    lanes = slice(pair * LANES, (pair + 1) * LANES)
    lanes3 = slice(3 * pair * LANES, 3 * (pair + 1) * LANES)
    each_block(
        place_ref,
        lambda given, natural: pltpu.make_async_copy(
            grad_hbm.at[given, lanes], grad.at[natural], sems.at[0]
        ).start(),
    )
    grad_k[...] = jnp.zeros_like(grad_k)
    grad_v[...] = jnp.zeros_like(grad_v)

    @pl.loop(0, tokens // tile)
    def _(step):
        part = pl.ds(pl.multiple_of(step * tile, tile), tile)
        keys_t[:, part] = rows[part, K_LANES].T

    pltpu.make_async_copy(grad_hbm.at[:, lanes], grad, sems.at[0]).wait()

    @pl.loop(0, tokens // wide)
    def _(step):
        part = pl.ds(pl.multiple_of(step * wide, wide), wide)
        column, begin, low = visible_range(ends_ref, step, wide, tile)
        query, back = rows[part, Q_LANES], grad[part, :]
        back_t = back.T
        queries, queries_t = each_head(query), each_head(query.T, 0)
        backs, backs_t = each_head(back), each_head(back_t, 0)
        grad_t[...] = back_t.astype(F32)
        delta = [
            jnp.sum(summed_ref[here, part] * grad_t[here, :], axis=0, keepdims=True)
            for here in HEAD_ROWS
        ]
        lse = [lse_ref[2 * pair + head : 2 * pair + head + 1, part] for head in range(2)]

        def back_step(index, sums):
            there = pl.ds(pl.multiple_of(index * tile, tile), tile)
            row = index * tile + lax.broadcasted_iota(jnp.int32, (tile, wide), 0)
            visible = (row <= column) & (row >= begin)
            key, value = rows[there, K_LANES], rows[there, V_LANES]
            result, add_k, add_v = [], 0.0, 0.0
            for head in range(2):
                scores = jnp.where(visible, dot_nn(key, queries_t[head]), -1e30)
                weight = jnp.exp(scores - lse[head])
                grad_w = dot_nn(value, backs_t[head])
                grad_s = (weight * (grad_w - delta[head])).astype(BF16)
                add_k = add_k + dot_nn(grad_s, queries[head])
                add_v = add_v + dot_nn(weight.astype(BF16), backs[head])
                result.append(sums[head] + dot_nn(keys_t[HEAD_ROWS[head], there], grad_s))
            grad_k[there, :] += add_k
            grad_v[there, :] += add_v
            return tuple(result)

        sums = lax.fori_loop(low, (step + 1) * (wide // tile), back_step, (jnp.zeros((HEAD_DIM, wide), F32),) * 2)
        grad_q = jnp.concatenate(sums, axis=0).T * HEAD_DIM ** (-0.5)
        mixed[part, Q_LANES] = turn(grad_q, cos_ref[part, :], -sin_ref[part, :]).astype(BF16)

    @pl.loop(0, tokens // tile)
    def _(step):
        part = pl.ds(pl.multiple_of(step * tile, tile), tile)
        turned = turn(grad_k[part, :], cos_ref[part, :], -sin_ref[part, :])
        mixed[part, K_LANES] = turned.astype(BF16)
        mixed[part, V_LANES] = grad_v[part, :].astype(BF16)

    each_block(
        place_ref,
        lambda given, natural: pltpu.make_async_copy(
            mixed.at[natural], mixed_hbm.at[given, lanes3], sems.at[0]
        ).start(),
    )
    pltpu.make_async_copy(mixed, mixed_hbm.at[:, lanes3], sems.at[0]).wait()


def turn_tables(position, ends):
    begin = jnp.max(jnp.where(position[:, None] >= ends[None, :], ends[None, :], 0), axis=1)
    within = (position - begin).astype(F32)
    half = ROT // 2
    lane = jnp.arange(LANES, dtype=jnp.int32) % HEAD_DIM
    frequency = 10000.0 ** (-(lane % half).astype(F32) * 2.0 / ROT)
    angles = within[:, None] * jnp.where(lane < ROT, frequency, 0.0)[None, :]
    return jnp.cos(angles), jnp.sin(angles) * jnp.where(lane < half, -1.0, 1.0)[None, :]


SMEM = pl.BlockSpec(memory_space=pltpu.SMEM)
VMEM = pl.BlockSpec(memory_space=pltpu.VMEM)
ANYWHERE = pl.BlockSpec(memory_space=pl.ANY)


def attention_forward(block_place, ends, linear):
    tokens, width3 = linear.shape
    width = width3 // 3
    return pl.pallas_call(
        forward_kernel,
        out_shape=(
            jax.ShapeDtypeStruct((tokens, width), BF16),
            jax.ShapeDtypeStruct((tokens, width3), BF16),
            jax.ShapeDtypeStruct((width, tokens), F32),
            jax.ShapeDtypeStruct((width // HEAD_DIM, tokens), F32),
        ),
        in_specs=[SMEM, SMEM, ANYWHERE],
        out_specs=(ANYWHERE, VMEM, VMEM, VMEM),
        scratch_shapes=[
            pltpu.VMEM((width, tokens), BF16),
            pltpu.VMEM((tokens, width), BF16),
            pltpu.SemaphoreType.DMA((1,)),
        ],
        compiler_params=pltpu.CompilerParams(vmem_limit_bytes=60 << 20),
        cost_estimate=pl.CostEstimate(
            flops=40 * 10**9, bytes_accessed=16 * 10**6, transcendentals=0
        ),
    )(block_place, ends, linear)


def attention_backward(pair, block_place, ends, tables, kept, grad_att, before):
    tokens, width = grad_att.shape
    return pl.pallas_call(
        functools.partial(backward_kernel, pair),
        out_shape=jax.ShapeDtypeStruct((tokens, 3 * width), BF16),
        grid=(1,),
        in_specs=[
            SMEM,
            SMEM,
            VMEM,
            VMEM,
            pl.BlockSpec((tokens, 3 * LANES), lambda i: (0, pair)),
            pl.BlockSpec((LANES, tokens), lambda i: (pair, 0)),
            VMEM,
        ]
        + [ANYWHERE] * (1 + len(before)),
        out_specs=ANYWHERE,
        input_output_aliases={8 + i: i for i in range(len(before))},
        scratch_shapes=[
            pltpu.VMEM((tokens, LANES), BF16),
            pltpu.VMEM((LANES, WIDE), F32),
            pltpu.VMEM((LANES, tokens), BF16),
            pltpu.VMEM((tokens, LANES), F32),
            pltpu.VMEM((tokens, LANES), F32),
            pltpu.VMEM((tokens, 3 * LANES), BF16),
            pltpu.SemaphoreType.DMA((1,)),
        ],
        compiler_params=pltpu.CompilerParams(vmem_limit_bytes=60 << 20),
        cost_estimate=pl.CostEstimate(
            flops=20 * 10**9, bytes_accessed=8 * 10**6, transcendentals=0
        ),
    )(block_place, ends, *tables, *kept, grad_att, *before)


def row_call(kernel, where, rows, whole, assembled, outs, sums, flops, split=False):
    count = rows[0].shape[0]
    tiles = count // ROWS
    shards = lax.axis_size("fsdp")
    pieces = [piece for _, group in assembled for _, _, piece in group]
    height = sum(sum(piece.shape[0] for _, _, piece in group) for _, group in assembled)

    def body(at, *refs):
        inputs = refs[: len(rows) + len(whole)]
        sources = refs[len(inputs) : len(inputs) + len(pieces)]
        targets = refs[len(inputs) + len(pieces) : -2]
        buffer, sems = refs[-2:]

        @pl.when(pl.program_id(0) == 0)
        def _():
            copies, base = [], 0
            for shard_height, group in assembled:
                for mask, start, piece in group:
                    first = start if mask is None else (at[0] ^ mask) * shard_height + start
                    size = piece.shape[0]
                    target = buffer.at[pl.ds(pl.multiple_of(base + first, size), size)]
                    slot = len(copies)
                    copies.append(pltpu.make_async_copy(sources[slot], target, sems.at[slot]))
                base += sum(piece.shape[0] for _, _, piece in group)
            for copy in copies:
                copy.start()
            for copy in copies:
                copy.wait()

        if split:
            mine, other, *rest = targets

            def put(part, value):
                even = at[1] == 0
                half = value.shape[0] // 2
                first, second = value[:half], value[half:]
                mine[0, :, part] = jnp.where(even, first, second)
                other[0, :, part] = jnp.where(even, second, first)

            kernel(*inputs, buffer, put, *rest)
        else:
            kernel(*inputs, buffer, *targets)

    by_tile = lambda columns: pl.BlockSpec((ROWS, columns), lambda i, at: (i, 0))
    stay = lambda shape: pl.BlockSpec(shape, lambda i, at: (0, 0))
    moved = sum(item.size * item.dtype.itemsize for item in (*rows, *whole, *pieces))
    moved += sum(count * columns * jnp.dtype(kind).itemsize for columns, kind in outs)
    if split:
        ((columns, kind),) = outs
        out_shape = [jax.ShapeDtypeStruct((tiles, ROWS // 2, columns), kind)] * 2
        out_specs = [pl.BlockSpec((1, ROWS // 2, columns), lambda i, at: (i, 0, 0))] * 2
    else:
        out_shape = [jax.ShapeDtypeStruct((count, columns), kind) for columns, kind in outs]
        out_specs = [by_tile(columns) for columns, _ in outs]
    return pl.pallas_call(
        body,
        out_shape=out_shape + [jax.ShapeDtypeStruct(shape, F32) for shape in sums],
        grid_spec=pltpu.PrefetchScalarGridSpec(
            num_scalar_prefetch=1,
            grid=(tiles,),
            in_specs=[by_tile(item.shape[1]) for item in rows]
            + [stay(item.shape) for item in whole]
            + [ANYWHERE] * len(pieces),
            out_specs=out_specs + [stay(shape) for shape in sums],
            scratch_shapes=[
                pltpu.VMEM((height, pieces[0].shape[1]), BF16),
                pltpu.SemaphoreType.DMA((len(pieces),)),
            ],
        ),
        compiler_params=pltpu.CompilerParams(vmem_limit_bytes=60 << 20),
        cost_estimate=pl.CostEstimate(flops=flops, bytes_accessed=moved, transcendentals=0),
    )(where, *rows, *whole, *pieces)


def chunks_of(columns, size=256):
    return [slice(start, min(start + size, columns)) for start in range(0, columns, size)]


def standard(rows):
    values = rows.astype(F32)
    centred = values - jnp.mean(values, axis=1, keepdims=True)
    inv_std = lax.rsqrt(jnp.mean(centred * centred, axis=1, keepdims=True) + 1e-05)
    return centred * inv_std, inv_std


def enter_kernel(
    tokens, cosine, sine, gain, shift, bias, inner, normed_out, slope_out, active_out, linear_out
):
    for start in range(0, tokens.shape[0], 32):
        part = slice(start, start + 32)
        scaled, _ = standard(tokens[part, :])
        normed_out[part, :] = (scaled * gain[...] + shift[...]).astype(BF16)
    normed = normed_out[...]
    units = active_out.shape[1]
    for part in chunks_of(units):
        hidden = dot_nn(normed, inner[:, part]) + bias[:, part]
        square = hidden * hidden
        gate = 1.0 / (1.0 + jnp.exp(hidden * (-1.5957691216057308 - 0.07135481627260025 * square)))
        value = hidden * gate
        active_out[:, part] = value.astype(BF16)
        inner_slope = 1.5957691216057308 + 0.21406444881780073 * square
        slope_out[:, part] = (gate + (value - value * gate) * inner_slope).astype(BF16)
    for part in chunks_of(linear_out.shape[1], 3 * LANES):
        there = slice(units + part.start, units + part.stop)
        value = dot_nn(normed, inner[:, there]) + bias[:, there]
        query = turn(value[:, Q_LANES], cosine[...], sine[...]) * HEAD_DIM ** (-0.5)
        key = turn(value[:, K_LANES], cosine[...], sine[...])
        joined = jnp.concatenate([query, key, value[:, V_LANES]], axis=1)
        linear_out[:, part] = joined.astype(BF16)


def back_kernel(first, second, slope, weights, hidden_out, att_out, hidden_sum):
    @pl.when(pl.program_id(0) == 0)
    def _():
        hidden_sum[...] = jnp.zeros_like(hidden_sum)

    rows = jnp.concatenate([first[...], second[...]], axis=1)
    units = slope.shape[1]
    for part in chunks_of(units):
        grad = (dot_nt(rows, weights[part, :]) * slope[:, part]).astype(BF16)
        hidden_out[:, part] = grad
        hidden_sum[:, part] += jnp.sum(grad.astype(F32), axis=0, keepdims=True)
    for part in chunks_of(att_out.shape[1]):
        there = slice(units + part.start, units + part.stop)
        att_out[:, part] = dot_nt(rows, weights[there, :]).astype(BF16)


def leave_kernel(attended, active, weights, put):
    rows = jnp.concatenate([active[...], attended[...]], axis=1)
    for part in chunks_of(weights.shape[1], 512):
        put(part, dot_nn(rows, weights[:, part]).astype(BF16))


def norm_back_kernel(tokens, mixed, hidden, inner, put, gain_sum, shift_sum, mixed_sum):
    @pl.when(pl.program_id(0) == 0)
    def _():
        for total in (gain_sum, shift_sum, mixed_sum):
            total[...] = jnp.zeros_like(total)

    scaled, _ = standard(tokens[...])
    mixed_sum[...] += jnp.sum(mixed[...].astype(F32), axis=0, keepdims=True)
    rows = jnp.concatenate([hidden[...], mixed[...]], axis=1)
    for part in chunks_of(inner.shape[0], 512):
        grad = dot_nt(rows, inner[part, :])
        put(part, grad.astype(BF16))
        shift_sum[:, part] += jnp.sum(grad, axis=0, keepdims=True)
        gain_sum[:, part] += jnp.sum(grad * scaled[:, part], axis=0, keepdims=True)


def pick_kernel(plans, index_ref, *refs):
    *weights, target, tiles, sems = refs
    at = index_ref[0]
    count = plans[0][2]
    copies, late, slot, column = [], [], 0, 0
    for weight, (unit, order, _) in zip(weights, plans):
        if unit % LANES == 0:
            for place in order:
                first = pl.multiple_of((place * count + at) * unit, unit)
                copies.append(
                    (weight.at[:, pl.ds(first, unit)], target.at[:, column : column + unit])
                )
                column += unit
            continue
        for one, two in zip(order[::2], order[1::2]):
            for which, place in enumerate((one, two)):
                first = pl.multiple_of((place * count + at) // 2 * LANES, LANES)
                copies.append((weight.at[:, pl.ds(first, LANES)], tiles.at[slot, which]))
            late.append((slot, column))
            slot, column = slot + 1, column + LANES
    copies = [
        pltpu.make_async_copy(source, there, sems.at[i])
        for i, (source, there) in enumerate(copies)
    ]
    for copy in copies:
        copy.start()
    for copy in copies:
        copy.wait()
    for slot, column in late:
        first, second = tiles[slot, 0].astype(F32), tiles[slot, 1].astype(F32)
        odd = at % 2 == 1
        first = jnp.where(odd, pltpu.roll(first, HEAD_DIM, 1), first)
        second = jnp.where(odd, second, pltpu.roll(second, HEAD_DIM, 1))
        target[:, column : column + LANES] = jnp.where(
            first_half(first.shape), first, second
        ).astype(target.dtype)


def pick_columns(weights, units, orders, index, count):
    rows = weights[0].shape[0]
    width = sum(unit * len(order) for unit, order in zip(units, orders))
    narrow = [len(order) // 2 for unit, order in zip(units, orders) if unit % LANES]
    copies = sum(len(order) for order in orders)
    return pl.pallas_call(
        functools.partial(pick_kernel, [(unit, order, count) for unit, order in zip(units, orders)]),
        out_shape=jax.ShapeDtypeStruct((rows, width), weights[0].dtype),
        in_specs=[SMEM] + [ANYWHERE] * len(weights),
        out_specs=VMEM,
        scratch_shapes=[
            pltpu.VMEM((sum(narrow), 2, rows, LANES), weights[0].dtype),
            pltpu.SemaphoreType.DMA((copies,)),
        ],
        compiler_params=pltpu.CompilerParams(vmem_limit_bytes=32 << 20),
        cost_estimate=pl.CostEstimate(
            flops=0, bytes_accessed=4 * rows * width, transcendentals=0
        ),
    )(index.reshape(1), *weights)


def deal_kernel(unit, order, at_ref, mine, other, target, *rest):
    line = mine.shape[0]
    count = 2 * line
    even = at_ref[1] == 0

    def both_cores(chip, tile):
        one, two = mine[chip, :, tile], other[chip, :, tile]
        return jnp.where(even, one, two).astype(F32), jnp.where(even, two, one).astype(F32)

    for chip in range(line):
        for group, place in enumerate(order):
            start = (place * count + 2 * chip) * unit
            if unit % LANES == 0:
                values = both_cores(chip, slice(group * unit, (group + 1) * unit))
                for core, value in enumerate(values):
                    target[:, start + core * unit : start + (core + 1) * unit] = value
                continue
            first, second = both_cores(chip, slice(group // 2 * LANES, (group // 2 + 1) * LANES))
            if group % 2:
                first = pltpu.roll(first, HEAD_DIM, 1)
            else:
                second = pltpu.roll(second, HEAD_DIM, 1)
            target[:, start : start + LANES] = jnp.where(first_half(first.shape), first, second)
    for out in rest:
        chips = out.shape[0] // HEAD_DIM // 2
        tail = slice(len(order) * unit, mine.shape[2])
        for chip in range(chips):
            source = chip if chips == line else at_ref[0] * chips + chip
            for core, value in enumerate(both_cores(source, tail)):
                row = (2 * chip + core) * HEAD_DIM
                out[row : row + HEAD_DIM, :] = value


def deal_columns(mine, other, unit, order, where, with_out=False):
    line, rows, columns = mine.shape
    rows, columns = 2 * rows, columns // 2
    width = len(order) * unit
    step = HEAD_DIM
    steps = rows // step
    out_shape = [jax.ShapeDtypeStruct((rows, 2 * line * width), F32)]
    out_specs = [pl.BlockSpec((step, 2 * line * width), lambda i, at: (i, 0))]
    if with_out:
        out_shape.append(jax.ShapeDtypeStruct((rows, (columns - width) * (rows // step)), F32))
        out_specs.append(pl.BlockSpec((rows, columns - width), lambda i, at: (0, i)))
    return pl.pallas_call(
        functools.partial(deal_kernel, unit, order),
        out_shape=out_shape,
        grid_spec=pltpu.PrefetchScalarGridSpec(
            num_scalar_prefetch=1,
            grid=(rows // step,),
            in_specs=[
                pl.BlockSpec(
                    (line, step, columns),
                    lambda i, at: (0, i % (steps // 2), i // (steps // 2)),
                )
            ]
            * 2,
            out_specs=out_specs,
        ),
        compiler_params=pltpu.CompilerParams(vmem_limit_bytes=32 << 20),
        cost_estimate=pl.CostEstimate(
            flops=0, bytes_accessed=12 * rows * line * columns, transcendentals=0
        ),
    )(where, mine, other)


def join_kernel(turns, turn_ref, left, *refs):
    *pieces, target = refs
    width = left.shape[1]
    size = target.shape[1] - width
    target[:, :width] = left[...]
    keep = pl.program_id(0) % turns == turn_ref[0]
    for piece_index, piece in enumerate(pieces):
        for chunk in range(piece.shape[1] // size):
            value = piece[:, chunk * size : (chunk + 1) * size]
            if turns > 1:
                value = jnp.where(keep, value, jnp.zeros_like(value))
            row = (piece_index * (piece.shape[1] // size) + chunk) * HEAD_DIM
            target[row : row + HEAD_DIM, width:] = value


def join_terms(left, pieces, shards, turns, turn_index):
    rows = left.shape[0] // shards
    extra = sum(piece.shape[1] for piece in pieces) * HEAD_DIM // rows
    width = left.shape[1]
    return pl.pallas_call(
        functools.partial(join_kernel, turns),
        out_shape=jax.ShapeDtypeStruct((left.shape[0], width + extra), left.dtype),
        grid_spec=pltpu.PrefetchScalarGridSpec(
            num_scalar_prefetch=1,
            grid=(shards,),
            in_specs=[pl.BlockSpec((rows, width), lambda i, at: (i, 0))]
            + [
                pl.BlockSpec((HEAD_DIM, piece.shape[1]), lambda i, at: (i // turns, 0))
                for piece in pieces
            ],
            out_specs=pl.BlockSpec((rows, width + extra), lambda i, at: (i, 0)),
        ),
        cost_estimate=pl.CostEstimate(
            flops=0, bytes_accessed=4 * left.shape[0] * (width + extra), transcendentals=0
        ),
    )(turn_index.reshape(1), left, *pieces)


def side_kernel(*refs):
    *pieces, target = refs
    start = 0
    for piece in pieces:
        target[:, start : start + piece.shape[1]] = piece[...].astype(F32)
        start += piece.shape[1]


def side_by_side(*pieces):
    rows = pieces[0].shape[0]
    width = sum(piece.shape[1] for piece in pieces)
    return pl.pallas_call(
        side_kernel,
        out_shape=jax.ShapeDtypeStruct((rows, width), F32),
        grid=(rows // TILE,),
        in_specs=[pl.BlockSpec((TILE, piece.shape[1]), lambda i: (i, 0)) for piece in pieces],
        out_specs=pl.BlockSpec((TILE, width), lambda i: (i, 0)),
        cost_estimate=pl.CostEstimate(flops=0, bytes_accessed=6 * rows * width, transcendentals=0),
    )(*pieces)


def after(value, *others):
    return lax.optimization_barrier((value,) + others)[0]


def shards(
    tokens,
    block_place,
    seq_lengths,
    norm_gain,
    norm_bias,
    qkv_weight,
    qkv_bias,
    out_weight,
    out_bias,
    up_weight,
    up_bias,
    down_weight,
    down_bias,
    out_grad,
):
    ctx_count, ctx_index = lax.axis_size("ctx"), lax.axis_index("ctx")
    shard_count, shard_index = lax.axis_size("fsdp"), lax.axis_index("fsdp")
    own_tokens, own_grad = tokens[0], out_grad[0]
    own_rows, model_width = own_tokens.shape
    hidden_width = up_weight.shape[1]
    heads = model_width // HEAD_DIM
    own_heads = heads // ctx_count
    shard_heads = heads // shard_count
    unit = hidden_width // shard_count // ctx_count
    own_width = own_heads * HEAD_DIM
    head_turns = ctx_count // shard_heads
    low_first = list(bits_of("fsdp"))
    high_first = low_first[::-1]

    def pick(value, axis):
        return lax.dynamic_index_in_dim(value, ctx_index, axis, keepdims=False)

    half_width = model_width // 2
    pairs = own_heads // 2

    def section_order(slot):
        pair, rest = slot // 6, slot % 6
        return rest // 2 * own_heads + pair * 2 + rest % 2

    def by_ctx(value):
        return lax.all_gather(value, "ctx", axis=0, tiled=True)

    def as_row(value):
        return value.reshape(1, -1)

    token_count = ctx_count * own_rows
    units = shard_count * unit
    flops = 2 * token_count * model_width
    shard_rows = model_width // shard_count
    both = (low_first, high_first)
    qkv_order = [section_order(slot) for slot in range(3 * own_heads)]
    turn_index, head_slot = ctx_index // shard_heads, ctx_index % shard_heads
    where = jnp.stack([shard_index, ctx_index % 2]).astype(jnp.int32)

    all_tokens = by_ctx(own_tokens)
    own_inner = pick_columns(
        [up_weight, qkv_weight],
        [unit, HEAD_DIM],
        [list(range(shard_count)), qkv_order],
        ctx_index,
        ctx_count,
    )
    vectors = (norm_gain, norm_bias, qkv_bias, out_bias, up_bias, down_bias)
    inner_flow = Flow(gather_steps(own_inner, *both))
    vector_flow = Flow(direct_steps(jnp.concatenate(vectors).reshape(8, -1)))
    grad_first = by_ctx(after(own_grad[:, :half_width], own_inner))

    def prepare(down_weight, out_weight):
        own_down = pick(down_weight.reshape(ctx_count, unit, model_width), 0)
        own_out = lax.dynamic_index_in_dim(
            out_weight.reshape(shard_heads, HEAD_DIM, model_width), head_slot, 0, keepdims=False
        )
        return own_down, own_out

    def both_tables(ends, block_place):
        natural = jnp.arange(token_count, dtype=jnp.int32)
        given = (block_place[:, None] * BLK + jnp.arange(BLK, dtype=jnp.int32)).reshape(-1)
        return turn_tables(natural, ends), turn_tables(given, ends)

    ends = jnp.cumsum(seq_lengths[0]).astype(jnp.int32)
    own_down, own_out = beside(prepare, (down_weight, out_weight), [inner_flow, vector_flow])
    grad_second = by_ctx(after(own_grad[:, half_width:], own_down))
    natural_tables, given_tables = beside(both_tables, (ends, block_place), [inner_flow])
    while inner_flow.moves:
        own_down, own_out = beside(lambda *same: same, (own_down, own_out), [inner_flow])
    packed = jnp.stack([piece.reshape(-1) for _, _, piece in vector_flow.result])
    packed = jnp.concatenate(
        [lax.dynamic_index_in_dim(packed, shard_index ^ i, 0) for i in range(shard_count)]
    )
    cuts = [0]
    for vector in vectors:
        cuts.append(cuts[-1] + vector.shape[0])
    gain_all, shift_all, qkv_bias_all, out_bias_all, up_bias_all, down_bias_all = [
        packed[:, start:stop].reshape(-1).astype(F32) for start, stop in zip(cuts, cuts[1:])
    ]
    own_qkv_bias = pick(qkv_bias_all.reshape(3, pairs, 2, ctx_count, HEAD_DIM), 3)
    own_qkv_bias = jnp.transpose(own_qkv_bias, (1, 0, 2, 3)).reshape(-1)
    own_up_bias = pick(up_bias_all.reshape(shard_count, ctx_count, unit), 1).reshape(-1)
    inner_bias = jnp.concatenate([own_up_bias, own_qkv_bias])
    inner = (shard_rows, inner_flow.result)
    down_flow = Flow(direct_steps(own_down))
    out_flow = Flow(direct_steps(own_out))

    def enter(rows):
        return row_call(
            enter_kernel,
            where,
            [rows, *given_tables],
            [as_row(gain_all), as_row(shift_all), as_row(inner_bias)],
            [inner],
            [(model_width, BF16), (units, BF16), (units, BF16), (3 * own_width, BF16)],
            [],
            flops * (units + 3 * own_width),
        )

    normed, slope, active, linear = beside(enter, (all_tokens,), [down_flow])

    def down_terms(rows):
        return dot_tn(active, rows).astype(BF16).reshape(shard_count, unit, half_width)

    first_terms = down_terms(after(grad_first, active))
    first_flow = Flow(scatter_steps(first_terms, *both))
    attended, *kept = beside(
        lambda rows: attention_forward(block_place, ends, rows),
        (linear,),
        [first_flow, out_flow],
    )
    down = (unit, down_flow.result)
    out = (HEAD_DIM, out_flow.result)
    if head_turns > 1:
        out_all = jnp.stack([piece for _, _, piece in out_flow.result])
        out_all = jnp.concatenate(
            [
                lax.dynamic_index_in_dim(
                    out_all, shard_index ^ (i * head_turns + turn_index), 0, keepdims=False
                )
                for i in range(own_heads)
            ]
        )
        out = (own_width, [(None, 0, out_all)])
    second_terms = beside(down_terms, (after(grad_second, attended),), [first_flow])
    while first_flow.moves:
        second_terms = beside(lambda same: same, (second_terms,), [first_flow])
    second_flow = Flow(scatter_steps(second_terms, *both))

    def leave(rows):
        return row_call(
            leave_kernel,
            where,
            [rows, active],
            [],
            [down, out],
            [(model_width, BF16)],
            [],
            flops * (units + own_width),
            split=True,
        )

    def back(rows):
        return row_call(
            back_kernel,
            where,
            [grad_first, rows, slope],
            [],
            [down, out],
            [(units, BF16), (own_width, BF16)],
            [(1, units)],
            flops * (units + own_width),
        )

    grad_hidden, grad_att, hidden_sum = beside(
        back, (after(grad_second, first_flow.result),), [second_flow]
    )
    up_terms = beside(
        lambda rows: dot_tn(normed, rows).astype(BF16), (grad_hidden,), [second_flow]
    )
    while second_flow.moves:
        up_terms = beside(lambda same: same, (up_terms,), [second_flow])
    up_flow = Flow(scatter_steps(up_terms.reshape(shard_count, shard_rows, units), *both, fold=1))
    out_halves = beside(leave, (after(attended, second_flow.result),), [up_flow])
    core_flow = Flow(swap_steps(out_halves[1], out_halves[0]))
    held = []
    down_total = tuple(by_ctx(flow.result) for flow in (first_flow, second_flow))
    grad_mixed, weave = (), None
    for pair in range(pairs):

        def backward(rows, *halves):
            if halves:
                held.append(add_pair(*halves))
            result = attention_backward(
                pair, block_place, ends, natural_tables, kept, rows, grad_mixed
            )
            return [result, *held]

        rows = after(grad_att, *out_halves, down_total[min(pair, 1)])
        halves = core_flow.result if weave else ()
        flows = [weave] if weave else [flow for flow in (up_flow, core_flow) if flow.moves]
        grad_mixed = (beside(backward, (rows, *halves), flows)[0],)
        while up_flow.moves and pair + 1 == pairs:
            out_halves = beside(lambda *same: same, tuple(out_halves), [up_flow])
        if not up_flow.moves and weave is None:
            weave = Flow(weave_steps(up_flow.result, held, out_halves[0].shape))
    if not held:
        held.append(add_pair(*core_flow.result))
    (grad_mixed,) = grad_mixed

    def joint(rows):
        late = after(attended, rows)
        out_terms = [dot_tn(late, piece).astype(BF16) for piece in (grad_first, grad_second)]
        return join_terms(
            dot_tn(normed, rows).astype(BF16), out_terms, shard_count, head_turns, turn_index
        )

    joint_terms = beside(joint, (grad_mixed,), [weave])
    joint_flow = Flow(
        scatter_steps(joint_terms.reshape(shard_count, shard_rows, -1), *both, fold=1)
    )

    def norm_back(rows):
        return row_call(
            norm_back_kernel,
            where,
            [all_tokens, rows, grad_hidden],
            [],
            [inner],
            [(model_width, BF16)],
            [(1, model_width), (1, model_width), (1, 3 * own_width)],
            flops * (units + 3 * own_width),
            split=True,
        )

    mine, other, gain_sum, shift_sum, mixed_sum = beside(
        norm_back, (after(grad_mixed, joint_terms),), [weave, joint_flow]
    )

    def spread(value, count):
        value = value.reshape(count, 1, -1)
        whole = jnp.zeros((count, ctx_count, value.shape[2]), F32)
        return lax.dynamic_update_slice_in_dim(whole, value, ctx_index, 1).reshape(-1)

    grad_float = own_grad.astype(F32)
    mixed_sum = jnp.transpose(mixed_sum.reshape(pairs, 3, 2 * HEAD_DIM), (1, 0, 2))
    sums = (
        gain_sum.reshape(-1),
        shift_sum.reshape(-1),
        spread(mixed_sum, 3 * own_heads),
        jnp.sum(grad_float, axis=0),
        spread(hidden_sum, shard_count),
    )
    total_flow = Flow(total_steps(jnp.concatenate(sums)))
    at = jnp.stack([shard_index % head_turns, ctx_index % 2]).astype(jnp.int32)

    def nothing():
        return ()

    while weave.moves:
        beside(nothing, (), [weave])
    up_blocks, out_finish = weave.result
    core_flow = Flow(swap_steps(other, mine))
    down_total = beside(side_by_side, down_total, [joint_flow, core_flow], late=[out_finish])
    while joint_flow.moves:
        beside(nothing, (), [joint_flow])
    held = []
    weave = Flow(weave_steps(joint_flow.result, held, mine.shape))

    def order_and_add(blocks, halves):
        held.append(add_pair(*halves))
        return in_order(*blocks), held[0]

    up_blocks, _ = beside(
        order_and_add, (up_blocks, core_flow.result), [weave, total_flow], early=[out_finish]
    )
    up_swap = Flow(swap_steps(up_blocks))
    output, scaled, inv_std = beside(
        lambda rows, sums, bias: (
            (rows.astype(F32) + sums + bias).astype(BF16),
            *standard(rows),
        ),
        (own_tokens, out_finish.result, out_bias_all + down_bias_all),
        [flow for flow in (weave, total_flow, up_swap) if flow.moves],
    )
    (up_dealt,) = beside(
        lambda *halves: deal_columns(*halves, unit, list(range(shard_count)), at),
        up_swap.result,
        [flow for flow in (weave, total_flow) if flow.moves],
    )
    while weave.moves:
        beside(nothing, (), [flow for flow in (weave, total_flow) if flow.moves])
    joint_blocks, norm_finish = weave.result
    joint_blocks = beside(
        in_order, joint_blocks, [flow for flow in (total_flow,) if flow.moves], late=[norm_finish]
    )
    joint_swap = Flow(swap_steps(joint_blocks))
    beside(nothing, (), [flow for flow in (joint_swap, total_flow) if flow.moves])
    qkv_dealt, out_dealt = beside(
        lambda *halves: deal_columns(*halves, HEAD_DIM, qkv_order, at, with_out=True),
        joint_swap.result,
        [flow for flow in (total_flow,) if flow.moves],
        early=[norm_finish],
    )
    grad_normed = norm_finish.result

    grad_scaled = grad_normed * gain_all
    grad_input = inv_std * (
        grad_scaled
        - jnp.mean(grad_scaled, axis=1, keepdims=True)
        - scaled * jnp.mean(grad_scaled * scaled, axis=1, keepdims=True)
    )
    input_grad = (grad_float + grad_input).astype(BF16)

    while total_flow.moves:
        beside(nothing, (), [total_flow])
    total = total_flow.result
    own_sums, start = [], 0
    for item in sums:
        size = item.shape[0] // shard_count
        own_sums.append(lax.dynamic_slice_in_dim(total, start + shard_index * size, size))
        start += item.shape[0]
    gain_total, shift_total, qkv_bias_total, bias_total, up_bias_total = own_sums

    return (
        output[None],
        input_grad[None],
        gain_total,
        shift_total,
        qkv_dealt,
        qkv_bias_total,
        out_dealt,
        bias_total,
        up_dealt,
        up_bias_total,
        down_total,
        bias_total,
    )


def solution(mesh):
    in_specs = (
        P("fsdp", "ctx", None),
        P(),
        P("fsdp", None),
        P("fsdp"),
        P("fsdp"),
        P("fsdp", None),
        P("fsdp"),
        P("fsdp", None),
        P("fsdp"),
        P("fsdp", None),
        P("fsdp"),
        P("fsdp", None),
        P("fsdp"),
        P("fsdp", "ctx", None),
    )
    out_specs = (
        P("fsdp", "ctx", None),
        P("fsdp", "ctx", None),
        P("fsdp"),
        P("fsdp"),
        P("fsdp", None),
        P("fsdp"),
        P("fsdp", None),
        P("fsdp"),
        P("fsdp", None),
        P("fsdp"),
        P("fsdp", None),
        P("fsdp"),
    )
    return jax.shard_map(shards, mesh=mesh, in_specs=in_specs, out_specs=out_specs, check_vma=False)
```
